32 devices in a mesh: facet: 4 (over y, core), sub: 8 (over z, x).
Axes of the slice: x: 2, y: 2, z: 4, core: 2. Of those that a mesh axis runs over, the one named last changes fastest.
Arguments:
- facet_strips: bfloat16 [2, 16384, 4096], P(None, 'facet', 'sub'), may hold values from -6 to 6
- row_window: float32 [4096], replicated, may hold values from 0.25 to 1.75
- col_window: float32 [4096], P('sub'), may hold values from 0.25 to 1.75
- row_offsets: int32 [4], replicated, may hold values from 0 to 3584
- col_offsets: int32 [4], replicated, may hold values from 0 to 3584
- tile_owner: int32 [8, 4, 128, 1], P('sub', 'facet'), may hold values from 0 to 7; in each aligned block of 128 rows (0 to 127, 128 to 255, ..., all dimensions but the last counted through in order) at most 64 rows name the same one
- measured: float32 [4, 8, 512, 2, 128], P('facet', 'sub'), may hold values from -12 to 12
- vis_weight: float32 [4, 8, 512, 128], P('facet', 'sub'), may hold values from 0.1 to 1
- uvw_pixels: int32 [4, 8, 512, 3, 128], P('facet', 'sub'), may hold values from 0 to 15
- vis_count: int32 [4, 8, 512], P('facet', 'sub'), may hold values from 1 to 128
Outputs:
- facet_update: bfloat16 [2, 16384, 4096], P(None, 'facet', 'sub')
The draws below stay inside these ranges and needn't reach their ends.
Inputs may be any that keep to these rules, and one draw needn't show every extreme that they name: Among the tiles of one row block of the subgrids of one facet index (the entries of tile_owner at one s and the 1 subgrids of one index of facet), no owner is named more than 64 times, and one owner is named exactly 64 times by some row block.
All inputs are finite; a program needn't handle non-finite values.
Results may differ from the reference program's by a relative error of at most 0.024.
Values may be sent and summed in bfloat16 or wider, within the bound.
No kernel may reach another device: no remote copies, remote signals or barrier semaphores. Data moves between devices by JAX's collectives and lax.ppermute only.
A program may use at most 128 MiB of HBM per device.

```python
import math
from functools import partial
import jax
import jax.numpy as jnp
import numpy as np
from jax import lax

FL = 4096
FW = 4096
SG = 512
RADIX = 64
TS = 16
SGF = 1
VPT = 128
FBLK = 4
OWNERS = 8
RBLK = 8
NSG = 4
TR = 4
TC = 32
TPS = 128
TILES_DEV = 128
CAP = 64
SLOTS = 512


def draw_vis_count(key, part):
    keys = jax.random.split(jax.random.fold_in(key, 17), 2)
    total_slots = FBLK * OWNERS * SLOTS
    counts = jax.random.randint(keys[0], (total_slots,), 1, VPT + 1)
    chosen = jax.random.randint(keys[1], (), 0, total_slots)
    positions = jnp.arange(total_slots, dtype=jnp.int32)
    counts = jnp.where(positions == chosen, VPT, counts)
    counts = jnp.where(positions == (chosen + 1) % total_slots, 1, counts)
    return counts.reshape(FBLK, OWNERS, SLOTS).astype(jnp.int32)


def place_ends(entries, stream_key, least, largest):
    index_at = [jax.random.randint(jax.random.fold_in(stream_key, axis), (), 0, length) for axis, length in enumerate(entries.shape)]
    widest = entries.shape.index(max(entries.shape))
    beside = index_at[:widest] + [(index_at[widest] + 1) % entries.shape[widest]] + index_at[widest + 1:]
    return entries.at[tuple(index_at)].set(least).at[tuple(beside)].set(largest)


def block_levels(key, shape, cuts, least, largest):
    def one(dim, parts):
        draws = jax.random.uniform(jax.random.fold_in(jax.random.fold_in(key, 6), dim), (parts,), jnp.float32, least / len(cuts), largest / len(cuts))
        return jnp.repeat(jnp.exp(draws), shape[dim] // parts).reshape((-1,) + (1,) * (len(shape) - dim - 1))

    loudness = one(*cuts[0])
    for cut in cuts[1:]:
        loudness = loudness * one(*cut)
    return loudness


def routed_block(stream_key, own, number, rows, count, top, limit, slope):
    order = jax.random.permutation(stream_key, count)
    crowded, ordinary = load_shares(count, rows * top, limit, slope, True), load_shares(count, rows * top, limit, slope, False)
    places = jnp.arange(count)

    def named(lengths, turn):
        used = int((lengths > 0).sum())
        fixed = max(1, used // 4)
        passed = fixed + (places - fixed + turn * (used - fixed)) % max(1, count - fixed)
        return jnp.zeros((count,), jnp.int32).at[order[jnp.where(places < fixed, places, passed)]].set(jnp.asarray(lengths, jnp.int32))

    lengths = jnp.where(number % 4 == 0, named(crowded, number // 4), named(ordinary, number - number // 4 - 1))
    mixed = jax.random.permutation(jax.random.fold_in(own, 3), count)
    giver, taker = mixed[0:count // 2 * 2:2], mixed[1:count // 2 * 2:2]
    margin = jnp.minimum(lengths[giver] - 1, limit - lengths[taker]) // 2
    margin = jnp.where((giver == order[0]) | (taker == order[0]) | (lengths[taker] == 0), 0, jnp.maximum(margin, 0))
    passed = jax.random.randint(jax.random.fold_in(own, 4), (count // 2,), 0, 1 << 20) % (margin + 1)
    lengths = lengths.at[giver].add(-passed).at[taker].add(passed)
    items = jnp.searchsorted(jnp.cumsum(lengths), jnp.arange(rows * top), side="right").astype(jnp.int32)
    listing = items.reshape(top, rows).T
    listing = listing[jax.random.permutation(jax.random.fold_in(own, 1), rows)]
    turn = jax.random.randint(jax.random.fold_in(own, 2), (rows, 1), 0, top)
    return jnp.take_along_axis(listing, (jnp.arange(top)[None, :] + turn) % top, axis=1)


def load_shares(amount, total, reach, slope, full):
    portions = [(1 << 20) // math.isqrt(rank ** slope) + 1 for rank in range(1, amount + 1)]
    largest = reach if full else min(reach, max(-(-total // amount), total * portions[0] // sum(portions)))
    least = 1 if total - largest >= amount - 1 else 0
    given, surplus = [largest] + [least] * (amount - 1), total - largest - least * (amount - 1)
    while surplus > 0:
        free = [i for i in range(1, amount) if given[i] < largest] or [i for i in range(1, amount) if given[i] < reach]
        mass, remaining = sum([portions[i] for i in free]), surplus
        for i in free:
            more = min(reach - given[i], max(1, remaining * portions[i] // mass), surplus)
            given[i] = given[i] + more
            surplus = surplus - more
    return np.array(given)


def scatter_about(rng, shape, deviation, reach, cuts=(), held_as=jnp.bfloat16):
    loudness = block_levels(rng, shape, cuts, -0.22, 0.18) if cuts else 1.0
    values = jax.random.normal(rng, shape, jnp.float32) * deviation * loudness
    return jnp.minimum(jnp.maximum(values, -reach), reach).astype(held_as)


def setup_inputs(seed: int = 0) -> dict:
    streams_of = jax.random.split(jax.random.key(seed), 11)
    facet_strips = scatter_about(streams_of[0], (2, FBLK * FL, FW), 1.0, 6.0, ((1, 4), (2, 8)))
    row_window = jnp.clip(1.0 + 0.15 * jax.random.normal(streams_of[1], (FL,), jnp.float32), 0.25, 1.75)
    col_window = jnp.clip(1.0 + 0.15 * jax.random.normal(streams_of[2], (FW,), jnp.float32), 0.25, 1.75)
    row_offsets = place_ends(jax.random.randint(streams_of[3], (NSG,), 0, FL - SG + 1), jax.random.fold_in(streams_of[3], 1), 0, FL - SG).astype(jnp.int32)
    col_offsets = place_ends(jax.random.randint(streams_of[4], (NSG,), 0, FW - SG + 1), jax.random.fold_in(streams_of[4], 1), 0, FW - SG).astype(jnp.int32)
    tile_owner_keys = jax.random.split(jax.random.fold_in(streams_of[5], 1), RBLK * NSG * TPS // TILES_DEV)
    tile_owner_turns = jax.random.permutation(jax.random.fold_in(streams_of[5], 3), RBLK * NSG * TPS // TILES_DEV)
    tile_owner = jax.vmap(lambda own, number: routed_block(jax.random.fold_in(streams_of[5], 2), own, number, TILES_DEV, OWNERS, 1, CAP, 2))(tile_owner_keys, tile_owner_turns).reshape((RBLK, NSG, TPS, 1))
    measured = scatter_about(streams_of[6], (FBLK, OWNERS, SLOTS, 2, VPT), 2.0, 12.0, ((0, 4), (1, 8)), jnp.float32)
    vis_weight = jnp.clip(jnp.exp(math.log(1.0) - 2.3025851 * jax.random.uniform(streams_of[7], (FBLK, OWNERS, SLOTS, VPT), jnp.float32) ** block_levels(streams_of[7], (FBLK, OWNERS, SLOTS, VPT), ((0, 4), (1, 8)), -0.2, 0.2)), 0.1, 1.0)
    uvw_pixels = place_ends(jax.random.randint(streams_of[8], (FBLK, OWNERS, SLOTS, 3, VPT), 0, TS), jax.random.fold_in(streams_of[8], 1), 0, TS - 1).astype(jnp.int32)
    vis_count = draw_vis_count(jax.random.fold_in(streams_of[10], 71), 0)
    return {"facet_strips": facet_strips, "row_window": row_window, "col_window": col_window, "row_offsets": row_offsets, "col_offsets": col_offsets, "tile_owner": tile_owner, "measured": measured, "vis_weight": vis_weight, "uvw_pixels": uvw_pixels, "vis_count": vis_count}


kernel_width = 2.5
kernel_norm = 0.565

def contract(pattern, first, other):
    return jnp.einsum(pattern, first.astype(jnp.float32), other.astype(jnp.float32), precision=lax.Precision.HIGHEST)

def angle_table(row_count, col_count, length):
    lefts = jnp.arange(row_count, dtype=jnp.int32)[:, None]
    rights = jnp.arange(col_count, dtype=jnp.int32)[None, :]
    turn_count = (lefts * rights % length).astype(jnp.float32)
    angles = turn_count * (2.0 * math.pi / length)
    return (jnp.cos(angles), jnp.sin(angles))

def complex_matrix(extent, direction):
    cosine, sine_table = angle_table(extent, extent, extent)
    sine_table = direction * sine_table
    upper = jnp.stack([cosine, -sine_table], axis=1)
    lower = jnp.stack([sine_table, cosine], axis=1)
    return jnp.stack([upper, lower], axis=0).astype(jnp.bfloat16)

def apply_twist(values, cosine, sine_table, direction):
    real_part = values[:, 0]
    imag_part = values[:, 1]
    sine_table = direction * sine_table
    return jnp.stack([cosine * real_part - sine_table * imag_part, sine_table * real_part + cosine * imag_part], axis=1).astype(jnp.bfloat16)

def rows_forward(values, radix_size):
    batches = values.shape[0]
    length = values.shape[2]
    columns = values.shape[3]
    second = length // radix_size
    shaped = values.reshape(batches, 2, radix_size, second, columns)
    inner_sum = contract('akzn,bznqc->bakqc', complex_matrix(radix_size, -1.0), shaped)
    cosine, sine_table = angle_table(radix_size, second, length)
    turned = apply_twist(inner_sum, cosine[:, :, None], sine_table[:, :, None], -1.0)
    outer_sum = contract('ajzq,bzkqc->bajkc', complex_matrix(second, -1.0), turned)
    return outer_sum.reshape(batches, 2, length, columns)

def rows_backward(values, radix_size):
    batches = values.shape[0]
    length = values.shape[2]
    columns = values.shape[3]
    second = length // radix_size
    shaped = values.reshape(batches, 2, second, radix_size, columns)
    inner_sum = contract('ajzq,bzqkc->bajkc', complex_matrix(second, 1.0), shaped)
    cosine, sine_table = angle_table(second, radix_size, length)
    turned = apply_twist(inner_sum, cosine[:, :, None], sine_table[:, :, None], 1.0)
    outer_sum = contract('anzk,bzjkc->banjc', complex_matrix(radix_size, 1.0), turned)
    return outer_sum.reshape(batches, 2, length, columns)

def cols_forward(values, radix_size):
    batches = values.shape[0]
    middle = values.shape[2]
    length = values.shape[3]
    second = length // radix_size
    shaped = values.reshape(batches, 2, middle, radix_size, second)
    inner_sum = contract('akzn,bzmnq->bamkq', complex_matrix(radix_size, -1.0), shaped)
    cosine, sine_table = angle_table(radix_size, second, length)
    turned = apply_twist(inner_sum, cosine, sine_table, -1.0)
    outer_sum = contract('ajzq,bzmkq->bamjk', complex_matrix(second, -1.0), turned)
    return outer_sum.reshape(batches, 2, middle, length)

def cols_backward(values, radix_size):
    batches = values.shape[0]
    middle = values.shape[2]
    length = values.shape[3]
    second = length // radix_size
    shaped = values.reshape(batches, 2, middle, second, radix_size)
    inner_sum = contract('ajzq,bzmqk->bamjk', complex_matrix(second, 1.0), shaped)
    cosine, sine_table = angle_table(second, radix_size, length)
    turned = apply_twist(inner_sum, cosine, sine_table, 1.0)
    outer_sum = contract('anzk,bzmjk->bamnj', complex_matrix(radix_size, 1.0), turned)
    return outer_sum.reshape(batches, 2, middle, length)

def rotate(values, facet_index, offsets, facet_count, direction):
    turn_count = (facet_index * offsets % facet_count).astype(jnp.float32)
    angles = turn_count * (2.0 * math.pi / facet_count)
    extra = (1,) * (values.ndim - 2)
    cosine = jnp.cos(angles).reshape(angles.shape + extra)
    sine_table = direction * jnp.sin(angles).reshape(angles.shape + extra)
    real_part = values[:, 0]
    imag_part = values[:, 1]
    return jnp.stack([cosine * real_part - sine_table * imag_part, sine_table * real_part + cosine * imag_part], axis=1)

def kernel_rows(centre, w_plane, tile_size):
    pixels = jnp.arange(tile_size, dtype=jnp.int32)
    offset = pixels[None, :, None] - centre[:, None, :]
    falloff = kernel_norm * jnp.exp(-jnp.square(offset.astype(jnp.float32) / kernel_width))
    square = jnp.square(pixels - tile_size // 2)
    turn_count = w_plane[:, None, :] * square[None, :, None] % (tile_size * tile_size)
    angles = turn_count.astype(jnp.float32) * (2.0 * math.pi / (tile_size * tile_size))
    return jnp.stack([falloff * jnp.cos(angles), -falloff * jnp.sin(angles)], axis=2).astype(jnp.bfloat16)

def visit_slots(slot_tiles, measured, weight, uvw_pixels, counts, tile_size):
    slots = slot_tiles.shape[0]
    visits = measured.shape[2]
    stacked_grid = slot_tiles.reshape(slots, 2 * tile_size, tile_size)
    row_kernel = kernel_rows(uvw_pixels[:, 0], uvw_pixels[:, 2], tile_size)
    col_kernel = kernel_rows(uvw_pixels[:, 1], uvw_pixels[:, 2], tile_size)
    products = contract('sab,sbv->sav', stacked_grid, col_kernel.reshape(slots, tile_size, 2 * visits))
    products = products.reshape(slots, 2, tile_size, 2, visits)
    part_real = products[:, 0, :, 0] - products[:, 1, :, 1]
    part_imag = products[:, 0, :, 1] + products[:, 1, :, 0]
    row_real = row_kernel[:, :, 0].astype(jnp.float32)
    row_imag = row_kernel[:, :, 1].astype(jnp.float32)
    pred_real = lax.optimization_barrier(jnp.sum(row_real * part_real - row_imag * part_imag, axis=1))
    pred_imag = lax.optimization_barrier(jnp.sum(row_real * part_imag + row_imag * part_real, axis=1))
    live_mask = jnp.arange(visits, dtype=jnp.int32)[None, :] < counts[:, None]
    res_real = jnp.where(live_mask, weight * (measured[:, 0] - pred_real), 0.0)
    res_imag = jnp.where(live_mask, weight * (measured[:, 1] - pred_imag), 0.0)
    spread_real = row_real * res_real[:, None, :] + row_imag * res_imag[:, None, :]
    spread_imag = row_real * res_imag[:, None, :] - row_imag * res_real[:, None, :]
    spread = jnp.stack([spread_real, spread_imag], axis=1).astype(jnp.bfloat16).reshape(slots, 2 * tile_size, visits)
    regrid = contract('sav,sbv->sab', spread, col_kernel.reshape(slots, 2 * tile_size, visits))
    regrid = regrid.reshape(slots, 2, tile_size, tile_size, 2)
    tile_real = regrid[:, 0, :, :, 0] + regrid[:, 1, :, :, 1]
    tile_imag = regrid[:, 1, :, :, 0] - regrid[:, 0, :, :, 1]
    return jnp.stack([tile_real, tile_imag], axis=1).astype(jnp.bfloat16).reshape(slots, 2 * tile_size * tile_size)

def routing(owners, sub_count):
    matches = (owners[:, None] == jnp.arange(sub_count, dtype=jnp.int32)[None, :]).astype(jnp.int32)
    return lax.optimization_barrier(jnp.sum(jnp.cumsum(matches, axis=0) * matches, axis=1)) - 1

def reference(facet_strips, row_window, col_window, row_offsets, col_offsets, tile_owner, measured, vis_weight, uvw_pixels, vis_count):
    facets = jnp.transpose(facet_strips.reshape(2, FBLK, FL, FW), (1, 0, 2, 3))

    def forward_facet(subgrids, packed):
        facet_index, one_facet = packed
        prepared = (one_facet.astype(jnp.float32) * row_window[None, :, None] * col_window[None, None, :]).astype(jnp.bfloat16)
        spectrum = rows_forward(prepared[None], RADIX)[0] * (1.0 / math.sqrt(FL))

        def per_subgrid(offset_pair):
            row_start, col_start = offset_pair
            piece = lax.dynamic_slice_in_dim(spectrum, row_start, SG, 1).astype(jnp.bfloat16)
            columns = cols_forward(piece[None], RADIX)[0] * (1.0 / math.sqrt(FW))
            return lax.dynamic_slice_in_dim(columns, col_start, SG, 2)
        extracted = lax.map(per_subgrid, (row_offsets, col_offsets))
        return (subgrids + rotate(extracted, facet_index, row_offsets, FBLK, -1.0), None)
    subgrids, _ = lax.scan(forward_facet, jnp.zeros((NSG, 2, SG, SG), jnp.float32), (jnp.arange(FBLK, dtype=jnp.int32), facets))
    tile_data = subgrids.astype(jnp.bfloat16).reshape(FBLK, SGF, 2, RBLK, TR, TS, TC, TS)
    tile_data = jnp.transpose(tile_data, (0, 3, 1, 4, 6, 2, 5, 7)).reshape(FBLK, RBLK, TILES_DEV, 2 * TS * TS)
    owners = jnp.transpose(tile_owner.reshape(RBLK, FBLK, TILES_DEV), (1, 0, 2))

    def visit_group(packed):
        group_tiles, group_owners, group_measured, group_weight, group_pixels, group_counts = packed
        ranks = jax.vmap(partial(routing, sub_count=OWNERS))(group_owners)
        source = jnp.arange(RBLK, dtype=jnp.int32)[:, None] * CAP + ranks
        buffers = jnp.zeros((OWNERS, SLOTS, 2 * TS * TS), jnp.bfloat16).at[group_owners, source].set(group_tiles)
        answered = jax.vmap(partial(visit_slots, tile_size=TS))(buffers, group_measured, group_weight, group_pixels, group_counts)
        return answered[group_owners, source]
    returned = lax.map(visit_group, (tile_data, owners, measured, vis_weight, uvw_pixels, vis_count))
    returned = returned.reshape(FBLK, RBLK, SGF, TR, TC, 2, TS, TS)
    residual_subgrids = jnp.transpose(returned, (0, 2, 5, 1, 3, 6, 4, 7)).reshape(NSG, 2, SG, SG)

    def column_image(packed):
        one_block, col_start = packed
        placed = lax.dynamic_update_slice_in_dim(jnp.zeros((2, SG, FW), jnp.bfloat16), one_block, col_start, 2)
        image = cols_backward(placed[None], RADIX)[0] * (1.0 / math.sqrt(FW))
        return image.astype(jnp.bfloat16)
    images = lax.map(column_image, (residual_subgrids, col_offsets))

    def backward_facet(facet_index):

        def add_one(which, running):
            one_image = lax.optimization_barrier(images[which]).astype(jnp.float32)
            turned = rotate(one_image[None], facet_index, row_offsets[which][None], FBLK, 1.0)
            turned = lax.optimization_barrier(turned.astype(jnp.bfloat16))
            current = lax.dynamic_slice_in_dim(running, row_offsets[which], SG, 1)
            return lax.dynamic_update_slice_in_dim(running, current + turned[0].astype(jnp.float32), row_offsets[which], 1)
        running = lax.fori_loop(0, NSG, add_one, jnp.zeros((2, FL, FW), jnp.float32))
        sums_bf = running.astype(jnp.bfloat16)
        update = rows_backward(sums_bf[None], RADIX)[0] * (1.0 / math.sqrt(FL))
        return (update * row_window[None, :, None] * col_window[None, None, :]).astype(jnp.bfloat16)
    updates = lax.map(backward_facet, jnp.arange(FBLK, dtype=jnp.int32))
    return jnp.transpose(updates, (1, 0, 2, 3)).reshape(2, FBLK * FL, FW)
```

```python
from functools import partial
import math

import jax
import jax.numpy as jnp
import numpy as np
from jax import lax
from jax.experimental import pallas as pl
from jax.experimental.pallas import tpu as pltpu
from jax.sharding import PartitionSpec as P

SG = 512
TS = 16
LANES = 128
GROUP = LANES // TS

kernel_width = 2.5
kernel_norm = 0.565

VMEM_LIMIT = 56 * 1024 * 1024
F32 = jnp.float32
BF16 = jnp.bfloat16


def column_order():
    lane = np.arange(SG)
    chunk, b, cl = lane // LANES, (lane % LANES) // GROUP, lane % GROUP
    return TS * (GROUP * chunk + cl) + b


def column_tables(full_width):
    turns = np.outer(np.arange(full_width, dtype=np.int64), column_order()) % full_width
    angles = turns * (2.0 * np.pi / full_width)
    return (
        jnp.asarray(np.cos(angles).astype(BF16)),
        jnp.asarray((-np.sin(angles)).astype(BF16)),
    )


def row_tables(length):
    q = np.arange(TS)[:, None] + TS * np.arange(SG // TS)[None, :]
    turns = (q[:, :, None] * np.arange(length // TS)[None, None, :]) % length
    angles = turns * (2.0 * np.pi / length)
    return (
        jnp.asarray(np.cos(angles).astype(np.float32)),
        jnp.asarray((-np.sin(angles)).astype(np.float32)),
    )


def pixel_tables():
    a = np.arange(TS)[:, None]
    lane = np.arange(LANES)[None, :] % TS
    fall = kernel_norm * np.exp(-np.square((a - lane) / kernel_width))
    angles = ((lane * np.square(a - TS // 2)) % (TS * TS)) * (2.0 * np.pi / (TS * TS))
    stacked = np.stack([fall, np.cos(angles), -np.sin(angles)])
    return jnp.asarray(
        np.broadcast_to(stacked[:, :, None, :], (3, TS, GROUP, LANES)).astype(np.float32)
    )


def group_tables():
    rows = 2 * TS * GROUP
    expand = (np.arange(rows)[:, None] // GROUP == np.arange(2 * TS)[None, :]).astype(BF16)
    mask = (
        np.arange(rows)[:, None] % GROUP == np.arange(LANES)[None, :] % GROUP
    ).astype(np.float32)
    return jnp.asarray(expand), jnp.asarray(expand.T.copy()), jnp.asarray(mask)


def radix4(x, direction):
    (r0, i0), (r1, i1), (r2, i2), (r3, i3) = x
    sr, si, dr, di = r0 + r2, i0 + i2, r0 - r2, i0 - i2
    tr, ti, er, ei = r1 + r3, i1 + i3, r1 - r3, i1 - i3
    if direction < 0:
        fr, fi = ei, -er
    else:
        fr, fi = -ei, er
    return [(sr + tr, si + ti), (dr + fr, di + fi), (sr - tr, si - ti), (dr - fr, di - fi)]


def turn(value, step, direction):
    r, i = value
    step = step % TS
    if step == 0:
        return value
    if step == 4:
        return (-i, r) if direction > 0 else (i, -r)
    angle = direction * 2.0 * math.pi * step / TS
    if step == 2:
        h = math.sqrt(0.5)
        return (h * (r - i), h * (r + i)) if direction > 0 else (h * (r + i), h * (i - r))
    if step == 6:
        h = math.sqrt(0.5)
        return (-h * (r + i), h * (r - i)) if direction > 0 else (h * (i - r), -h * (r + i))
    c, s = math.cos(angle), math.sin(angle)
    return (c * r - s * i, s * r + c * i)


def dft16(x, direction):
    inner = [radix4([x[4 * a + b] for a in range(4)], direction) for b in range(4)]
    out = [None] * 16
    for c in range(4):
        column = radix4([turn(inner[b][c], b * c, direction) for b in range(4)], direction)
        for d in range(4):
            out[c + 4 * d] = column[d]
    return out


def fill_matrix(off_ref, t_r, t_i, d_ref, write, count):
    def per_q1(q1, carry):
        a_r, a_i = t_r[q1], t_i[q1]
        for jr in range(count):
            d_r, d_i = d_ref[jr, 0:1, :], d_ref[jr, 1:2, :]
            m_r = a_r * d_r - a_i * d_i
            m_i = a_r * d_i + a_i * d_r
            upper = jnp.concatenate([m_r, -m_i], axis=1)
            lower = jnp.concatenate([m_i, m_r], axis=1)
            block = jnp.concatenate([upper, lower], axis=0).astype(BF16)
            write(jnp.bitwise_and(off_ref[jr] + q1, TS - 1), jr, block)
        return carry

    lax.fori_loop(0, TS, per_q1, 0)


def rows_forward_kernel(
    off_ref, x_ref, rw_ref, tr_ref, ti_ref, d_ref, l_ref, out_ref, mat, inner
):
    count = d_ref.shape[0]
    quarter = tr_ref.shape[2]
    width = x_ref.shape[2]
    part = 2 * (SG // TS)

    @pl.when(pl.program_id(0) == 0)
    def _():
        def write(k1, jr, block):
            mat[k1, jr * part : (jr + 1) * part, :] = block

        fill_matrix(off_ref, tr_ref, ti_ref, d_ref, write, count)

    def butterfly(chunk, carry):
        n2 = pl.multiple_of(chunk * 16, 16)
        for lane in range(0, width, LANES):
            values = []
            for n1 in range(TS):
                rows = pl.ds(pl.multiple_of(n1 * quarter + n2, 16), 16)
                window = rw_ref[rows, :]
                values.append(
                    tuple(
                        x_ref[z, rows, lane : lane + LANES].astype(F32) * window for z in range(2)
                    )
                )
            for k1, pair in enumerate(dft16(values, -1)):
                for z in range(2):
                    rows = pl.ds(pl.multiple_of(z * quarter + n2, 16), 16)
                    inner[k1, rows, lane : lane + LANES] = pair[z].astype(BF16)
        return carry

    lax.fori_loop(0, quarter // 16, butterfly, 0)

    def per_k1(k1, carry):
        sums = jnp.dot(mat[k1], inner[k1], preferred_element_type=F32)
        for jr in range(count):
            q1 = jnp.bitwise_and(k1 - off_ref[jr], TS - 1)
            real = sums[jr * part : jr * part + part // 2]
            imag = sums[jr * part + part // 2 : (jr + 1) * part]
            l_r, l_i = l_ref[jr, 0:1, :], l_ref[jr, 1:2, :]
            out_ref[jr, 0, q1] = (real * l_r - imag * l_i).astype(BF16)
            out_ref[jr, 1, q1] = (real * l_i + imag * l_r).astype(BF16)
        return carry

    lax.fori_loop(0, TS, per_k1, 0)


def rows_forward(offsets, strips, window, tables, turns, levels):
    _, length, width = strips.shape
    count = offsets.shape[0]
    quarter = length // TS
    q2 = SG // TS
    block = min(2 * LANES, width)
    return pl.pallas_call(
        rows_forward_kernel,
        grid_spec=pltpu.PrefetchScalarGridSpec(
            num_scalar_prefetch=1,
            grid=(width // block,),
            in_specs=[
                pl.BlockSpec((2, length, block), lambda c, o: (0, 0, c)),
                pl.BlockSpec((length, LANES), lambda c, o: (0, 0)),
                pl.BlockSpec((TS, q2, quarter), lambda c, o: (0, 0, 0)),
                pl.BlockSpec((TS, q2, quarter), lambda c, o: (0, 0, 0)),
                pl.BlockSpec((count, 2, quarter), lambda c, o: (0, 0, 0)),
                pl.BlockSpec((count, 2, block), lambda c, o: (0, 0, c)),
            ],
            out_specs=pl.BlockSpec((count, 2, TS, q2, block), lambda c, o: (0, 0, 0, 0, c)),
            scratch_shapes=[
                pltpu.VMEM((TS, count * 2 * q2, 2 * quarter), BF16),
                pltpu.VMEM((TS, 2 * quarter, block), BF16),
            ],
        ),
        out_shape=jax.ShapeDtypeStruct((count, 2, TS, q2, width), BF16),
        compiler_params=pltpu.CompilerParams(vmem_limit_bytes=VMEM_LIMIT),
        name="rows_forward",
    )(offsets, strips, window, *tables, turns, levels)


def cols_forward_kernel(me_ref, r_ref, fr_ref, fi_ref, a_ref, b_ref, full):
    subs, tile_rows = a_ref.shape[1], a_ref.shape[2] // (2 * TS)
    half = a_ref.shape[3]
    real, imag = r_ref[0, 0], r_ref[0, 1]
    f_r, f_i = fr_ref[...], fi_ref[...]
    for z, (u, v) in enumerate(((f_r, -f_i), (f_i, f_r))):
        sums = jnp.dot(real, u, preferred_element_type=F32)
        sums += jnp.dot(imag, v, preferred_element_type=F32)
        for chunk in range(SG // LANES):
            full[z, chunk] = sums[:, chunk * LANES : (chunk + 1) * LANES]

    me = me_ref[0]
    per_half = half // LANES

    def per_block(s, carry):
        place = jnp.bitwise_xor(s, me)
        for r2 in range(tile_rows):
            for z in range(2):
                rows = pl.ds(r2 * 2 * TS + z * TS, TS)
                for chunk in range(SG // LANES):
                    picked = full[z, chunk, pl.ds(s * tile_rows + r2, TS, stride=SG // TS), :]
                    out_ref = a_ref if chunk < per_half else b_ref
                    lane = (chunk % per_half) * LANES
                    out_ref[0, place, rows, lane : lane + LANES] = picked.astype(BF16)
        return carry

    lax.fori_loop(0, subs, per_block, 0)


def cols_forward(me, rows, tables, sub_count, first, step):
    count, _, _, width = rows.shape
    used = len(range(first, count, step))
    block_rows = 2 * SG // sub_count
    half = SG // 2
    shape = jax.ShapeDtypeStruct((used, sub_count, block_rows, half), BF16)
    return pl.pallas_call(
        cols_forward_kernel,
        grid_spec=pltpu.PrefetchScalarGridSpec(
            num_scalar_prefetch=1,
            grid=(used,),
            in_specs=[
                pl.BlockSpec((1, 2, SG, width), lambda j, m: (first + step * j, 0, 0, 0)),
                pl.BlockSpec((width, SG), lambda j, m: (m[0], 0)),
                pl.BlockSpec((width, SG), lambda j, m: (m[0], 0)),
            ],
            out_specs=[
                pl.BlockSpec((1, sub_count, block_rows, half), lambda j, m: (j, 0, 0, 0))
            ] * 2,
            scratch_shapes=[pltpu.VMEM((2, SG // LANES, SG, LANES), F32)],
        ),
        out_shape=[shape, shape],
        compiler_params=pltpu.CompilerParams(vmem_limit_bytes=VMEM_LIMIT),
        name="cols_forward",
    )(me, rows, *tables)


def route_kernel(me_ref, owner_ref, *refs):
    subs = len(refs) - 8
    parts, outs = refs[:4], refs[4 : 4 + subs]
    where_ref, held, slots, counts = refs[4 + subs :]
    tile_rows = held.shape[0]
    chunks = SG // LANES
    groups = outs[0].shape[0]
    me = me_ref[0]
    for h in range(2):
        total = parts[2 * h][...].astype(F32) + parts[2 * h + 1][...].astype(F32)
        for r2 in range(tile_rows):
            for c in range(chunks // 2):
                held[r2, h * (chunks // 2) + c] = total[
                    r2 * 2 * TS : (r2 + 1) * 2 * TS, c * LANES : (c + 1) * LANES
                ]

    def clear(g, carry):
        slots[g] = jnp.zeros(slots.shape[1:], F32)
        return carry

    lax.fori_loop(0, slots.shape[0], clear, 0)
    for o in range(subs):
        counts[o] = 0
    lane = lax.broadcasted_iota(jnp.int32, (2 * TS, LANES), 1) % GROUP

    def per_chunk(n, carry):
        value = held[n // chunks, n % chunks]
        for cl in range(GROUP):
            t = n * GROUP + cl
            owner = owner_ref[t]
            rank = counts[owner]
            counts[owner] = rank + 1
            g = jnp.bitwise_xor(owner, me) * groups + rank // GROUP
            sl = rank % GROUP
            where_ref[t] = g * GROUP + sl
            moved = pltpu.roll(value, jnp.bitwise_and(sl - cl, LANES - 1), 1)
            slots[g] = jnp.where(lane == sl, moved, slots[g])
        return carry

    lax.fori_loop(0, tile_rows * chunks, per_chunk, 0)
    for o in range(subs):
        outs[o][...] = slots[o * groups : (o + 1) * groups].astype(BF16)


def route(me, owners, parts, sub_count, groups):
    rows = parts[0].shape[0]
    tile_rows = rows // (2 * TS)
    smem = pl.BlockSpec(memory_space=pltpu.SMEM)
    vmem = pl.BlockSpec(memory_space=pltpu.VMEM)
    block = jax.ShapeDtypeStruct((groups, 2 * TS, LANES), BF16)
    return pl.pallas_call(
        route_kernel,
        in_specs=[smem, smem] + [vmem] * 4,
        out_specs=[vmem] * sub_count + [smem],
        out_shape=[block] * sub_count + [jax.ShapeDtypeStruct(owners.shape, jnp.int32)],
        scratch_shapes=[
            pltpu.VMEM((tile_rows, SG // LANES, 2 * TS, LANES), F32),
            pltpu.VMEM((sub_count * groups, 2 * TS, LANES), F32),
            pltpu.SMEM((sub_count,), jnp.int32),
        ],
        compiler_params=pltpu.CompilerParams(vmem_limit_bytes=VMEM_LIMIT),
        name="route",
    )(me, owners, *parts)


def unroute_kernel(where_ref, *refs):
    subs = len(refs) - 3
    ins, (a_ref, b_ref, slots) = refs[:subs], refs[subs:]
    groups = ins[0].shape[0]
    chunks = SG // LANES
    for o in range(subs):
        slots[o * groups : (o + 1) * groups] = ins[o][...].astype(F32)
    lane = lax.broadcasted_iota(jnp.int32, (2 * TS, LANES), 1) % GROUP

    def per_row(r2, carry):
        rows = pl.ds(pl.multiple_of(r2 * 2 * TS, 2 * TS), 2 * TS)
        for chunk in range(chunks):
            total = jnp.zeros((2 * TS, LANES), F32)
            for cl in range(GROUP):
                slot = where_ref[(r2 * chunks + chunk) * GROUP + cl]
                moved = pltpu.roll(
                    slots[slot // GROUP], jnp.bitwise_and(cl - slot % GROUP, LANES - 1), 1
                )
                total = jnp.where(lane == cl, moved, total)
            out_ref = a_ref if chunk < chunks // 2 else b_ref
            at = (chunk % (chunks // 2)) * LANES
            out_ref[rows, at : at + LANES] = total.astype(BF16)
        return carry

    lax.fori_loop(0, a_ref.shape[0] // (2 * TS), per_row, 0)


def unroute(where, blocks, rows):
    groups = blocks[0].shape[0]
    smem = pl.BlockSpec(memory_space=pltpu.SMEM)
    vmem = pl.BlockSpec(memory_space=pltpu.VMEM)
    half = jax.ShapeDtypeStruct((rows, SG // 2), BF16)
    return pl.pallas_call(
        unroute_kernel,
        in_specs=[smem] + [vmem] * len(blocks),
        out_specs=[vmem] * 2,
        out_shape=[half] * 2,
        scratch_shapes=[pltpu.VMEM((len(blocks) * groups, 2 * TS, LANES), F32)],
        compiler_params=pltpu.CompilerParams(vmem_limit_bytes=VMEM_LIMIT),
        name="unroute",
    )(where, *blocks)


def visit_kernel(me_ref, *refs):
    subs = (len(refs) - 7) // 2
    ins, outs = refs[:subs], refs[7 + subs :]
    meas_ref, weight_ref, pixel_ref, pix_ref, expand_ref, gather_ref, mask_ref = refs[
        subs : subs + 7
    ]
    groups = ins[0].shape[0]
    rows = TS * GROUP
    me = me_ref[0]

    def look_up(table, index):
        return jnp.concatenate(
            [jnp.take_along_axis(pix_ref[table, a], index, axis=1) for a in range(TS)], axis=0
        )

    def one_group(in_ref, out_ref, g, first):
        at = pl.ds(pl.multiple_of(first + g * GROUP, GROUP), GROUP)
        fall_x = look_up(0, pixel_ref[0, at, :])
        fall_y = look_up(0, pixel_ref[1, at, :])
        w0 = pixel_ref[2, at, :]
        cosine, sine = look_up(1, w0), look_up(2, w0)
        row_r, row_i = fall_x * cosine, fall_x * sine
        col = jnp.concatenate([fall_y * cosine, fall_y * sine], axis=1).astype(BF16)
        spread_out = jnp.dot(expand_ref[...], in_ref[g], preferred_element_type=F32)
        blocks = (spread_out * mask_ref[...]).astype(BF16)
        sums = jnp.dot(blocks, col, preferred_element_type=F32)
        part_r = sums[:rows, :LANES] - sums[rows:, LANES:]
        part_i = sums[:rows, LANES:] + sums[rows:, :LANES]
        pred_r = jnp.sum((row_r * part_r - row_i * part_i).reshape(TS, GROUP, LANES), axis=0)
        pred_i = jnp.sum((row_r * part_i + row_i * part_r).reshape(TS, GROUP, LANES), axis=0)
        weight = weight_ref[at, :]
        res_r = jnp.tile(weight * (meas_ref[0, at, :] - pred_r), (TS, 1))
        res_i = jnp.tile(weight * (meas_ref[1, at, :] - pred_i), (TS, 1))
        s_r = (row_r * res_r + row_i * res_i).astype(BF16)
        s_i = (row_r * res_i - row_i * res_r).astype(BF16)
        both = jnp.concatenate(
            [jnp.concatenate([s_r, s_i], axis=1), jnp.concatenate([s_i, -s_r], axis=1)], axis=0
        )
        grid = lax.dot_general(
            both, col, (((1,), (1,)), ((), ())), preferred_element_type=F32
        )
        grid = (grid * mask_ref[...]).astype(BF16)
        out_ref[g] = jnp.dot(gather_ref[...], grid, preferred_element_type=F32).astype(BF16)

    for r in range(subs):
        first = jnp.bitwise_xor(me, r) * (groups * GROUP)

        def body(g, carry, r=r, first=first):
            one_group(ins[r], outs[r], g, first)
            return carry

        lax.fori_loop(0, groups, body, 0)


def visit(me, blocks, measured, weight, pixels, tables):
    vmem = pl.BlockSpec(memory_space=pltpu.VMEM)
    smem = pl.BlockSpec(memory_space=pltpu.SMEM)
    return pl.pallas_call(
        visit_kernel,
        in_specs=[smem] + [vmem] * (len(blocks) + 7),
        out_specs=[vmem] * len(blocks),
        out_shape=[jax.ShapeDtypeStruct(b.shape, b.dtype) for b in blocks],
        compiler_params=pltpu.CompilerParams(vmem_limit_bytes=VMEM_LIMIT),
        name="visit",
    )(me, *blocks, measured, weight, pixels, *tables)


def cols_backward_kernel(me_ref, off_ref, a_ref, b_ref, fr_ref, fi_ref, l_ref, out_ref, image):
    subs, rows = a_ref.shape[1], a_ref.shape[2]
    tile_rows = rows // (2 * TS)
    half = a_ref.shape[3]
    width = fr_ref.shape[0]
    block = tile_rows * TS
    me = me_ref[0]

    def pick(ref, z):
        value = ref[0].reshape(subs, tile_rows, 2, TS, half)[:, :, z]
        return value.reshape(subs * block, half)

    def times(left, right):
        return lax.dot_general(left, right, (((1,), (1,)), ((), ())), preferred_element_type=F32)

    parts = [(pick(ref, 0), pick(ref, 1)) for ref in (a_ref, b_ref)]
    real = imag = 0.0
    for h, (p_r, p_i) in enumerate(parts):
        f_r = fr_ref[:, h * half : (h + 1) * half]
        f_i = fi_ref[:, h * half : (h + 1) * half]
        real += times(p_r, f_r) + times(p_i, f_i)
        imag += times(p_i, f_r) + times(p_r, -f_i)
    l_r, l_i = l_ref[0, 0:1, :], l_ref[0, 1:2, :]
    for z, value in enumerate((real * l_r + imag * l_i, imag * l_r - real * l_i)):
        for s in range(subs):
            at = pl.ds(pl.multiple_of(jnp.bitwise_xor(s, me) * block, TS), block)
            for chunk in range(width // LANES):
                image[z, chunk, at, :] = value[
                    s * block : (s + 1) * block, chunk * LANES : (chunk + 1) * LANES
                ]
    off = off_ref[pl.program_id(0)]
    q2 = SG // TS

    def per_q1(q1, carry):
        k1 = jnp.bitwise_and(off + q1, TS - 1)
        for z in range(2):
            for chunk in range(width // LANES):
                picked = image[z, chunk, pl.ds(q1, q2, stride=TS), :]
                out_ref[k1, z * q2 : (z + 1) * q2, chunk * LANES : (chunk + 1) * LANES] = (
                    picked.astype(BF16)
                )
        return carry

    lax.fori_loop(0, TS, per_q1, 0)


def cols_backward(me, offsets, halves, tables, levels):
    count, subs, rows, half = halves[0].shape
    width = levels.shape[2]
    part = 2 * (SG // TS)
    return pl.pallas_call(
        cols_backward_kernel,
        grid_spec=pltpu.PrefetchScalarGridSpec(
            num_scalar_prefetch=2,
            grid=(count,),
            in_specs=[pl.BlockSpec((1, subs, rows, half), lambda j, m, o: (j, 0, 0, 0))] * 2
            + [pl.BlockSpec((width, SG), lambda j, m, o: (m[0], 0))] * 2
            + [pl.BlockSpec((1, 2, width), lambda j, m, o: (j, 0, 0))],
            out_specs=pl.BlockSpec((TS, part, width), lambda j, m, o: (0, j, 0)),
            scratch_shapes=[pltpu.VMEM((2, width // LANES, SG, LANES), F32)],
        ),
        out_shape=jax.ShapeDtypeStruct((TS, count * part, width), BF16),
        compiler_params=pltpu.CompilerParams(vmem_limit_bytes=VMEM_LIMIT),
        name="cols_backward",
    )(me, offsets, *halves, *tables, levels)


def transposed_kernel(off_ref, tr_ref, ti_ref, d_ref, out_ref, mat):
    part = 2 * (SG // TS)

    def write(k1, jr, block):
        mat[k1, jr * part : (jr + 1) * part, :] = block.astype(F32)

    fill_matrix(off_ref, tr_ref, ti_ref, d_ref, write, d_ref.shape[0])

    def per_k1(k1, carry):
        out_ref[k1] = mat[k1].T.astype(BF16)
        return carry

    lax.fori_loop(0, TS, per_k1, 0)


def transposed_matrix(offsets, tables, turns):
    count, _, quarter = turns.shape
    part = 2 * (SG // TS)
    vmem = pl.BlockSpec(memory_space=pltpu.VMEM)
    return pl.pallas_call(
        transposed_kernel,
        in_specs=[pl.BlockSpec(memory_space=pltpu.SMEM)] + [vmem] * 3,
        out_specs=vmem,
        out_shape=jax.ShapeDtypeStruct((TS, 2 * quarter, count * part), BF16),
        scratch_shapes=[pltpu.VMEM((TS, count * part, 2 * quarter), F32)],
        compiler_params=pltpu.CompilerParams(vmem_limit_bytes=VMEM_LIMIT),
        name="transposed_matrix",
    )(offsets, *tables, turns)


def rows_backward_kernel(image_ref, mat_ref, rw_ref, out_ref, middle):
    quarter = mat_ref.shape[1] // 2
    width = image_ref.shape[2]

    def per_k1(k1, carry):
        middle[k1] = jnp.dot(mat_ref[k1], image_ref[k1], preferred_element_type=F32)
        return carry

    lax.fori_loop(0, TS, per_k1, 0)

    def butterfly(chunk, carry):
        n2 = pl.multiple_of(chunk * 16, 16)
        for lane in range(0, width, LANES):
            values = [
                tuple(
                    middle[k1, pl.ds(pl.multiple_of(z * quarter + n2, 16), 16), lane : lane + LANES]
                    for z in range(2)
                )
                for k1 in range(TS)
            ]
            for n1, pair in enumerate(dft16(values, 1)):
                rows = pl.ds(pl.multiple_of(n1 * quarter + n2, 16), 16)
                window = rw_ref[rows, :]
                for z in range(2):
                    out_ref[z, rows, lane : lane + LANES] = (pair[z] * window).astype(BF16)
        return carry

    lax.fori_loop(0, quarter // 16, butterfly, 0)


def rows_backward(images, matrix, window):
    _, depth, width = images.shape
    length = window.shape[0]
    quarter = length // TS
    block = min(2 * LANES, width)
    return pl.pallas_call(
        rows_backward_kernel,
        grid=(width // block,),
        in_specs=[
            pl.BlockSpec((TS, depth, block), lambda c: (0, 0, c)),
            pl.BlockSpec((TS, 2 * quarter, depth), lambda c: (0, 0, 0)),
            pl.BlockSpec((length, LANES), lambda c: (0, 0)),
        ],
        out_specs=pl.BlockSpec((2, length, block), lambda c: (0, 0, c)),
        out_shape=jax.ShapeDtypeStruct((2, length, width), BF16),
        scratch_shapes=[pltpu.VMEM((TS, 2 * quarter, block), F32)],
        compiler_params=pltpu.CompilerParams(vmem_limit_bytes=VMEM_LIMIT),
        name="rows_backward",
    )(images, matrix, window)


def swap(value, axis, bit):
    return lax.ppermute(value, axis, [(i, i ^ bit) for i in range(lax.axis_size(axis))])


def bits_of(axis):
    return [(axis, 1 << n) for n in range(lax.axis_size(axis).bit_length() - 1)]


def orders():
    facet, sub = bits_of("facet")[1:], bits_of("sub")
    rest = facet[1:] + sub[1:]
    return facet[:1] + sub[:1] + rest, sub[:1] + facet[:1] + rest


def dimensions():
    return bits_of("facet")[:0:-1] + bits_of("sub")[::-1]


def sum_blocks(kept, sent):
    result = []
    for kept_half, sent_half, order in zip(kept, sent, orders()):
        value = kept_half + swap(sent_half, "facet", 1)
        dims = dimensions()
        value = value.reshape((2,) * len(dims) + value.shape[2:])
        for step in order:
            at = dims.index(step)
            dims.remove(step)
            mine = lax.index_in_dim(value, 0, at, keepdims=False)
            arrived = swap(lax.index_in_dim(value, 1, at, keepdims=False), *step)
            value = mine + arrived if dims else None
        result += [mine, arrived]
    return result


def gather_blocks(halves, facet_count, sub_count):
    result = []
    for value, order in zip(halves, orders()):
        shape = value.shape
        have = []
        every = dimensions()
        for step in order[::-1]:
            at = len([d for d in every if d in have and every.index(d) < every.index(step)])
            have.append(step)
            value = jnp.stack([value, swap(value, *step)], axis=at)
        value = value.reshape((facet_count // 2, sub_count) + shape)
        result.append((value, swap(value, "facet", 1)))
    return result


def per_device(
    facet_strips,
    row_window,
    col_window,
    row_offsets,
    col_offsets,
    tile_owner,
    measured,
    vis_weight,
    uvw_pixels,
    vis_count,
):
    sub_count = lax.axis_size("sub")
    facet_count = lax.axis_size("facet")
    my_facet = lax.axis_index("facet")
    my_sub = lax.axis_index("sub")
    _, length, strip_width = facet_strips.shape
    count = row_offsets.shape[0]
    full_width = strip_width * sub_count
    quarter = length // TS
    me = my_sub.reshape(1).astype(jnp.int32)

    relative = jnp.arange(count, dtype=jnp.int32)
    chosen = (relative[:, None] ^ my_facet) == relative[None, :]
    rows_at = jnp.sum(jnp.where(chosen, row_offsets[None, :], 0), axis=1)
    cols_at = jnp.sum(jnp.where(chosen, col_offsets[None, :], 0), axis=1)

    n2 = jnp.arange(quarter, dtype=jnp.int32)
    theta = (my_facet * rows_at % facet_count) * (length // facet_count)
    angles = ((n2[None, :] * rows_at[:, None] + theta[:, None]) % length).astype(F32) * (
        2.0 * math.pi / length
    )
    turns = jnp.stack([jnp.cos(angles), -jnp.sin(angles)], axis=1)
    c = my_sub * strip_width + jnp.arange(strip_width, dtype=jnp.int32)
    angles = (c[None, :] * cols_at[:, None] % full_width).astype(F32) * (2.0 * math.pi / full_width)
    level = col_window[None, :] * (1.0 / math.sqrt(length * full_width))
    levels = jnp.stack([level * jnp.cos(angles), -level * jnp.sin(angles)], axis=1)
    window = jnp.broadcast_to(row_window[:, None], (length, LANES))
    row_consts = row_tables(length)
    col_consts = column_tables(full_width)

    spectrum = rows_forward(rows_at, facet_strips, window, row_consts, turns, levels)
    spectrum = spectrum.reshape(count, 2, SG, strip_width)
    sent = cols_forward(me, spectrum, col_consts, sub_count, 1, 2)
    kept = cols_forward(me, spectrum, col_consts, sub_count, 0, 2)
    parts = sum_blocks(kept, sent)

    owners = tile_owner.reshape(-1)
    slots = measured.shape[2]
    capacity = slots // sub_count
    padded = -(-capacity // GROUP) * GROUP
    groups = padded // GROUP

    def per_slot(value):
        if padded == capacity:
            return value
        value = value.reshape((sub_count, capacity) + value.shape[1:])
        value = jnp.pad(value, ((0, 0), (0, padded - capacity)) + ((0, 0),) * (value.ndim - 2))
        return value.reshape((sub_count * padded,) + value.shape[2:])

    visits = vis_weight.shape[3]
    live = jnp.arange(visits, dtype=jnp.int32)[None, :] < vis_count[0, 0][:, None]
    weights = per_slot(jnp.where(live, vis_weight[0, 0], 0.0))
    values = jnp.transpose(per_slot(measured[0, 0]), (1, 0, 2))
    pixels = jnp.transpose(per_slot(uvw_pixels[0, 0]), (1, 0, 2))

    routed = route(me, owners, parts, sub_count, groups)
    outgoing, where = routed[:-1], routed[-1]
    arrived = [outgoing[0]] + [swap(outgoing[r], "sub", r) for r in range(1, sub_count)]
    answered = visit(
        me, arrived, values, weights, pixels, (pixel_tables(),) + group_tables()
    )
    returned = [answered[0]] + [swap(answered[r], "sub", r) for r in range(1, sub_count)]
    halves = unroute(where, returned, 2 * SG // sub_count)

    matrix = transposed_matrix(rows_at, row_consts, turns)
    (a_own, a_other), (b_own, b_other) = gather_blocks(halves, facet_count, sub_count)
    own = cols_backward(me, rows_at[0::2], (a_own, b_own), col_consts, levels[0::2])
    other = cols_backward(me, rows_at[1::2], (a_other, b_other), col_consts, levels[1::2])
    part = 2 * (SG // TS)
    images = jnp.stack(
        [
            own.reshape(TS, count // 2, part, strip_width),
            other.reshape(TS, count // 2, part, strip_width),
        ],
        axis=2,
    ).reshape(TS, count * part, strip_width)
    return rows_backward(images, matrix, window)


def solution(mesh):
    in_specs = (
        P(None, "facet", "sub"),
        P(),
        P("sub"),
        P(),
        P(),
        P("sub", "facet", None, None),
        P("facet", "sub", None, None, None),
        P("facet", "sub", None, None),
        P("facet", "sub", None, None, None),
        P("facet", "sub", None),
    )
    out_specs = P(None, "facet", "sub")
    return jax.shard_map(
        per_device, mesh=mesh, in_specs=in_specs, out_specs=out_specs, check_vma=False
    )
```

```python
from functools import partial
import math

import jax
import jax.numpy as jnp
import numpy as np
from jax import lax
from jax.experimental import pallas as pl
from jax.experimental.pallas import tpu as pltpu
from jax.sharding import PartitionSpec as P

SG = 512
TS = 16
LANES = 128
GROUP = LANES // TS

kernel_width = 2.5
kernel_norm = 0.565

VMEM_LIMIT = 56 * 1024 * 1024
F32 = jnp.float32
BF16 = jnp.bfloat16


def column_order():
    lane = np.arange(SG)
    chunk, b, cl = lane // LANES, (lane % LANES) // GROUP, lane % GROUP
    return TS * (GROUP * chunk + cl) + b


def column_tables(full_width):
    turns = np.outer(np.arange(full_width, dtype=np.int64), column_order()) % full_width
    angles = turns * (2.0 * np.pi / full_width)
    return (
        jnp.asarray(np.cos(angles).astype(BF16)),
        jnp.asarray((-np.sin(angles)).astype(BF16)),
    )


def row_tables(length):
    q = np.arange(TS)[:, None] + TS * np.arange(SG // TS)[None, :]
    turns = (q[:, :, None] * np.arange(length // TS)[None, None, :]) % length
    angles = turns * (2.0 * np.pi / length)
    return (
        jnp.asarray(np.cos(angles).astype(np.float32)),
        jnp.asarray((-np.sin(angles)).astype(np.float32)),
    )


def radix4(x, direction):
    (r0, i0), (r1, i1), (r2, i2), (r3, i3) = x
    sr, si, dr, di = r0 + r2, i0 + i2, r0 - r2, i0 - i2
    tr, ti, er, ei = r1 + r3, i1 + i3, r1 - r3, i1 - i3
    if direction < 0:
        fr, fi = ei, -er
    else:
        fr, fi = -ei, er
    return [(sr + tr, si + ti), (dr + fr, di + fi), (sr - tr, si - ti), (dr - fr, di - fi)]


def turn(value, step, direction):
    r, i = value
    step = step % TS
    if step == 0:
        return value
    if step == 4:
        return (-i, r) if direction > 0 else (i, -r)
    angle = direction * 2.0 * math.pi * step / TS
    if step == 2:
        h = math.sqrt(0.5)
        return (h * (r - i), h * (r + i)) if direction > 0 else (h * (r + i), h * (i - r))
    if step == 6:
        h = math.sqrt(0.5)
        return (-h * (r + i), h * (r - i)) if direction > 0 else (h * (i - r), -h * (r + i))
    c, s = math.cos(angle), math.sin(angle)
    return (c * r - s * i, s * r + c * i)


def dft16(x, direction):
    inner = [radix4([x[4 * a + b] for a in range(4)], direction) for b in range(4)]
    out = [None] * 16
    for c in range(4):
        column = radix4([turn(inner[b][c], b * c, direction) for b in range(4)], direction)
        for d in range(4):
            out[c + 4 * d] = column[d]
    return out


def wave(turns, length):
    angles = turns.astype(F32) * (2.0 * math.pi / length)
    return jnp.cos(angles), -jnp.sin(angles)


def row_phase(ids, row_off, jr, quarter, facets):
    length = quarter * TS
    off = row_off[jnp.bitwise_xor(ids[0], jr)]
    theta = jnp.bitwise_and(ids[0] * off, facets - 1) * (length // facets)
    n2 = lax.broadcasted_iota(jnp.int32, (1, quarter), 1)
    return wave(jnp.bitwise_and(n2 * off + theta, length - 1), length)


def col_level(ids, col_off, jr, window, full_width, length):
    width = window.shape[1]
    off = col_off[jnp.bitwise_xor(ids[0], jr)]
    c = ids[1] * width + lax.broadcasted_iota(jnp.int32, (1, width), 1)
    cosine, sine = wave(jnp.bitwise_and(c * off, full_width - 1), full_width)
    level = window * (1.0 / math.sqrt(length * full_width))
    return level * cosine, level * sine


def spread_window(window_ref, spread):
    def one(i, carry):
        row = jnp.broadcast_to(window_ref[pl.ds(i, 1), :], (LANES, LANES))
        spread[pl.ds(pl.multiple_of(i * LANES, LANES), LANES), :] = row.T
        return carry

    lax.fori_loop(0, window_ref.shape[0], one, 0)


def place_of(jr, count):
    return (jr % 2) * (count // 2) + jr // 2


def fill_matrix(ids, row_off, tables, write, count):
    t_r, t_i = tables
    quarter = t_r.shape[2]
    phases = [row_phase(ids, row_off, jr, quarter, count) for jr in range(count)]

    def per_q1(q1, carry):
        a_r, a_i = t_r[q1], t_i[q1]
        for jr, (d_r, d_i) in enumerate(phases):
            m_r = a_r * d_r - a_i * d_i
            m_i = a_r * d_i + a_i * d_r
            upper = jnp.concatenate([m_r, -m_i], axis=1)
            lower = jnp.concatenate([m_i, m_r], axis=1)
            block = jnp.concatenate([upper, lower], axis=0).astype(BF16)
            off = row_off[jnp.bitwise_xor(ids[0], jr)]
            write(jnp.bitwise_and(off + q1, TS - 1), place_of(jr, count), block)
        return carry

    lax.fori_loop(0, TS, per_q1, 0)


def exchange(first, second):
    upper = lax.broadcasted_iota(jnp.int32, first.shape, 0) < 4
    return (
        jnp.where(upper, first, pltpu.roll(second, 4, 0)),
        jnp.where(upper, pltpu.roll(first, 4, 0), second),
    )


def columns_out(real, imag, f_r, f_i, full):
    for z, (u, v) in enumerate(((f_r, -f_i), (f_i, f_r))):
        sums = jnp.dot(real, u, preferred_element_type=F32)
        sums += jnp.dot(imag, v, preferred_element_type=F32)
        for chunk in range(SG // LANES):
            full[z, chunk] = sums[:, chunk * LANES : (chunk + 1) * LANES]


def send_blocks(full, me, subs, a_ref, b_ref, at):
    tile_rows = SG // TS // subs
    q2 = SG // TS
    chunks = SG // LANES

    def store(place, row, chunk, value):
        out_ref = a_ref if chunk < chunks // 2 else b_ref
        lane = (chunk % (chunks // 2)) * LANES
        out_ref[at, place, row : row + TS, lane : lane + LANES] = value.astype(BF16)

    if tile_rows == 4:

        def per_pair(m, carry):
            for z in range(2):
                for chunk in range(chunks):
                    for quad in range(0, TS, 4):
                        v = [
                            full[z, chunk, pl.ds(pl.multiple_of((quad + n) * q2 + m * 8, 8), 8), :]
                            for n in range(4)
                        ]
                        pairs = [exchange(v[0], v[1]), exchange(v[2], v[3])]
                        for n in range(2):
                            value = jnp.concatenate([pairs[0][n], pairs[1][n]], axis=0)
                            place = jnp.bitwise_xor(2 * m + n, me)
                            store(place, z * TS * tile_rows + quad * tile_rows, chunk, value)
            return carry

        lax.fori_loop(0, subs // 2, per_pair, 0)
    else:
        assert tile_rows == 1

        def per_block(s, carry):
            for z in range(2):
                for chunk in range(chunks):
                    value = full[z, chunk, pl.ds(s, TS, stride=q2), :]
                    store(jnp.bitwise_xor(s, me), z * TS, chunk, value)
            return carry

        lax.fori_loop(0, subs, per_block, 0)


def forward_kernel(
    ids,
    row_off,
    col_off,
    x_ref,
    rw_ref,
    cw_ref,
    tr_ref,
    ti_ref,
    fr_ref,
    fi_ref,
    kept_ref,
    a_ref,
    b_ref,
    mat,
    inner,
    spread,
    level,
    odd,
    full,
):
    count = level.shape[0]
    quarter = tr_ref.shape[2]
    length = quarter * TS
    block = x_ref.shape[2]
    width = fr_ref.shape[0]
    blocks = width // block
    subs = a_ref.shape[1]
    part = 2 * (SG // TS)
    step = pl.program_id(0)

    @pl.when(step == 0)
    def _():
        def write(k1, place, value):
            mat[k1, place * part : (place + 1) * part, :] = value

        fill_matrix(ids, row_off, (tr_ref, ti_ref), write, count)
        spread_window(rw_ref, spread)
        for jr in range(count):
            l_r, l_i = col_level(ids, col_off, jr, cw_ref[...], width * subs, length)
            level[jr, 0:1, :] = l_r
            level[jr, 1:2, :] = l_i

    @pl.when(step < blocks)
    def _():
        def butterfly(chunk, carry):
            n2 = pl.multiple_of(chunk * 16, 16)
            for lane in range(0, block, LANES):
                values = []
                for n1 in range(TS):
                    rows = pl.ds(pl.multiple_of(n1 * quarter + n2, 16), 16)
                    window = spread[rows, :]
                    values.append(
                        tuple(
                            x_ref[z, rows, lane : lane + LANES].astype(F32) * window
                            for z in range(2)
                        )
                    )
                for k1, pair in enumerate(dft16(values, -1)):
                    for z in range(2):
                        rows = pl.ds(pl.multiple_of(z * quarter + n2, 16), 16)
                        inner[k1, rows, lane : lane + LANES] = pair[z].astype(BF16)
            return carry

        lax.fori_loop(0, quarter // 16, butterfly, 0)
        lanes = pl.ds(pl.multiple_of(step * block, block), block)

        def per_k1(k1, carry):
            sums = jnp.dot(mat[k1], inner[k1], preferred_element_type=F32)
            for jr in range(count):
                off = row_off[jnp.bitwise_xor(ids[0], jr)]
                q1 = jnp.bitwise_and(k1 - off, TS - 1)
                at = place_of(jr, count) * part
                real = sums[at : at + part // 2]
                imag = sums[at + part // 2 : at + part]
                l_r, l_i = level[jr, 0:1, lanes], level[jr, 1:2, lanes]
                out_r = (real * l_r - imag * l_i).astype(BF16)
                out_i = (real * l_i + imag * l_r).astype(BF16)
                if jr % 2:
                    odd[jr // 2, 0, q1, :, lanes] = out_r
                    odd[jr // 2, 1, q1, :, lanes] = out_i
                else:
                    kept_ref[jr // 2, 0, q1] = out_r
                    kept_ref[jr // 2, 1, q1] = out_i
            return carry

        lax.fori_loop(0, TS, per_k1, 0, unroll=4)

    @pl.when(step >= blocks)
    def _():
        j = step - blocks
        columns_out(
            odd[j, 0].reshape(SG, width),
            odd[j, 1].reshape(SG, width),
            fr_ref[...],
            fi_ref[...],
            full,
        )
        send_blocks(full, ids[1], subs, a_ref, b_ref, 0)


def forward(ids, row_off, col_off, strips, row_window, col_window, row_consts, col_consts, subs):
    _, length, width = strips.shape
    count = row_off.shape[0]
    quarter = length // TS
    q2 = SG // TS
    block = min(2 * LANES, width)
    blocks = width // block
    half = SG // 2
    used = count // 2
    rows = 2 * SG // subs
    sent = jax.ShapeDtypeStruct((used, subs, rows, half), BF16)
    kept = jax.ShapeDtypeStruct((used, 2, TS, q2, width), BF16)

    def late(c, *_):
        return (jnp.maximum(c - blocks, 0), 0, 0, 0)

    return pl.pallas_call(
        forward_kernel,
        grid_spec=pltpu.PrefetchScalarGridSpec(
            num_scalar_prefetch=3,
            grid=(blocks + used,),
            in_specs=[
                pl.BlockSpec((2, length, block), lambda c, *_: (0, 0, jnp.minimum(c, blocks - 1))),
                pl.BlockSpec((length // LANES, LANES), lambda c, *_: (0, 0)),
                pl.BlockSpec((1, width), lambda c, *_: (0, 0)),
                pl.BlockSpec((TS, q2, quarter), lambda c, *_: (0, 0, 0)),
                pl.BlockSpec((TS, q2, quarter), lambda c, *_: (0, 0, 0)),
                pl.BlockSpec((width, SG), lambda c, m, *_: (m[1], 0)),
                pl.BlockSpec((width, SG), lambda c, m, *_: (m[1], 0)),
            ],
            out_specs=[
                pl.BlockSpec(
                    (used, 2, TS, q2, block),
                    lambda c, *_: (0, 0, 0, 0, jnp.minimum(c, blocks - 1)),
                ),
                pl.BlockSpec((1, subs, rows, half), late),
                pl.BlockSpec((1, subs, rows, half), late),
            ],
            scratch_shapes=[
                pltpu.VMEM((TS, count * 2 * q2, 2 * quarter), BF16),
                pltpu.VMEM((TS, 2 * quarter, block), BF16),
                pltpu.VMEM((length, LANES), F32),
                pltpu.VMEM((count, 2, width), F32),
                pltpu.VMEM((used, 2, TS, q2, width), BF16),
                pltpu.VMEM((2, SG // LANES, SG, LANES), F32),
            ],
        ),
        out_shape=[kept, sent, sent],
        compiler_params=pltpu.CompilerParams(vmem_limit_bytes=VMEM_LIMIT),
        cost_estimate=pl.CostEstimate(
            flops=12_000_000_000, bytes_accessed=16 << 20, transcendentals=0
        ),
        name="forward",
    )(ids, row_off, col_off, strips, row_window, col_window, *row_consts, *col_consts)


def cols_forward_kernel(ids, r_ref, fr_ref, fi_ref, a_ref, b_ref, full):
    columns_out(r_ref[0, 0], r_ref[0, 1], fr_ref[...], fi_ref[...], full)
    send_blocks(full, ids[1], a_ref.shape[1], a_ref, b_ref, 0)


def cols_forward(ids, rows, tables, subs):
    used, _, _, width = rows.shape
    block_rows = 2 * SG // subs
    half = SG // 2
    shape = jax.ShapeDtypeStruct((used, subs, block_rows, half), BF16)
    return pl.pallas_call(
        cols_forward_kernel,
        grid_spec=pltpu.PrefetchScalarGridSpec(
            num_scalar_prefetch=1,
            grid=(used,),
            in_specs=[
                pl.BlockSpec((1, 2, SG, width), lambda j, m: (j, 0, 0, 0)),
                pl.BlockSpec((width, SG), lambda j, m: (m[1], 0)),
                pl.BlockSpec((width, SG), lambda j, m: (m[1], 0)),
            ],
            out_specs=[pl.BlockSpec((1, subs, block_rows, half), lambda j, m: (j, 0, 0, 0))] * 2,
            scratch_shapes=[pltpu.VMEM((2, SG // LANES, SG, LANES), F32)],
        ),
        out_shape=[shape, shape],
        compiler_params=pltpu.CompilerParams(vmem_limit_bytes=VMEM_LIMIT),
        cost_estimate=pl.CostEstimate(
            flops=4_000_000_000, bytes_accessed=6 << 20, transcendentals=0
        ),
        name="cols_forward",
    )(ids, rows, *tables)


def route_kernel(ids, owner_ref, *refs):
    subs = len(refs) - 8
    parts, outs = refs[:4], refs[4 : 4 + subs]
    where_ref, held, slots, counts = refs[4 + subs :]
    chunks = SG // LANES
    tile_rows = held.shape[1] // (2 * TS)
    groups = outs[0].shape[0]
    me = ids[1]
    for h in range(2):
        total = parts[2 * h][...].astype(F32) + parts[2 * h + 1][...].astype(F32)
        for c in range(chunks // 2):
            held[h * (chunks // 2) + c] = total[:, c * LANES : (c + 1) * LANES]

    def clear(g, carry):
        slots[g] = jnp.zeros(slots.shape[1:], F32)
        return carry

    lax.fori_loop(0, slots.shape[0], clear, 0, unroll=8)
    for o in range(subs):
        counts[o] = 0
    lane = lax.broadcasted_iota(jnp.int32, (2 * TS, LANES), 1) % GROUP

    def per_chunk(n, carry):
        value = held[n % chunks, pl.ds(n // chunks, 2 * TS, stride=tile_rows), :]
        for cl in range(GROUP):
            t = n * GROUP + cl
            owner = owner_ref[t]
            rank = counts[owner]
            counts[owner] = rank + 1
            g = jnp.bitwise_xor(owner, me) * groups + rank // GROUP
            sl = rank % GROUP
            where_ref[t] = g * GROUP + sl
            moved = pltpu.roll(value, jnp.bitwise_and(sl - cl, LANES - 1), 1)
            slots[g] = jnp.where(lane == sl, moved, slots[g])
        return carry

    lax.fori_loop(0, tile_rows * chunks, per_chunk, 0)
    for o in range(subs):
        outs[o][...] = slots[o * groups : (o + 1) * groups].astype(BF16)


def route(ids, owners, parts, subs, groups):
    rows = parts[0].shape[0]
    smem = pl.BlockSpec(memory_space=pltpu.SMEM)
    vmem = pl.BlockSpec(memory_space=pltpu.VMEM)
    block = jax.ShapeDtypeStruct((groups, 2 * TS, LANES), BF16)
    return pl.pallas_call(
        route_kernel,
        in_specs=[smem, smem] + [vmem] * 4,
        out_specs=[vmem] * subs + [smem],
        out_shape=[block] * subs + [jax.ShapeDtypeStruct(owners.shape, jnp.int32)],
        scratch_shapes=[
            pltpu.VMEM((SG // LANES, rows, LANES), F32),
            pltpu.VMEM((subs * groups, 2 * TS, LANES), F32),
            pltpu.SMEM((subs,), jnp.int32),
        ],
        compiler_params=pltpu.CompilerParams(vmem_limit_bytes=VMEM_LIMIT),
        name="route",
    )(ids, owners, *parts)


def unroute_kernel(where_ref, *refs):
    subs = len(refs) - 4
    ins, (a_ref, b_ref, slots, held) = refs[:subs], refs[subs:]
    groups = ins[0].shape[0]
    chunks = SG // LANES
    tile_rows = held.shape[1] // (2 * TS)
    for o in range(subs):
        slots[o * groups : (o + 1) * groups] = ins[o][...].astype(F32)
    lane = lax.broadcasted_iota(jnp.int32, (2 * TS, LANES), 1) % GROUP

    def per_row(r2, carry):
        for chunk in range(chunks):
            total = jnp.zeros((2 * TS, LANES), F32)
            for cl in range(GROUP):
                slot = where_ref[(r2 * chunks + chunk) * GROUP + cl]
                moved = pltpu.roll(
                    slots[slot // GROUP], jnp.bitwise_and(cl - slot % GROUP, LANES - 1), 1
                )
                total = jnp.where(lane == cl, moved, total)
            held[chunk, pl.ds(r2, 2 * TS, stride=tile_rows), :] = total
        return carry

    lax.fori_loop(0, tile_rows, per_row, 0)
    for chunk in range(chunks):
        out_ref = a_ref if chunk < chunks // 2 else b_ref
        at = (chunk % (chunks // 2)) * LANES
        out_ref[:, at : at + LANES] = held[chunk].astype(BF16)


def unroute(where, blocks, rows):
    groups = blocks[0].shape[0]
    smem = pl.BlockSpec(memory_space=pltpu.SMEM)
    vmem = pl.BlockSpec(memory_space=pltpu.VMEM)
    half = jax.ShapeDtypeStruct((rows, SG // 2), BF16)
    return pl.pallas_call(
        unroute_kernel,
        in_specs=[smem] + [vmem] * len(blocks),
        out_specs=[vmem] * 2,
        out_shape=[half] * 2,
        scratch_shapes=[
            pltpu.VMEM((len(blocks) * groups, 2 * TS, LANES), F32),
            pltpu.VMEM((SG // LANES, rows, LANES), F32),
        ],
        compiler_params=pltpu.CompilerParams(vmem_limit_bytes=VMEM_LIMIT),
        name="unroute",
    )(where, *blocks)


def falloffs(centre):
    spread = kernel_width * kernel_width
    c = centre.astype(F32)
    value = kernel_norm * jnp.exp(c * c * (-1.0 / spread))
    ratio = jnp.exp((2.0 * c - 1.0) * (1.0 / spread))
    out = [value]
    for _ in range(1, TS):
        value = value * ratio
        ratio = ratio * math.exp(-2.0 / spread)
        out.append(value)
    return out


def plane_phases(plane):
    base_r, base_i = wave(plane, TS * TS)
    step_r, step_i = base_r * base_r - base_i * base_i, 2.0 * base_r * base_i
    value_r, value_i, turn_r, turn_i = base_r, base_i, base_r, base_i
    out = [(None, None), (value_r, value_i)]
    for _ in range(2, TS // 2 + 1):
        turn_r, turn_i = (
            turn_r * step_r - turn_i * step_i,
            turn_r * step_i + turn_i * step_r,
        )
        value_r, value_i = (
            value_r * turn_r - value_i * turn_i,
            value_r * turn_i + value_i * turn_r,
        )
        out.append((value_r, value_i))
    return out


def kernels_kernel(pixel_ref, row_ref, col_ref):
    def one(g, carry):
        at = pl.ds(pl.multiple_of(g * GROUP, GROUP), GROUP)
        across, along = falloffs(pixel_ref[0, at, :]), falloffs(pixel_ref[1, at, :])
        phases = plane_phases(pixel_ref[2, at, :])
        zero = jnp.zeros(across[0].shape, F32)

        def times(falls, a, z):
            if a == TS // 2:
                return zero if z else falls[a]
            return falls[a] * phases[abs(a - TS // 2)][z]

        for a in range(0, TS, 2):
            rows = pl.ds(a * GROUP, 2 * GROUP)
            for z in range(2):
                row = jnp.concatenate([times(across, a, z), times(across, a + 1, z)], axis=0)
                col = jnp.concatenate([times(along, a, z), times(along, a + 1, z)], axis=0)
                row_ref[g, z, rows, :] = row.astype(BF16)
                col_ref[g, rows, z * LANES : (z + 1) * LANES] = col.astype(BF16)
        return carry

    lax.fori_loop(0, row_ref.shape[0], one, 0, unroll=2)


def kernels(pixels, steps):
    slots = pixels.shape[1]
    groups = slots // GROUP
    rows = TS * GROUP
    return pl.pallas_call(
        kernels_kernel,
        grid=(steps,),
        in_specs=[pl.BlockSpec((3, slots // steps, LANES), lambda i: (0, i, 0))],
        out_specs=[
            pl.BlockSpec((groups // steps, 2, rows, LANES), lambda i: (i, 0, 0, 0)),
            pl.BlockSpec((groups // steps, rows, 2 * LANES), lambda i: (i, 0, 0)),
        ],
        out_shape=[
            jax.ShapeDtypeStruct((groups, 2, rows, LANES), BF16),
            jax.ShapeDtypeStruct((groups, rows, 2 * LANES), BF16),
        ],
        compiler_params=pltpu.CompilerParams(vmem_limit_bytes=VMEM_LIMIT),
        cost_estimate=pl.CostEstimate(
            flops=6_000_000_000, bytes_accessed=9 << 20, transcendentals=0
        ),
        name="kernels",
    )(pixels)


def visit_kernel(sources, *refs):
    n = (len(refs) - 7) // 2
    ins, outs = refs[:n], refs[n + 5 : 2 * n + 5]
    meas_ref, weight_ref, row_ref, col_ref, mask_ref = refs[n : n + 5]
    held, wide = refs[-2:]
    groups = held.shape[0]
    rows = TS * GROUP
    lane = lax.broadcasted_iota(jnp.int32, (2 * TS, LANES), 1) % GROUP

    def one(g, v):
        at = pl.ds(g * GROUP, GROUP)
        blocks = jnp.concatenate(
            [held[g, pl.ds(k, 1), :] * mask_ref[...] for k in range(2 * TS)], axis=0
        ).astype(BF16)
        col = col_ref[g]
        sums = jnp.dot(blocks, col, preferred_element_type=F32)
        part_r = sums[:rows, :LANES] - sums[rows:, LANES:]
        part_i = sums[:rows, LANES:] + sums[rows:, :LANES]
        row_r, row_i = row_ref[g, 0].astype(F32), row_ref[g, 1].astype(F32)
        pred_r = jnp.sum((row_r * part_r - row_i * part_i).reshape(TS, GROUP, LANES), axis=0)
        pred_i = jnp.sum((row_r * part_i + row_i * part_r).reshape(TS, GROUP, LANES), axis=0)
        weight = weight_ref[at, :]
        res_r = jnp.tile(weight * (meas_ref[0, at, :] - pred_r), (TS, 1))
        res_i = jnp.tile(weight * (meas_ref[1, at, :] - pred_i), (TS, 1))
        s_r = (row_r * res_r + row_i * res_i).astype(BF16)
        s_i = (row_r * res_i - row_i * res_r).astype(BF16)
        both = jnp.concatenate(
            [jnp.concatenate([s_r, s_i], axis=1), jnp.concatenate([s_i, -s_r], axis=1)], axis=0
        )
        wide[v] = lax.dot_general(both, col, (((1,), (1,)), ((), ())), preferred_element_type=F32)
        total = wide[v, pl.ds(0, 2 * TS, stride=GROUP), :]
        for slot in range(1, GROUP):
            total = jnp.where(lane == slot, wide[v, pl.ds(slot, 2 * TS, stride=GROUP), :], total)
        return total.astype(BF16)

    for i in range(n):

        @pl.when(pl.program_id(0) == i)
        def _(i=i):
            held[...] = ins[i][...].astype(F32)
            for g, value in enumerate([one(g, g) for g in range(groups)]):
                outs[i][g] = value


def visit(sources, blocks, measured, weight, row, col):
    n = len(blocks)
    shape = blocks[0].shape
    groups = shape[0]
    slots = groups * GROUP
    rows = TS * GROUP
    mask = np.arange(GROUP)[:, None] == np.arange(LANES)[None, :] % GROUP
    whole = pl.BlockSpec(shape, lambda i, m: (0, 0, 0))
    return pl.pallas_call(
        visit_kernel,
        grid_spec=pltpu.PrefetchScalarGridSpec(
            num_scalar_prefetch=1,
            grid=(n,),
            in_specs=[whole] * n
            + [
                pl.BlockSpec((2, slots, LANES), lambda i, m: (0, m[i], 0)),
                pl.BlockSpec((slots, LANES), lambda i, m: (m[i], 0)),
                pl.BlockSpec((groups, 2, rows, LANES), lambda i, m: (m[i], 0, 0, 0)),
                pl.BlockSpec((groups, rows, 2 * LANES), lambda i, m: (m[i], 0, 0)),
                pl.BlockSpec((GROUP, LANES), lambda i, m: (0, 0)),
            ],
            out_specs=[whole] * n,
            scratch_shapes=[
                pltpu.VMEM((groups, 2 * TS, LANES), F32),
                pltpu.VMEM((groups, 2 * rows, LANES), F32),
            ],
        ),
        out_shape=[jax.ShapeDtypeStruct(b.shape, b.dtype) for b in blocks],
        compiler_params=pltpu.CompilerParams(vmem_limit_bytes=VMEM_LIMIT),
        cost_estimate=pl.CostEstimate(
            flops=1_800_000_000 * n, bytes_accessed=(5 << 18) * n, transcendentals=0
        ),
        name="visit",
    )(sources, *blocks, measured, weight, row, col, jnp.asarray(mask.astype(np.float32)))


def columns_back(ids, jr, col_off, halves, fr_ref, fi_ref, cw_ref, image, length):
    subs, rows, half = halves[0].shape
    width = fr_ref.shape[0]
    block = rows // 2

    def times(left, right):
        return lax.dot_general(left, right, (((1,), (1,)), ((), ())), preferred_element_type=F32)

    real = imag = 0.0
    for h, ref in enumerate(halves):
        p_r = ref[:, :block, :].reshape(subs * block, half)
        p_i = ref[:, block:, :].reshape(subs * block, half)
        f_r = fr_ref[:, h * half : (h + 1) * half]
        f_i = fi_ref[:, h * half : (h + 1) * half]
        real += times(p_r, f_r) + times(p_i, f_i)
        imag += times(p_i, f_r) + times(p_r, -f_i)
    l_r, l_i = col_level(ids, col_off, jr, cw_ref[...], width * subs, length)
    for z, value in enumerate((real * l_r + imag * l_i, imag * l_r - real * l_i)):
        for s in range(subs):
            for chunk in range(width // LANES):
                image[z, chunk, jnp.bitwise_xor(s, ids[1])] = value[
                    s * block : (s + 1) * block, chunk * LANES : (chunk + 1) * LANES
                ]


def sort_rows(image, off, write):
    _, chunks, subs, block, _ = image.shape
    tile_rows = block // TS
    q2 = SG // TS

    def k1_of(q1):
        return jnp.bitwise_and(off + q1, TS - 1)

    if tile_rows == 4:

        def per_pair(pair, carry):
            rows = pl.ds(pl.multiple_of(pair * 8, 8), 8)
            for z in range(2):
                for chunk in range(chunks):
                    for s in range(0, subs, 4):
                        v = [image[z, chunk, s + n, rows, :] for n in range(4)]
                        pairs = [exchange(v[0], v[1]), exchange(v[2], v[3])]
                        for n in range(2):
                            value = jnp.concatenate([pairs[0][n], pairs[1][n]], axis=0)
                            write(k1_of(2 * pair + n), z * q2 + s * tile_rows, chunk, value)
            return carry

        lax.fori_loop(0, TS // 2, per_pair, 0)
    else:
        assert tile_rows == 1
        for q1 in range(TS):
            for z in range(2):
                for chunk in range(chunks):
                    value = jnp.concatenate(
                        [image[z, chunk, s, q1 : q1 + 1, :] for s in range(subs)], axis=0
                    )
                    write(k1_of(q1), z * q2, chunk, value)


def cols_backward_kernel(
    ids, row_off, col_off, a_ref, b_ref, fr_ref, fi_ref, cw_ref, out_ref, image, *, length
):
    jr = 2 * pl.program_id(0)
    columns_back(
        ids, jr, col_off, (a_ref.at[0], b_ref.at[0]), fr_ref, fi_ref, cw_ref, image, length
    )

    def write(k1, row, chunk, value):
        lanes = slice(chunk * LANES, (chunk + 1) * LANES)
        out_ref[k1, row : row + value.shape[0], lanes] = value.astype(BF16)

    sort_rows(image, row_off[jnp.bitwise_xor(ids[0], jr)], write)


def image_scratch(width, subs):
    return pltpu.VMEM((2, width // LANES, subs, SG // subs, LANES), F32)


def cols_backward(ids, row_off, col_off, halves, tables, col_window, length):
    used, subs, rows, half = halves[0].shape
    width = col_window.shape[1]
    part = 2 * (SG // TS)
    return pl.pallas_call(
        partial(cols_backward_kernel, length=length),
        grid_spec=pltpu.PrefetchScalarGridSpec(
            num_scalar_prefetch=3,
            grid=(used,),
            in_specs=[pl.BlockSpec((1, subs, rows, half), lambda j, *_: (j, 0, 0, 0))] * 2
            + [pl.BlockSpec((width, SG), lambda j, m, *_: (m[1], 0))] * 2
            + [pl.BlockSpec((1, width), lambda j, *_: (0, 0))],
            out_specs=pl.BlockSpec((TS, part, width), lambda j, *_: (0, j, 0)),
            scratch_shapes=[image_scratch(width, subs)],
        ),
        out_shape=jax.ShapeDtypeStruct((TS, used * part, width), BF16),
        compiler_params=pltpu.CompilerParams(vmem_limit_bytes=VMEM_LIMIT),
        cost_estimate=pl.CostEstimate(
            flops=5_000_000_000, bytes_accessed=6 << 20, transcendentals=0
        ),
        name="cols_backward",
    )(ids, row_off, col_off, *halves, *tables, col_window)


def transposed_kernel(ids, row_off, tr_ref, ti_ref, out_ref, mat):
    part = 2 * (SG // TS)

    def write(k1, place, block):
        mat[k1, place * part : (place + 1) * part, :] = block.astype(F32)

    fill_matrix(ids, row_off, (tr_ref, ti_ref), write, row_off.shape[0])

    def per_k1(k1, carry):
        out_ref[k1] = mat[k1].T.astype(BF16)
        return carry

    lax.fori_loop(0, TS, per_k1, 0)


def transposed_matrix(ids, row_off, tables):
    count = row_off.shape[0]
    quarter = tables[0].shape[2]
    part = 2 * (SG // TS)
    vmem = pl.BlockSpec(memory_space=pltpu.VMEM)
    smem = pl.BlockSpec(memory_space=pltpu.SMEM)
    return pl.pallas_call(
        transposed_kernel,
        in_specs=[smem] * 2 + [vmem] * 2,
        out_specs=vmem,
        out_shape=jax.ShapeDtypeStruct((TS, 2 * quarter, count * part), BF16),
        scratch_shapes=[pltpu.VMEM((TS, count * part, 2 * quarter), F32)],
        compiler_params=pltpu.CompilerParams(vmem_limit_bytes=VMEM_LIMIT),
        cost_estimate=pl.CostEstimate(
            flops=5_000_000_000, bytes_accessed=5 << 20, transcendentals=0
        ),
        name="transposed_matrix",
    )(ids, row_off, *tables)


def backward_kernel(
    ids,
    row_off,
    col_off,
    a_ref,
    b_ref,
    fr_ref,
    fi_ref,
    cw_ref,
    even_ref,
    mat_ref,
    rw_ref,
    out_ref,
    image,
    odd,
    middle,
    spread,
):
    used = row_off.shape[0] // 2
    quarter = mat_ref.shape[1] // 2
    block = even_ref.shape[2]
    part = 2 * (SG // TS)
    step = pl.program_id(0)

    @pl.when(step == 0)
    def _():
        spread_window(rw_ref, spread)

    @pl.when(step < used)
    def _():
        jr = 2 * step + 1
        columns_back(
            ids,
            jr,
            col_off,
            (a_ref.at[0], b_ref.at[0]),
            fr_ref,
            fi_ref,
            cw_ref,
            image,
            quarter * TS,
        )

        def write(k1, row, chunk, value):
            rows = pl.ds(pl.multiple_of(step * part + row, 16), value.shape[0])
            odd[k1, rows, chunk * LANES : (chunk + 1) * LANES] = value.astype(BF16)

        sort_rows(image, row_off[jnp.bitwise_xor(ids[0], jr)], write)

    @pl.when(step >= used)
    def _():
        lanes = pl.ds(pl.multiple_of((step - used) * block, block), block)

        def per_k1(k1, carry):
            rows = jnp.concatenate([even_ref[k1], odd[k1, :, lanes]], axis=0)
            middle[k1] = jnp.dot(mat_ref[k1], rows, preferred_element_type=F32)
            return carry

        lax.fori_loop(0, TS, per_k1, 0, unroll=4)

        def butterfly(chunk, carry):
            n2 = pl.multiple_of(chunk * 16, 16)
            for lane in range(0, block, LANES):
                values = [
                    tuple(
                        middle[
                            k1,
                            pl.ds(pl.multiple_of(z * quarter + n2, 16), 16),
                            lane : lane + LANES,
                        ]
                        for z in range(2)
                    )
                    for k1 in range(TS)
                ]
                for n1, pair in enumerate(dft16(values, 1)):
                    rows = pl.ds(pl.multiple_of(n1 * quarter + n2, 16), 16)
                    window = spread[rows, :]
                    for z in range(2):
                        out_ref[z, rows, lane : lane + LANES] = (pair[z] * window).astype(BF16)
            return carry

        lax.fori_loop(0, quarter // 16, butterfly, 0)


def backward(ids, row_off, col_off, halves, tables, col_window, even, matrix, row_window):
    used, subs, rows, half = halves[0].shape
    _, depth, width = even.shape
    length = row_window.size
    quarter = length // TS
    block = min(2 * LANES, width)

    def early(c, *_):
        return (jnp.minimum(c, used - 1), 0, 0, 0)

    def late(c, *_):
        return (0, 0, jnp.maximum(c - used, 0))

    return pl.pallas_call(
        backward_kernel,
        grid_spec=pltpu.PrefetchScalarGridSpec(
            num_scalar_prefetch=3,
            grid=(used + width // block,),
            in_specs=[pl.BlockSpec((1, subs, rows, half), early)] * 2
            + [pl.BlockSpec((width, SG), lambda c, m, *_: (m[1], 0))] * 2
            + [
                pl.BlockSpec((1, width), lambda c, *_: (0, 0)),
                pl.BlockSpec((TS, depth, block), late),
                pl.BlockSpec((TS, 2 * quarter, 2 * depth), lambda c, *_: (0, 0, 0)),
                pl.BlockSpec((length // LANES, LANES), lambda c, *_: (0, 0)),
            ],
            out_specs=pl.BlockSpec((2, length, block), late),
            scratch_shapes=[
                image_scratch(width, subs),
                pltpu.VMEM((TS, depth, width), BF16),
                pltpu.VMEM((TS, 2 * quarter, block), F32),
                pltpu.VMEM((length, LANES), F32),
            ],
        ),
        out_shape=jax.ShapeDtypeStruct((2, length, width), BF16),
        compiler_params=pltpu.CompilerParams(vmem_limit_bytes=VMEM_LIMIT),
        name="backward",
    )(ids, row_off, col_off, *halves, *tables, col_window, even, matrix, row_window)


def swap(value, axis, bit):
    return lax.ppermute(value, axis, [(i, i ^ bit) for i in range(lax.axis_size(axis))])


def bits_of(axis):
    return [(axis, 1 << n) for n in range(lax.axis_size(axis).bit_length() - 1)]


def orders():
    facet, sub = bits_of("facet")[1:], bits_of("sub")
    rest = facet[1:] + sub[1:]
    return facet[:1] + sub[:1] + rest, sub[:1] + facet[:1] + rest


def dimensions():
    return bits_of("facet")[:0:-1] + bits_of("sub")[::-1]


def sum_blocks(kept, sent):
    result = []
    for kept_half, sent_half, order in zip(kept, sent, orders()):
        value = kept_half + swap(sent_half, "facet", 1)
        dims = dimensions()
        value = value.reshape((2,) * len(dims) + value.shape[2:])
        for step in order:
            at = dims.index(step)
            dims.remove(step)
            mine = lax.index_in_dim(value, 0, at, keepdims=False)
            arrived = swap(lax.index_in_dim(value, 1, at, keepdims=False), *step)
            value = mine + arrived if dims else None
        result += [mine, arrived]
    return result


def gather_blocks(halves, facet_count, sub_count):
    result = []
    for value, order in zip(halves, orders()):
        shape = value.shape
        have = []
        every = dimensions()
        for step in order[::-1]:
            at = len([d for d in every if d in have and every.index(d) < every.index(step)])
            have.append(step)
            value = jnp.stack([value, swap(value, *step)], axis=at)
        value = value.reshape((facet_count // 2, sub_count) + shape)
        result.append((value, swap(value, "facet", 1)))
    return result


def per_device(
    facet_strips,
    row_window,
    col_window,
    row_offsets,
    col_offsets,
    tile_owner,
    measured,
    vis_weight,
    uvw_pixels,
    vis_count,
):
    sub_count = lax.axis_size("sub")
    facet_count = lax.axis_size("facet")
    _, length, strip_width = facet_strips.shape
    full_width = strip_width * sub_count
    ids = jnp.stack([lax.axis_index("facet"), lax.axis_index("sub")]).astype(jnp.int32)
    row_win = row_window.reshape(length // LANES, LANES)
    col_win = col_window.reshape(1, strip_width)
    row_consts = row_tables(length)
    col_consts = column_tables(full_width)

    spectrum, *sent = forward(
        ids,
        row_offsets,
        col_offsets,
        facet_strips,
        row_win,
        col_win,
        row_consts,
        col_consts,
        sub_count,
    )
    spectrum = spectrum.reshape(facet_count // 2, 2, SG, strip_width)
    kept = cols_forward(ids, spectrum, col_consts, sub_count)

    owners = tile_owner.reshape(-1)
    slots = measured.shape[2]
    capacity = slots // sub_count
    padded = -(-capacity // GROUP) * GROUP
    groups = padded // GROUP

    def per_slot(value):
        if padded == capacity:
            return value
        value = value.reshape((sub_count, capacity) + value.shape[1:])
        value = jnp.pad(value, ((0, 0), (0, padded - capacity)) + ((0, 0),) * (value.ndim - 2))
        return value.reshape((sub_count * padded,) + value.shape[2:])

    visits = vis_weight.shape[3]
    live = jnp.arange(visits, dtype=jnp.int32)[None, :] < vis_count[0, 0][:, None]
    weights = per_slot(jnp.where(live, vis_weight[0, 0], 0.0))
    values = jnp.transpose(per_slot(measured[0, 0]), (1, 0, 2))
    pixels = jnp.transpose(per_slot(uvw_pixels[0, 0]), (1, 0, 2))

    parts = sum_blocks(kept, sent)
    row_kernels, col_kernels = kernels(pixels, 4)
    matrix = transposed_matrix(ids, row_offsets, row_consts)
    routed = route(ids, owners, parts, sub_count, groups)
    outgoing, where = routed[:-1], routed[-1]
    arrived = [outgoing[0]] + [swap(outgoing[r], "sub", r) for r in range(1, sub_count)]
    returned = []
    for first in range(0, sub_count, 2):
        sources = jnp.stack([ids[1] ^ first, ids[1] ^ (first + 1)])
        answered = visit(
            sources, arrived[first : first + 2], values, weights, row_kernels, col_kernels
        )
        returned += [
            swap(value, "sub", first + n) if first + n else value
            for n, value in enumerate(answered)
        ]
    halves = unroute(where, returned, 2 * SG // sub_count)

    (a_own, a_other), (b_own, b_other) = gather_blocks(halves, facet_count, sub_count)
    even = cols_backward(
        ids, row_offsets, col_offsets, (a_own, b_own), col_consts, col_win, length
    )
    return backward(
        ids,
        row_offsets,
        col_offsets,
        (a_other, b_other),
        col_consts,
        col_win,
        even,
        matrix,
        row_win,
    )


def solution(mesh):
    in_specs = (
        P(None, "facet", "sub"),
        P(),
        P("sub"),
        P(),
        P(),
        P("sub", "facet", None, None),
        P("facet", "sub", None, None, None),
        P("facet", "sub", None, None),
        P("facet", "sub", None, None, None),
        P("facet", "sub", None),
    )
    out_specs = P(None, "facet", "sub")
    return jax.shard_map(
        per_device, mesh=mesh, in_specs=in_specs, out_specs=out_specs, check_vma=False
    )
```

```python
from functools import partial
import math

import jax
import jax.numpy as jnp
import numpy as np
from jax import lax
from jax.experimental import pallas as pl
from jax.experimental.pallas import tpu as pltpu
from jax.sharding import PartitionSpec as P

SG = 512
TS = 16
LANES = 128
GROUP = LANES // TS

kernel_width = 2.5
kernel_norm = 0.565

VMEM_LIMIT = 56 * 1024 * 1024
F32 = jnp.float32
BF16 = jnp.bfloat16


def column_order():
    lane = np.arange(SG)
    chunk, b, cl = lane // LANES, (lane % LANES) // GROUP, lane % GROUP
    return TS * (GROUP * chunk + cl) + b


def column_tables(full_width):
    turns = np.outer(np.arange(full_width, dtype=np.int64), column_order()) % full_width
    angles = turns * (2.0 * np.pi / full_width)
    return (
        jnp.asarray(np.cos(angles).astype(BF16)),
        jnp.asarray((-np.sin(angles)).astype(BF16)),
    )


def row_tables(length):
    q = np.arange(TS)[:, None] + TS * np.arange(SG // TS)[None, :]
    turns = (q[:, :, None] * np.arange(length // TS)[None, None, :]) % length
    angles = turns * (2.0 * np.pi / length)
    return (
        jnp.asarray(np.cos(angles).astype(np.float32)),
        jnp.asarray((-np.sin(angles)).astype(np.float32)),
    )


def radix4(x, direction):
    (r0, i0), (r1, i1), (r2, i2), (r3, i3) = x
    sr, si, dr, di = r0 + r2, i0 + i2, r0 - r2, i0 - i2
    tr, ti, er, ei = r1 + r3, i1 + i3, r1 - r3, i1 - i3
    if direction < 0:
        fr, fi = ei, -er
    else:
        fr, fi = -ei, er
    return [(sr + tr, si + ti), (dr + fr, di + fi), (sr - tr, si - ti), (dr - fr, di - fi)]


def turn(value, step, direction):
    r, i = value
    step = step % TS
    if step == 0:
        return value
    if step == 4:
        return (-i, r) if direction > 0 else (i, -r)
    angle = direction * 2.0 * math.pi * step / TS
    if step == 2:
        h = math.sqrt(0.5)
        return (h * (r - i), h * (r + i)) if direction > 0 else (h * (r + i), h * (i - r))
    if step == 6:
        h = math.sqrt(0.5)
        return (-h * (r + i), h * (r - i)) if direction > 0 else (h * (i - r), -h * (r + i))
    c, s = math.cos(angle), math.sin(angle)
    return (c * r - s * i, s * r + c * i)


def dft16(x, direction):
    inner = [radix4([x[4 * a + b] for a in range(4)], direction) for b in range(4)]
    out = [None] * 16
    for c in range(4):
        column = radix4([turn(inner[b][c], b * c, direction) for b in range(4)], direction)
        for d in range(4):
            out[c + 4 * d] = column[d]
    return out


def wave(turns, length):
    angles = turns.astype(F32) * (2.0 * math.pi / length)
    return jnp.cos(angles), -jnp.sin(angles)


def row_phase(ids, row_off, jr, quarter, facets):
    length = quarter * TS
    off = row_off[jnp.bitwise_xor(ids[0], jr)]
    theta = jnp.bitwise_and(ids[0] * off, facets - 1) * (length // facets)
    n2 = lax.broadcasted_iota(jnp.int32, (1, quarter), 1)
    return wave(jnp.bitwise_and(n2 * off + theta, length - 1), length)


def col_level(ids, col_off, jr, window, full_width, length):
    width = window.shape[1]
    off = col_off[jnp.bitwise_xor(ids[0], jr)]
    c = ids[1] * width + lax.broadcasted_iota(jnp.int32, (1, width), 1)
    cosine, sine = wave(jnp.bitwise_and(c * off, full_width - 1), full_width)
    level = window * (1.0 / math.sqrt(length * full_width))
    return level * cosine, level * sine


def spread_window(window_ref, spread):
    def one(i, carry):
        row = jnp.broadcast_to(window_ref[pl.ds(i, 1), :], (LANES, LANES))
        spread[pl.ds(pl.multiple_of(i * LANES, LANES), LANES), :] = row.T
        return carry

    lax.fori_loop(0, window_ref.shape[0], one, 0, unroll=8)


def place_of(jr, count):
    return (jr % 2) * (count // 2) + jr // 2


def fill_matrix(ids, row_off, tables, write, count):
    t_r, t_i = tables
    quarter = t_r.shape[2]
    phases = [row_phase(ids, row_off, jr, quarter, count) for jr in range(count)]

    def per_q1(q1, carry):
        a_r, a_i = t_r[q1], t_i[q1]
        for jr, (d_r, d_i) in enumerate(phases):
            m_r = a_r * d_r - a_i * d_i
            m_i = a_r * d_i + a_i * d_r
            upper = jnp.concatenate([m_r, -m_i], axis=1)
            lower = jnp.concatenate([m_i, m_r], axis=1)
            block = jnp.concatenate([upper, lower], axis=0).astype(BF16)
            off = row_off[jnp.bitwise_xor(ids[0], jr)]
            write(jnp.bitwise_and(off + q1, TS - 1), place_of(jr, count), block)
        return carry

    lax.fori_loop(0, TS, per_q1, 0)


def exchange(first, second):
    upper = lax.broadcasted_iota(jnp.int32, first.shape, 0) < 4
    return (
        jnp.where(upper, first, pltpu.roll(second, 4, 0)),
        jnp.where(upper, pltpu.roll(first, 4, 0), second),
    )


def columns_out(real, imag, f_r, f_i, full):
    for z, (u, v) in enumerate(((f_r, -f_i), (f_i, f_r))):
        sums = jnp.dot(real, u, preferred_element_type=F32)
        sums += jnp.dot(imag, v, preferred_element_type=F32)
        for chunk in range(SG // LANES):
            full[z, chunk] = sums[:, chunk * LANES : (chunk + 1) * LANES]


def send_blocks(full, me, subs, a_ref, b_ref, at):
    tile_rows = SG // TS // subs
    q2 = SG // TS
    chunks = SG // LANES

    def store(place, row, chunk, value):
        out_ref = a_ref if chunk < chunks // 2 else b_ref
        lane = (chunk % (chunks // 2)) * LANES
        out_ref[at, place, row : row + TS, lane : lane + LANES] = value.astype(BF16)

    if tile_rows == 4:

        def per_pair(m, carry):
            for z in range(2):
                for chunk in range(chunks):
                    for quad in range(0, TS, 4):
                        v = [
                            full[z, chunk, pl.ds(pl.multiple_of((quad + n) * q2 + m * 8, 8), 8), :]
                            for n in range(4)
                        ]
                        pairs = [exchange(v[0], v[1]), exchange(v[2], v[3])]
                        for n in range(2):
                            value = jnp.concatenate([pairs[0][n], pairs[1][n]], axis=0)
                            place = jnp.bitwise_xor(2 * m + n, me)
                            store(place, z * TS * tile_rows + quad * tile_rows, chunk, value)
            return carry

        lax.fori_loop(0, subs // 2, per_pair, 0)
    else:
        assert tile_rows == 1

        def per_block(s, carry):
            for z in range(2):
                for chunk in range(chunks):
                    value = full[z, chunk, pl.ds(s, TS, stride=q2), :]
                    store(jnp.bitwise_xor(s, me), z * TS, chunk, value)
            return carry

        lax.fori_loop(0, subs, per_block, 0)


def forward_kernel(
    ids,
    row_off,
    col_off,
    x_ref,
    rw_ref,
    cw_ref,
    tr_ref,
    ti_ref,
    fr_ref,
    fi_ref,
    kept_ref,
    a_ref,
    b_ref,
    strips,
    arrived,
    mat,
    inner,
    spread,
    level,
    odd,
    full,
):
    count = level.shape[0]
    quarter = tr_ref.shape[2]
    length = quarter * TS
    blocks, _, _, block = strips.shape
    width = fr_ref.shape[0]
    subs = a_ref.shape[1]
    part = 2 * (SG // TS)
    step = pl.program_id(0)

    def fetch(b):
        lanes = pl.ds(pl.multiple_of(b * block, block), block)
        return pltpu.make_async_copy(x_ref.at[:, :, lanes], strips.at[b], arrived.at[b])

    @pl.when(step == 0)
    def _():
        for b in range(blocks):
            fetch(b).start()

        def write(k1, place, value):
            mat[k1, place * part : (place + 1) * part, :] = value

        fill_matrix(ids, row_off, (tr_ref, ti_ref), write, count)
        spread_window(rw_ref, spread)
        for jr in range(count):
            l_r, l_i = col_level(ids, col_off, jr, cw_ref[...], width * subs, length)
            level[jr, 0:1, :] = l_r
            level[jr, 1:2, :] = l_i

    @pl.when(step < blocks)
    def _():
        fetch(step).wait()

        def butterfly(chunk, carry):
            n2 = pl.multiple_of(chunk * 16, 16)
            for lane in range(0, block, LANES):
                values = []
                for n1 in range(TS):
                    rows = pl.ds(pl.multiple_of(n1 * quarter + n2, 16), 16)
                    window = spread[rows, :]
                    values.append(
                        tuple(
                            strips[step, z, rows, lane : lane + LANES].astype(F32) * window
                            for z in range(2)
                        )
                    )
                for k1, pair in enumerate(dft16(values, -1)):
                    for z in range(2):
                        rows = pl.ds(pl.multiple_of(z * quarter + n2, 16), 16)
                        inner[k1, rows, lane : lane + LANES] = pair[z].astype(BF16)
            return carry

        lax.fori_loop(0, quarter // 16, butterfly, 0)
        lanes = pl.ds(pl.multiple_of(step * block, block), block)

        def per_k1(k1, carry):
            sums = jnp.dot(mat[k1], inner[k1], preferred_element_type=F32)
            for jr in range(count):
                off = row_off[jnp.bitwise_xor(ids[0], jr)]
                q1 = jnp.bitwise_and(k1 - off, TS - 1)
                at = place_of(jr, count) * part
                real = sums[at : at + part // 2]
                imag = sums[at + part // 2 : at + part]
                l_r, l_i = level[jr, 0:1, lanes], level[jr, 1:2, lanes]
                out_r = (real * l_r - imag * l_i).astype(BF16)
                out_i = (real * l_i + imag * l_r).astype(BF16)
                if jr % 2:
                    odd[jr // 2, 0, q1, :, lanes] = out_r
                    odd[jr // 2, 1, q1, :, lanes] = out_i
                else:
                    kept_ref[jr // 2, 0, q1] = out_r
                    kept_ref[jr // 2, 1, q1] = out_i
            return carry

        lax.fori_loop(0, TS, per_k1, 0, unroll=4)

    @pl.when(step >= blocks)
    def _():
        j = step - blocks
        columns_out(
            odd[j, 0].reshape(SG, width),
            odd[j, 1].reshape(SG, width),
            fr_ref[...],
            fi_ref[...],
            full,
        )
        send_blocks(full, ids[1], subs, a_ref, b_ref, 0)


def forward(ids, row_off, col_off, strips, row_window, col_window, row_consts, col_consts, subs):
    _, length, width = strips.shape
    count = row_off.shape[0]
    quarter = length // TS
    q2 = SG // TS
    block = min(2 * LANES, width)
    blocks = width // block
    half = SG // 2
    used = count // 2
    rows = 2 * SG // subs
    sent = jax.ShapeDtypeStruct((used, subs, rows, half), BF16)
    kept = jax.ShapeDtypeStruct((used, 2, TS, q2, width), BF16)

    def late(c, *_):
        return (jnp.maximum(c - blocks, 0), 0, 0, 0)

    return pl.pallas_call(
        forward_kernel,
        grid_spec=pltpu.PrefetchScalarGridSpec(
            num_scalar_prefetch=3,
            grid=(blocks + used,),
            in_specs=[
                pl.BlockSpec(memory_space=pl.ANY),
                pl.BlockSpec((length // LANES, LANES), lambda c, *_: (0, 0)),
                pl.BlockSpec((1, width), lambda c, *_: (0, 0)),
                pl.BlockSpec((TS, q2, quarter), lambda c, *_: (0, 0, 0)),
                pl.BlockSpec((TS, q2, quarter), lambda c, *_: (0, 0, 0)),
                pl.BlockSpec((width, SG), lambda c, m, *_: (m[1], 0)),
                pl.BlockSpec((width, SG), lambda c, m, *_: (m[1], 0)),
            ],
            out_specs=[
                pl.BlockSpec(
                    (used, 2, TS, q2, block),
                    lambda c, *_: (0, 0, 0, 0, jnp.minimum(c, blocks - 1)),
                ),
                pl.BlockSpec((1, subs, rows, half), late),
                pl.BlockSpec((1, subs, rows, half), late),
            ],
            scratch_shapes=[
                pltpu.VMEM((blocks, 2, length, block), BF16),
                pltpu.SemaphoreType.DMA((blocks,)),
                pltpu.VMEM((TS, count * 2 * q2, 2 * quarter), BF16),
                pltpu.VMEM((TS, 2 * quarter, block), BF16),
                pltpu.VMEM((length, LANES), F32),
                pltpu.VMEM((count, 2, width), F32),
                pltpu.VMEM((used, 2, TS, q2, width), BF16),
                pltpu.VMEM((2, SG // LANES, SG, LANES), F32),
            ],
        ),
        out_shape=[kept, sent, sent],
        compiler_params=pltpu.CompilerParams(vmem_limit_bytes=VMEM_LIMIT),
        cost_estimate=pl.CostEstimate(
            flops=12_000_000_000, bytes_accessed=16 << 20, transcendentals=0
        ),
        name="forward",
    )(ids, row_off, col_off, strips, row_window, col_window, *row_consts, *col_consts)


def cols_forward_kernel(ids, r_ref, fr_ref, fi_ref, a_ref, b_ref, full):
    columns_out(r_ref[0, 0], r_ref[0, 1], fr_ref[...], fi_ref[...], full)
    send_blocks(full, ids[1], a_ref.shape[1], a_ref, b_ref, 0)


def cols_forward(ids, rows, tables, subs):
    used, _, _, width = rows.shape
    block_rows = 2 * SG // subs
    half = SG // 2
    shape = jax.ShapeDtypeStruct((used, subs, block_rows, half), BF16)
    return pl.pallas_call(
        cols_forward_kernel,
        grid_spec=pltpu.PrefetchScalarGridSpec(
            num_scalar_prefetch=1,
            grid=(used,),
            in_specs=[
                pl.BlockSpec((1, 2, SG, width), lambda j, m: (j, 0, 0, 0)),
                pl.BlockSpec((width, SG), lambda j, m: (m[1], 0)),
                pl.BlockSpec((width, SG), lambda j, m: (m[1], 0)),
            ],
            out_specs=[pl.BlockSpec((1, subs, block_rows, half), lambda j, m: (j, 0, 0, 0))] * 2,
            scratch_shapes=[pltpu.VMEM((2, SG // LANES, SG, LANES), F32)],
        ),
        out_shape=[shape, shape],
        compiler_params=pltpu.CompilerParams(vmem_limit_bytes=VMEM_LIMIT),
        cost_estimate=pl.CostEstimate(
            flops=4_000_000_000, bytes_accessed=6 << 20, transcendentals=0
        ),
        name="cols_forward",
    )(ids, rows, *tables)


def route_kernel(ids, owner_ref, *refs):
    subs = len(refs) - 8
    parts, outs = refs[:4], refs[4 : 4 + subs]
    where_ref, held, slots, counts = refs[4 + subs :]
    chunks = SG // LANES
    tile_rows = held.shape[1] // (2 * TS)
    groups = outs[0].shape[0]
    me = ids[1]
    for h in range(2):
        total = parts[2 * h][...].astype(F32) + parts[2 * h + 1][...].astype(F32)
        for c in range(chunks // 2):
            held[h * (chunks // 2) + c] = total[:, c * LANES : (c + 1) * LANES]

    def clear(g, carry):
        slots[g] = jnp.zeros(slots.shape[1:], F32)
        return carry

    lax.fori_loop(0, slots.shape[0], clear, 0, unroll=8)
    for o in range(subs):
        counts[o] = 0
    lane = lax.broadcasted_iota(jnp.int32, (2 * TS, LANES), 1) % GROUP

    def per_chunk(n, carry):
        value = held[n % chunks, pl.ds(n // chunks, 2 * TS, stride=tile_rows), :]
        for cl in range(GROUP):
            t = n * GROUP + cl
            owner = owner_ref[t]
            rank = counts[owner]
            counts[owner] = rank + 1
            g = jnp.bitwise_xor(owner, me) * groups + rank // GROUP
            sl = rank % GROUP
            where_ref[t] = g * GROUP + sl
            moved = pltpu.roll(value, jnp.bitwise_and(sl - cl, LANES - 1), 1)
            slots[g] = jnp.where(lane == sl, moved, slots[g])
        return carry

    lax.fori_loop(0, tile_rows * chunks, per_chunk, 0)
    for o in range(subs):
        outs[o][...] = slots[o * groups : (o + 1) * groups].astype(BF16)


def route(ids, owners, parts, subs, groups):
    rows = parts[0].shape[0]
    smem = pl.BlockSpec(memory_space=pltpu.SMEM)
    vmem = pl.BlockSpec(memory_space=pltpu.VMEM)
    block = jax.ShapeDtypeStruct((groups, 2 * TS, LANES), BF16)
    return pl.pallas_call(
        route_kernel,
        in_specs=[smem, smem] + [vmem] * 4,
        out_specs=[vmem] * subs + [smem],
        out_shape=[block] * subs + [jax.ShapeDtypeStruct(owners.shape, jnp.int32)],
        scratch_shapes=[
            pltpu.VMEM((SG // LANES, rows, LANES), F32),
            pltpu.VMEM((subs * groups, 2 * TS, LANES), F32),
            pltpu.SMEM((subs,), jnp.int32),
        ],
        compiler_params=pltpu.CompilerParams(vmem_limit_bytes=VMEM_LIMIT),
        name="route",
    )(ids, owners, *parts)


def unroute_kernel(where_ref, *refs):
    subs = len(refs) - 4
    ins, (a_ref, b_ref, slots, held) = refs[:subs], refs[subs:]
    groups = ins[0].shape[0]
    chunks = SG // LANES
    tile_rows = held.shape[1] // (2 * TS)
    for o in range(subs):
        slots[o * groups : (o + 1) * groups] = ins[o][...].astype(F32)
    lane = lax.broadcasted_iota(jnp.int32, (2 * TS, LANES), 1) % GROUP

    def per_row(r2, carry):
        for chunk in range(chunks):
            total = jnp.zeros((2 * TS, LANES), F32)
            for cl in range(GROUP):
                slot = where_ref[(r2 * chunks + chunk) * GROUP + cl]
                moved = pltpu.roll(
                    slots[slot // GROUP], jnp.bitwise_and(cl - slot % GROUP, LANES - 1), 1
                )
                total = jnp.where(lane == cl, moved, total)
            held[chunk, pl.ds(r2, 2 * TS, stride=tile_rows), :] = total
        return carry

    lax.fori_loop(0, tile_rows, per_row, 0)
    for chunk in range(chunks):
        out_ref = a_ref if chunk < chunks // 2 else b_ref
        at = (chunk % (chunks // 2)) * LANES
        out_ref[:, at : at + LANES] = held[chunk].astype(BF16)


def unroute(where, blocks, rows):
    groups = blocks[0].shape[0]
    smem = pl.BlockSpec(memory_space=pltpu.SMEM)
    vmem = pl.BlockSpec(memory_space=pltpu.VMEM)
    half = jax.ShapeDtypeStruct((rows, SG // 2), BF16)
    return pl.pallas_call(
        unroute_kernel,
        in_specs=[smem] + [vmem] * len(blocks),
        out_specs=[vmem] * 2,
        out_shape=[half] * 2,
        scratch_shapes=[
            pltpu.VMEM((len(blocks) * groups, 2 * TS, LANES), F32),
            pltpu.VMEM((SG // LANES, rows, LANES), F32),
        ],
        compiler_params=pltpu.CompilerParams(vmem_limit_bytes=VMEM_LIMIT),
        name="unroute",
    )(where, *blocks)


def falloffs(centre):
    spread = kernel_width * kernel_width
    c = centre.astype(F32)
    value = kernel_norm * jnp.exp(c * c * (-1.0 / spread))
    ratio = jnp.exp((2.0 * c - 1.0) * (1.0 / spread))
    out = [value]
    for _ in range(1, TS):
        value = value * ratio
        ratio = ratio * math.exp(-2.0 / spread)
        out.append(value)
    return out


def plane_phases(plane):
    base_r, base_i = wave(plane, TS * TS)
    step_r, step_i = base_r * base_r - base_i * base_i, 2.0 * base_r * base_i
    value_r, value_i, turn_r, turn_i = base_r, base_i, base_r, base_i
    out = [(None, None), (value_r, value_i)]
    for _ in range(2, TS // 2 + 1):
        turn_r, turn_i = (
            turn_r * step_r - turn_i * step_i,
            turn_r * step_i + turn_i * step_r,
        )
        value_r, value_i = (
            value_r * turn_r - value_i * turn_i,
            value_r * turn_i + value_i * turn_r,
        )
        out.append((value_r, value_i))
    return out


def kernels_kernel(pixel_ref, row_ref, col_ref):
    def one(g, carry):
        at = pl.ds(pl.multiple_of(g * GROUP, GROUP), GROUP)
        across, along = falloffs(pixel_ref[0, at, :]), falloffs(pixel_ref[1, at, :])
        phases = plane_phases(pixel_ref[2, at, :])
        zero = jnp.zeros(across[0].shape, F32)

        def times(falls, a, z):
            if a == TS // 2:
                return zero if z else falls[a]
            return falls[a] * phases[abs(a - TS // 2)][z]

        for a in range(0, TS, 2):
            rows = pl.ds(a * GROUP, 2 * GROUP)
            for z in range(2):
                row = jnp.concatenate([times(across, a, z), times(across, a + 1, z)], axis=0)
                col = jnp.concatenate([times(along, a, z), times(along, a + 1, z)], axis=0)
                row_ref[g, z, rows, :] = row.astype(BF16)
                col_ref[g, rows, z * LANES : (z + 1) * LANES] = col.astype(BF16)
        return carry

    lax.fori_loop(0, row_ref.shape[0], one, 0, unroll=2)


def kernels(pixels, steps):
    slots = pixels.shape[1]
    groups = slots // GROUP
    rows = TS * GROUP
    return pl.pallas_call(
        kernels_kernel,
        grid=(steps,),
        in_specs=[pl.BlockSpec((3, slots // steps, LANES), lambda i: (0, i, 0))],
        out_specs=[
            pl.BlockSpec((groups // steps, 2, rows, LANES), lambda i: (i, 0, 0, 0)),
            pl.BlockSpec((groups // steps, rows, 2 * LANES), lambda i: (i, 0, 0)),
        ],
        out_shape=[
            jax.ShapeDtypeStruct((groups, 2, rows, LANES), BF16),
            jax.ShapeDtypeStruct((groups, rows, 2 * LANES), BF16),
        ],
        compiler_params=pltpu.CompilerParams(vmem_limit_bytes=VMEM_LIMIT),
        cost_estimate=pl.CostEstimate(
            flops=6_000_000_000, bytes_accessed=9 << 20, transcendentals=0
        ),
        name="kernels",
    )(pixels)


def visit_kernel(ids, *refs):
    n = (len(refs) - 7) // 2
    ins, outs = refs[:n], refs[n + 5 : 2 * n + 5]
    meas_ref, weight_ref, row_ref, col_ref, mask_ref = refs[n : n + 5]
    held, wide = refs[-2:]
    groups = held.shape[0]
    rows = TS * GROUP
    lane = lax.broadcasted_iota(jnp.int32, (2 * TS, LANES), 1) % GROUP

    def one(g, v):
        at = pl.ds(g * GROUP, GROUP)
        blocks = jnp.concatenate(
            [held[g, pl.ds(k, 1), :] * mask_ref[...] for k in range(2 * TS)], axis=0
        ).astype(BF16)
        col = col_ref[g]
        sums = jnp.dot(blocks, col, preferred_element_type=F32)
        part_r = sums[:rows, :LANES] - sums[rows:, LANES:]
        part_i = sums[:rows, LANES:] + sums[rows:, :LANES]
        row_r, row_i = row_ref[g, 0].astype(F32), row_ref[g, 1].astype(F32)
        pred_r = jnp.sum((row_r * part_r - row_i * part_i).reshape(TS, GROUP, LANES), axis=0)
        pred_i = jnp.sum((row_r * part_i + row_i * part_r).reshape(TS, GROUP, LANES), axis=0)
        weight = weight_ref[at, :]
        res_r = jnp.tile(weight * (meas_ref[0, at, :] - pred_r), (TS, 1))
        res_i = jnp.tile(weight * (meas_ref[1, at, :] - pred_i), (TS, 1))
        s_r = (row_r * res_r + row_i * res_i).astype(BF16)
        s_i = (row_r * res_i - row_i * res_r).astype(BF16)
        both = jnp.concatenate(
            [jnp.concatenate([s_r, s_i], axis=1), jnp.concatenate([s_i, -s_r], axis=1)], axis=0
        )
        wide[v] = lax.dot_general(both, col, (((1,), (1,)), ((), ())), preferred_element_type=F32)
        total = wide[v, pl.ds(0, 2 * TS, stride=GROUP), :]
        for slot in range(1, GROUP):
            total = jnp.where(lane == slot, wide[v, pl.ds(slot, 2 * TS, stride=GROUP), :], total)
        return total.astype(BF16)

    for i in range(n):

        @pl.when(pl.program_id(0) == i)
        def _(i=i):
            held[...] = ins[i][...].astype(F32)
            for g, value in enumerate([one(g, g) for g in range(groups)]):
                outs[i][g] = value


def visit(ids, first, blocks, measured, weight, row, col):
    n = len(blocks)
    shape = blocks[0].shape
    groups = shape[0]
    slots = groups * GROUP
    rows = TS * GROUP
    mask = np.arange(GROUP)[:, None] == np.arange(LANES)[None, :] % GROUP
    whole = pl.BlockSpec(shape, lambda i, m: (0, 0, 0))

    def source(i, m):
        return jnp.bitwise_xor(m[1], first + i)

    return pl.pallas_call(
        visit_kernel,
        grid_spec=pltpu.PrefetchScalarGridSpec(
            num_scalar_prefetch=1,
            grid=(n,),
            in_specs=[whole] * n
            + [
                pl.BlockSpec((2, slots, LANES), lambda i, m: (0, source(i, m), 0)),
                pl.BlockSpec((slots, LANES), lambda i, m: (source(i, m), 0)),
                pl.BlockSpec((groups, 2, rows, LANES), lambda i, m: (source(i, m), 0, 0, 0)),
                pl.BlockSpec((groups, rows, 2 * LANES), lambda i, m: (source(i, m), 0, 0)),
                pl.BlockSpec((GROUP, LANES), lambda i, m: (0, 0)),
            ],
            out_specs=[whole] * n,
            scratch_shapes=[
                pltpu.VMEM((groups, 2 * TS, LANES), F32),
                pltpu.VMEM((groups, 2 * rows, LANES), F32),
            ],
        ),
        out_shape=[jax.ShapeDtypeStruct(b.shape, b.dtype) for b in blocks],
        compiler_params=pltpu.CompilerParams(vmem_limit_bytes=VMEM_LIMIT),
        cost_estimate=pl.CostEstimate(
            flops=1_800_000_000 * n, bytes_accessed=(5 << 18) * n, transcendentals=0
        ),
        name="visit",
    )(ids, *blocks, measured, weight, row, col, jnp.asarray(mask.astype(np.float32)))


def columns_back(ids, jr, col_off, halves, fr_ref, fi_ref, cw_ref, image, length):
    subs, rows, half = halves[0].shape
    width = fr_ref.shape[0]
    block = rows // 2

    def times(left, right):
        return lax.dot_general(left, right, (((1,), (1,)), ((), ())), preferred_element_type=F32)

    real = imag = 0.0
    for h, ref in enumerate(halves):
        p_r = ref[:, :block, :].reshape(subs * block, half)
        p_i = ref[:, block:, :].reshape(subs * block, half)
        f_r = fr_ref[:, h * half : (h + 1) * half]
        f_i = fi_ref[:, h * half : (h + 1) * half]
        real += times(p_r, f_r) + times(p_i, f_i)
        imag += times(p_i, f_r) + times(p_r, -f_i)
    l_r, l_i = col_level(ids, col_off, jr, cw_ref[...], width * subs, length)
    for z, value in enumerate((real * l_r + imag * l_i, imag * l_r - real * l_i)):
        for s in range(subs):
            for chunk in range(width // LANES):
                image[z, chunk, jnp.bitwise_xor(s, ids[1])] = value[
                    s * block : (s + 1) * block, chunk * LANES : (chunk + 1) * LANES
                ]


def sort_rows(image, off, write):
    _, chunks, subs, block, _ = image.shape
    tile_rows = block // TS
    q2 = SG // TS

    def k1_of(q1):
        return jnp.bitwise_and(off + q1, TS - 1)

    if tile_rows == 4:

        def per_pair(pair, carry):
            rows = pl.ds(pl.multiple_of(pair * 8, 8), 8)
            for z in range(2):
                for chunk in range(chunks):
                    for s in range(0, subs, 4):
                        v = [image[z, chunk, s + n, rows, :] for n in range(4)]
                        pairs = [exchange(v[0], v[1]), exchange(v[2], v[3])]
                        for n in range(2):
                            value = jnp.concatenate([pairs[0][n], pairs[1][n]], axis=0)
                            write(k1_of(2 * pair + n), z * q2 + s * tile_rows, chunk, value)
            return carry

        lax.fori_loop(0, TS // 2, per_pair, 0)
    else:
        assert tile_rows == 1
        for q1 in range(TS):
            for z in range(2):
                for chunk in range(chunks):
                    value = jnp.concatenate(
                        [image[z, chunk, s, q1 : q1 + 1, :] for s in range(subs)], axis=0
                    )
                    write(k1_of(q1), z * q2, chunk, value)


def cols_backward_kernel(
    ids, row_off, col_off, a_ref, b_ref, fr_ref, fi_ref, cw_ref, out_ref, image, *, length
):
    jr = 2 * pl.program_id(0)
    columns_back(
        ids, jr, col_off, (a_ref.at[0], b_ref.at[0]), fr_ref, fi_ref, cw_ref, image, length
    )

    def write(k1, row, chunk, value):
        lanes = slice(chunk * LANES, (chunk + 1) * LANES)
        out_ref[k1, row : row + value.shape[0], lanes] = value.astype(BF16)

    sort_rows(image, row_off[jnp.bitwise_xor(ids[0], jr)], write)


def image_scratch(width, subs):
    return pltpu.VMEM((2, width // LANES, subs, SG // subs, LANES), F32)


def cols_backward(ids, row_off, col_off, halves, tables, col_window, length):
    used, subs, rows, half = halves[0].shape
    width = col_window.shape[1]
    part = 2 * (SG // TS)
    return pl.pallas_call(
        partial(cols_backward_kernel, length=length),
        grid_spec=pltpu.PrefetchScalarGridSpec(
            num_scalar_prefetch=3,
            grid=(used,),
            in_specs=[pl.BlockSpec((1, subs, rows, half), lambda j, *_: (j, 0, 0, 0))] * 2
            + [pl.BlockSpec((width, SG), lambda j, m, *_: (m[1], 0))] * 2
            + [pl.BlockSpec((1, width), lambda j, *_: (0, 0))],
            out_specs=pl.BlockSpec((TS, part, width), lambda j, *_: (0, j, 0)),
            scratch_shapes=[image_scratch(width, subs)],
        ),
        out_shape=jax.ShapeDtypeStruct((TS, used * part, width), BF16),
        compiler_params=pltpu.CompilerParams(vmem_limit_bytes=VMEM_LIMIT),
        cost_estimate=pl.CostEstimate(
            flops=5_000_000_000, bytes_accessed=6 << 20, transcendentals=0
        ),
        name="cols_backward",
    )(ids, row_off, col_off, *halves, *tables, col_window)


def adjoint_tables_kernel(ids, row_off, tr_ref, ti_ref, rw_ref, out_ref, spread_ref, mat):
    part = 2 * (SG // TS)

    def write(k1, place, block):
        mat[k1, place * part : (place + 1) * part, :] = block.astype(F32)

    fill_matrix(ids, row_off, (tr_ref, ti_ref), write, row_off.shape[0])

    def per_k1(k1, carry):
        out_ref[k1] = mat[k1].T.astype(BF16)
        return carry

    lax.fori_loop(0, TS, per_k1, 0)
    spread_window(rw_ref, spread_ref)


def adjoint_tables(ids, row_off, tables, row_window):
    count = row_off.shape[0]
    quarter = tables[0].shape[2]
    part = 2 * (SG // TS)
    vmem = pl.BlockSpec(memory_space=pltpu.VMEM)
    smem = pl.BlockSpec(memory_space=pltpu.SMEM)
    return pl.pallas_call(
        adjoint_tables_kernel,
        in_specs=[smem] * 2 + [vmem] * 3,
        out_specs=[vmem] * 2,
        out_shape=[
            jax.ShapeDtypeStruct((TS, 2 * quarter, count * part), BF16),
            jax.ShapeDtypeStruct((row_window.size, LANES), F32),
        ],
        scratch_shapes=[pltpu.VMEM((TS, count * part, 2 * quarter), F32)],
        compiler_params=pltpu.CompilerParams(vmem_limit_bytes=VMEM_LIMIT),
        cost_estimate=pl.CostEstimate(
            flops=7_000_000_000, bytes_accessed=7 << 20, transcendentals=0
        ),
        name="adjoint_tables",
    )(ids, row_off, *tables, row_window)


def backward_kernel(
    ids,
    row_off,
    col_off,
    a_ref,
    b_ref,
    fr_ref,
    fi_ref,
    cw_ref,
    even_ref,
    mat_ref,
    spread_ref,
    out_ref,
    image,
    odd,
    middle,
    mat,
    spread,
    update,
    arrived,
    left,
):
    used = row_off.shape[0] // 2
    quarter = mat.shape[1] // 2
    blocks, _, _, _, block = update.shape
    pieces = left.shape[1]
    piece = quarter // pieces
    part = 2 * (SG // TS)
    step = pl.program_id(0)

    def fetches():
        return (
            pltpu.make_async_copy(mat_ref, mat, arrived.at[0]),
            pltpu.make_async_copy(spread_ref, spread, arrived.at[1]),
        )

    def leave(b, n):
        rows = pl.ds(pl.multiple_of(n * piece, piece), piece)
        lanes = pl.ds(pl.multiple_of(b * block, block), block)
        return pltpu.make_async_copy(
            update.at[b, :, :, rows, :], out_ref.at[:, :, rows, lanes], left.at[b, n]
        )

    @pl.when(step == 0)
    def _():
        for copy in fetches():
            copy.start()

    @pl.when(step < used)
    def _():
        jr = 2 * step + 1
        columns_back(
            ids,
            jr,
            col_off,
            (a_ref.at[0], b_ref.at[0]),
            fr_ref,
            fi_ref,
            cw_ref,
            image,
            quarter * TS,
        )

        def write(k1, row, chunk, value):
            rows = pl.ds(pl.multiple_of(step * part + row, 16), value.shape[0])
            odd[k1, rows, chunk * LANES : (chunk + 1) * LANES] = value.astype(BF16)

        sort_rows(image, row_off[jnp.bitwise_xor(ids[0], jr)], write)

    @pl.when(step == used)
    def _():
        for copy in fetches():
            copy.wait()

    @pl.when(step >= used)
    def _():
        b = step - used
        lanes = pl.ds(pl.multiple_of(b * block, block), block)

        def per_k1(k1, carry):
            rows = jnp.concatenate([even_ref[k1], odd[k1, :, lanes]], axis=0)
            middle[k1] = jnp.dot(mat[k1], rows, preferred_element_type=F32)
            return carry

        lax.fori_loop(0, TS, per_k1, 0, unroll=4)

        def butterfly(chunk, carry):
            n2 = pl.multiple_of(chunk * 16, 16)
            for lane in range(0, block, LANES):
                values = [
                    tuple(
                        middle[
                            k1,
                            pl.ds(pl.multiple_of(z * quarter + n2, 16), 16),
                            lane : lane + LANES,
                        ]
                        for z in range(2)
                    )
                    for k1 in range(TS)
                ]
                for n1, pair in enumerate(dft16(values, 1)):
                    window = spread[pl.ds(pl.multiple_of(n1 * quarter + n2, 16), 16), :]
                    for z in range(2):
                        update[b, z, n1, pl.ds(n2, 16), lane : lane + LANES] = (
                            pair[z] * window
                        ).astype(BF16)
            return carry

        def per_piece(n, carry):
            chunks = piece // 16
            lax.fori_loop(n * chunks, (n + 1) * chunks, butterfly, 0)
            leave(b, n).start()
            return carry

        lax.fori_loop(0, pieces, per_piece, 0)

    @pl.when(step == used + blocks - 1)
    def _():
        for b in range(blocks):
            for n in range(pieces):
                leave(b, n).wait()


def backward(ids, row_off, col_off, halves, tables, col_window, even, matrix, spread):
    used, subs, rows, half = halves[0].shape
    _, depth, width = even.shape
    length = spread.shape[0]
    quarter = length // TS
    block = min(2 * LANES, width)
    blocks = width // block
    pieces = 4

    def early(c, *_):
        return (jnp.minimum(c, used - 1), 0, 0, 0)

    update = pl.pallas_call(
        backward_kernel,
        grid_spec=pltpu.PrefetchScalarGridSpec(
            num_scalar_prefetch=3,
            grid=(used + blocks,),
            in_specs=[pl.BlockSpec((1, subs, rows, half), early)] * 2
            + [pl.BlockSpec((width, SG), lambda c, m, *_: (m[1], 0))] * 2
            + [
                pl.BlockSpec((1, width), lambda c, *_: (0, 0)),
                pl.BlockSpec((TS, depth, block), lambda c, *_: (0, 0, jnp.maximum(c - used, 0))),
                pl.BlockSpec(memory_space=pl.ANY),
                pl.BlockSpec(memory_space=pl.ANY),
            ],
            out_specs=pl.BlockSpec(memory_space=pl.ANY),
            scratch_shapes=[
                image_scratch(width, subs),
                pltpu.VMEM((TS, depth, width), BF16),
                pltpu.VMEM((TS, 2 * quarter, block), F32),
                pltpu.VMEM(matrix.shape, BF16),
                pltpu.VMEM(spread.shape, F32),
                pltpu.VMEM((blocks, 2, TS, quarter, block), BF16),
                pltpu.SemaphoreType.DMA((2,)),
                pltpu.SemaphoreType.DMA((blocks, pieces)),
            ],
        ),
        out_shape=jax.ShapeDtypeStruct((2, TS, quarter, width), BF16),
        compiler_params=pltpu.CompilerParams(vmem_limit_bytes=VMEM_LIMIT),
        name="backward",
    )(ids, row_off, col_off, *halves, *tables, col_window, even, matrix, spread)
    return update.reshape(2, length, width)


def swap(value, axis, bit):
    return lax.ppermute(value, axis, [(i, i ^ bit) for i in range(lax.axis_size(axis))])


def bits_of(axis):
    return [(axis, 1 << n) for n in range(lax.axis_size(axis).bit_length() - 1)]


def orders():
    facet, sub = bits_of("facet")[1:], bits_of("sub")
    rest = facet[1:] + sub[1:]
    return facet[:1] + sub[:1] + rest, sub[:1] + facet[:1] + rest


def dimensions():
    return bits_of("facet")[:0:-1] + bits_of("sub")[::-1]


def sum_blocks(kept, sent, beside, operand):
    values = [k + swap(s, "facet", 1) for k, s in zip(kept, sent)]
    values, operand = lax.optimization_barrier((values, operand))
    extra = beside(operand)
    left = [dimensions(), dimensions()]
    values = [value.reshape((2,) * len(left[0]) + value.shape[2:]) for value in values]

    def halve(n, step):
        at = left[n].index(step)
        left[n].remove(step)
        mine = lax.index_in_dim(values[n], 0, at, keepdims=False)
        return mine, swap(lax.index_in_dim(values[n], 1, at, keepdims=False), *step)

    steps = list(zip(*orders()))
    for pair in steps[:-1]:
        halved = [halve(n, step) for n, step in enumerate(pair)]
        if pair is steps[0]:
            halved, extra = lax.optimization_barrier((halved, extra))
        values = [mine + arrived for mine, arrived in halved]
    last = [halve(n, step) for n, step in enumerate(steps[-1])]
    return last[0] + last[1], extra


def gather_blocks(halves, facet_count, sub_count, beside, operand):
    shape = halves[0].shape
    every = dimensions()
    have = [[], []]
    values = list(halves)

    def grow(n, step):
        at = len([d for d in every if d in have[n] and every.index(d) < every.index(step)])
        have[n].append(step)
        values[n] = jnp.stack([values[n], swap(values[n], *step)], axis=at)

    steps = list(zip(*[order[::-1] for order in orders()]))
    for pair in steps[:-1]:
        for n, step in enumerate(pair):
            grow(n, step)
    values, operand = lax.optimization_barrier((values, operand))
    extra = beside(operand)
    for n, step in enumerate(steps[-1]):
        grow(n, step)
    values, extra = lax.optimization_barrier((values, extra))
    result = []
    for value in values:
        value = value.reshape((facet_count // 2, sub_count) + shape)
        result.append((value, swap(value, "facet", 1)))
    return result, extra


def per_device(
    facet_strips,
    row_window,
    col_window,
    row_offsets,
    col_offsets,
    tile_owner,
    measured,
    vis_weight,
    uvw_pixels,
    vis_count,
):
    sub_count = lax.axis_size("sub")
    facet_count = lax.axis_size("facet")
    _, length, strip_width = facet_strips.shape
    full_width = strip_width * sub_count
    ids = jnp.stack([lax.axis_index("facet"), lax.axis_index("sub")]).astype(jnp.int32)
    row_win = row_window.reshape(length // LANES, LANES)
    col_win = col_window.reshape(1, strip_width)
    row_consts = row_tables(length)
    col_consts = column_tables(full_width)

    spectrum, *sent = forward(
        ids,
        row_offsets,
        col_offsets,
        facet_strips,
        row_win,
        col_win,
        row_consts,
        col_consts,
        sub_count,
    )
    spectrum = spectrum.reshape(facet_count // 2, 2, SG, strip_width)
    kept = cols_forward(ids, spectrum, col_consts, sub_count)

    owners = tile_owner.reshape(-1)
    slots = measured.shape[2]
    capacity = slots // sub_count
    padded = -(-capacity // GROUP) * GROUP
    groups = padded // GROUP

    def per_slot(value):
        if padded == capacity:
            return value
        value = value.reshape((sub_count, capacity) + value.shape[1:])
        value = jnp.pad(value, ((0, 0), (0, padded - capacity)) + ((0, 0),) * (value.ndim - 2))
        return value.reshape((sub_count * padded,) + value.shape[2:])

    visits = vis_weight.shape[3]
    live = jnp.arange(visits, dtype=jnp.int32)[None, :] < vis_count[0, 0][:, None]
    weights = per_slot(jnp.where(live, vis_weight[0, 0], 0.0))
    values = jnp.transpose(per_slot(measured[0, 0]), (1, 0, 2))
    pixels = jnp.transpose(per_slot(uvw_pixels[0, 0]), (1, 0, 2))

    parts, (row_kernels, col_kernels) = sum_blocks(kept, sent, partial(kernels, steps=4), pixels)
    routed = route(ids, owners, parts, sub_count, groups)
    outgoing, where = routed[:-1], routed[-1]
    arrived = [outgoing[0]] + [swap(outgoing[r], "sub", r) for r in range(1, sub_count)]
    returned = []
    for first in range(0, sub_count, sub_count // 2):
        chosen = arrived[first : first + sub_count // 2]
        answered = visit(ids, first, chosen, values, weights, row_kernels, col_kernels)
        returned += [
            swap(value, "sub", first + n) if first + n else value
            for n, value in enumerate(answered)
        ]
    halves = unroute(where, returned, 2 * SG // sub_count)

    ((a_own, a_other), (b_own, b_other)), (matrix, spread) = gather_blocks(
        halves,
        facet_count,
        sub_count,
        lambda window: adjoint_tables(ids, row_offsets, row_consts, window),
        row_win,
    )
    even = cols_backward(
        ids, row_offsets, col_offsets, (a_own, b_own), col_consts, col_win, length
    )
    return backward(
        ids,
        row_offsets,
        col_offsets,
        (a_other, b_other),
        col_consts,
        col_win,
        even,
        matrix,
        spread,
    )


def solution(mesh):
    in_specs = (
        P(None, "facet", "sub"),
        P(),
        P("sub"),
        P(),
        P(),
        P("sub", "facet", None, None),
        P("facet", "sub", None, None, None),
        P("facet", "sub", None, None),
        P("facet", "sub", None, None, None),
        P("facet", "sub", None),
    )
    out_specs = P(None, "facet", "sub")
    return jax.shard_map(
        per_device, mesh=mesh, in_specs=in_specs, out_specs=out_specs, check_vma=False
    )
```

```python
from functools import partial
import math

import jax
import jax.numpy as jnp
import numpy as np
from jax import lax
from jax.experimental import pallas as pl
from jax.experimental.pallas import tpu as pltpu
from jax.sharding import PartitionSpec as P

SG = 512
TS = 16
LANES = 128
GROUP = LANES // TS

kernel_width = 2.5
kernel_norm = 0.565

VMEM_LIMIT = 56 * 1024 * 1024
F32 = jnp.float32
BF16 = jnp.bfloat16


def column_order():
    lane = np.arange(SG)
    chunk, b, cl = lane // LANES, (lane % LANES) // GROUP, lane % GROUP
    return TS * (GROUP * chunk + cl) + b


def column_tables(full_width):
    turns = np.outer(np.arange(full_width, dtype=np.int64), column_order()) % full_width
    angles = turns * (2.0 * np.pi / full_width)
    return (
        jnp.asarray(np.cos(angles).astype(BF16)),
        jnp.asarray((-np.sin(angles)).astype(BF16)),
    )


def row_tables(length):
    q = np.arange(TS)[:, None] + TS * np.arange(SG // TS)[None, :]
    turns = (q[:, :, None] * np.arange(length // TS)[None, None, :]) % length
    angles = turns * (2.0 * np.pi / length)
    return (
        jnp.asarray(np.cos(angles).astype(np.float32)),
        jnp.asarray((-np.sin(angles)).astype(np.float32)),
    )


def radix4(x, direction):
    (r0, i0), (r1, i1), (r2, i2), (r3, i3) = x
    sr, si, dr, di = r0 + r2, i0 + i2, r0 - r2, i0 - i2
    tr, ti, er, ei = r1 + r3, i1 + i3, r1 - r3, i1 - i3
    if direction < 0:
        fr, fi = ei, -er
    else:
        fr, fi = -ei, er
    return [(sr + tr, si + ti), (dr + fr, di + fi), (sr - tr, si - ti), (dr - fr, di - fi)]


def turn(value, step, direction):
    r, i = value
    step = step % TS
    if step == 0:
        return value
    if step == 4:
        return (-i, r) if direction > 0 else (i, -r)
    angle = direction * 2.0 * math.pi * step / TS
    if step == 2:
        h = math.sqrt(0.5)
        return (h * (r - i), h * (r + i)) if direction > 0 else (h * (r + i), h * (i - r))
    if step == 6:
        h = math.sqrt(0.5)
        return (-h * (r + i), h * (r - i)) if direction > 0 else (h * (i - r), -h * (r + i))
    c, s = math.cos(angle), math.sin(angle)
    return (c * r - s * i, s * r + c * i)


def dft16(x, direction):
    inner = [radix4([x[4 * a + b] for a in range(4)], direction) for b in range(4)]
    out = [None] * 16
    for c in range(4):
        column = radix4([turn(inner[b][c], b * c, direction) for b in range(4)], direction)
        for d in range(4):
            out[c + 4 * d] = column[d]
    return out


def wave(turns, length):
    angles = turns.astype(F32) * (2.0 * math.pi / length)
    return jnp.cos(angles), -jnp.sin(angles)


def row_phase(ids, row_off, jr, quarter, facets):
    length = quarter * TS
    off = row_off[jnp.bitwise_xor(ids[0], jr)]
    theta = jnp.bitwise_and(ids[0] * off, facets - 1) * (length // facets)
    n2 = lax.broadcasted_iota(jnp.int32, (1, quarter), 1)
    return wave(jnp.bitwise_and(n2 * off + theta, length - 1), length)


def col_level(ids, col_off, jr, window, full_width, length):
    width = window.shape[1]
    off = col_off[jnp.bitwise_xor(ids[0], jr)]
    c = ids[1] * width + lax.broadcasted_iota(jnp.int32, (1, width), 1)
    cosine, sine = wave(jnp.bitwise_and(c * off, full_width - 1), full_width)
    level = window * (1.0 / math.sqrt(length * full_width))
    return level * cosine, level * sine


def spread_window(window_ref, spread):
    def one(i, carry):
        row = jnp.broadcast_to(window_ref[pl.ds(i, 1), :], (LANES, LANES))
        spread[pl.ds(pl.multiple_of(i * LANES, LANES), LANES), :] = row.T
        return carry

    lax.fori_loop(0, window_ref.shape[0], one, 0, unroll=8)


def place_of(jr, count):
    return (jr % 2) * (count // 2) + jr // 2


def fill_matrix(ids, row_off, tables, write, count):
    t_r, t_i = tables
    quarter = t_r.shape[2]
    phases = [row_phase(ids, row_off, jr, quarter, count) for jr in range(count)]

    def per_q1(q1, carry):
        a_r, a_i = t_r[q1], t_i[q1]
        for jr, (d_r, d_i) in enumerate(phases):
            m_r = a_r * d_r - a_i * d_i
            m_i = a_r * d_i + a_i * d_r
            upper = jnp.concatenate([m_r, -m_i], axis=1)
            lower = jnp.concatenate([m_i, m_r], axis=1)
            block = jnp.concatenate([upper, lower], axis=0).astype(BF16)
            off = row_off[jnp.bitwise_xor(ids[0], jr)]
            write(jnp.bitwise_and(off + q1, TS - 1), place_of(jr, count), block)
        return carry

    lax.fori_loop(0, TS, per_q1, 0)


def exchange(first, second):
    upper = lax.broadcasted_iota(jnp.int32, first.shape, 0) < 4
    return (
        jnp.where(upper, first, pltpu.roll(second, 4, 0)),
        jnp.where(upper, pltpu.roll(first, 4, 0), second),
    )


def columns_out(real, imag, f_r, f_i, full):
    for z, (u, v) in enumerate(((f_r, -f_i), (f_i, f_r))):
        sums = jnp.dot(real, u, preferred_element_type=F32)
        sums += jnp.dot(imag, v, preferred_element_type=F32)
        for chunk in range(SG // LANES):
            full[z, chunk] = sums[:, chunk * LANES : (chunk + 1) * LANES]


def send_blocks(full, me, subs, a_ref, b_ref, at):
    tile_rows = SG // TS // subs
    q2 = SG // TS
    chunks = SG // LANES

    def store(place, row, chunk, value):
        out_ref = a_ref if chunk < chunks // 2 else b_ref
        lane = (chunk % (chunks // 2)) * LANES
        out_ref[at, place, row : row + TS, lane : lane + LANES] = value.astype(BF16)

    if tile_rows == 4:

        def per_pair(m, carry):
            for z in range(2):
                for chunk in range(chunks):
                    for quad in range(0, TS, 4):
                        v = [
                            full[z, chunk, pl.ds(pl.multiple_of((quad + n) * q2 + m * 8, 8), 8), :]
                            for n in range(4)
                        ]
                        pairs = [exchange(v[0], v[1]), exchange(v[2], v[3])]
                        for n in range(2):
                            value = jnp.concatenate([pairs[0][n], pairs[1][n]], axis=0)
                            place = jnp.bitwise_xor(2 * m + n, me)
                            store(place, z * TS * tile_rows + quad * tile_rows, chunk, value)
            return carry

        lax.fori_loop(0, subs // 2, per_pair, 0)
    else:
        assert tile_rows == 1

        def per_block(s, carry):
            for z in range(2):
                for chunk in range(chunks):
                    value = full[z, chunk, pl.ds(s, TS, stride=q2), :]
                    store(jnp.bitwise_xor(s, me), z * TS, chunk, value)
            return carry

        lax.fori_loop(0, subs, per_block, 0)


def forward_kernel(
    ids,
    row_off,
    col_off,
    x_ref,
    rw_ref,
    cw_ref,
    tr_ref,
    ti_ref,
    fr_ref,
    fi_ref,
    kept_ref,
    a_ref,
    b_ref,
    strips,
    arrived,
    mat,
    inner,
    spread,
    level,
    odd,
    full,
):
    count = level.shape[0]
    quarter = tr_ref.shape[2]
    length = quarter * TS
    blocks, _, _, block = strips.shape
    width = fr_ref.shape[0]
    subs = a_ref.shape[1]
    part = 2 * (SG // TS)
    step = pl.program_id(0)

    def fetch(b):
        lanes = pl.ds(pl.multiple_of(b * block, block), block)
        return pltpu.make_async_copy(x_ref.at[:, :, lanes], strips.at[b], arrived.at[b])

    @pl.when(step == 0)
    def _():
        for b in range(blocks):
            fetch(b).start()

        def write(k1, place, value):
            mat[k1, place * part : (place + 1) * part, :] = value

        fill_matrix(ids, row_off, (tr_ref, ti_ref), write, count)
        spread_window(rw_ref, spread)
        for jr in range(count):
            l_r, l_i = col_level(ids, col_off, jr, cw_ref[...], width * subs, length)
            level[jr, 0:1, :] = l_r
            level[jr, 1:2, :] = l_i

    @pl.when(step < blocks)
    def _():
        fetch(step).wait()

        def butterfly(chunk, carry):
            n2 = pl.multiple_of(chunk * 16, 16)
            for lane in range(0, block, LANES):
                values = []
                for n1 in range(TS):
                    rows = pl.ds(pl.multiple_of(n1 * quarter + n2, 16), 16)
                    window = spread[rows, :]
                    values.append(
                        tuple(
                            strips[step, z, rows, lane : lane + LANES].astype(F32) * window
                            for z in range(2)
                        )
                    )
                for k1, pair in enumerate(dft16(values, -1)):
                    for z in range(2):
                        rows = pl.ds(pl.multiple_of(z * quarter + n2, 16), 16)
                        inner[k1, rows, lane : lane + LANES] = pair[z].astype(BF16)
            return carry

        lax.fori_loop(0, quarter // 16, butterfly, 0)
        lanes = pl.ds(pl.multiple_of(step * block, block), block)

        def per_k1(k1, carry):
            sums = jnp.dot(mat[k1], inner[k1], preferred_element_type=F32)
            for jr in range(count):
                off = row_off[jnp.bitwise_xor(ids[0], jr)]
                q1 = jnp.bitwise_and(k1 - off, TS - 1)
                at = place_of(jr, count) * part
                real = sums[at : at + part // 2]
                imag = sums[at + part // 2 : at + part]
                l_r, l_i = level[jr, 0:1, lanes], level[jr, 1:2, lanes]
                out_r = (real * l_r - imag * l_i).astype(BF16)
                out_i = (real * l_i + imag * l_r).astype(BF16)
                if jr % 2:
                    odd[jr // 2, 0, q1, :, lanes] = out_r
                    odd[jr // 2, 1, q1, :, lanes] = out_i
                else:
                    kept_ref[jr // 2, 0, q1] = out_r
                    kept_ref[jr // 2, 1, q1] = out_i
            return carry

        lax.fori_loop(0, TS, per_k1, 0, unroll=4)

    @pl.when(step >= blocks)
    def _():
        j = step - blocks
        columns_out(
            odd[j, 0].reshape(SG, width),
            odd[j, 1].reshape(SG, width),
            fr_ref[...],
            fi_ref[...],
            full,
        )
        send_blocks(full, ids[1], subs, a_ref, b_ref, 0)


def forward(ids, row_off, col_off, strips, row_window, col_window, row_consts, col_consts, subs):
    _, length, width = strips.shape
    count = row_off.shape[0]
    quarter = length // TS
    q2 = SG // TS
    block = min(2 * LANES, width)
    blocks = width // block
    half = SG // 2
    used = count // 2
    rows = 2 * SG // subs
    sent = jax.ShapeDtypeStruct((used, subs, rows, half), BF16)
    kept = jax.ShapeDtypeStruct((used, 2, TS, q2, width), BF16)

    def late(c, *_):
        return (jnp.maximum(c - blocks, 0), 0, 0, 0)

    return pl.pallas_call(
        forward_kernel,
        grid_spec=pltpu.PrefetchScalarGridSpec(
            num_scalar_prefetch=3,
            grid=(blocks + used,),
            in_specs=[
                pl.BlockSpec(memory_space=pl.ANY),
                pl.BlockSpec((length // LANES, LANES), lambda c, *_: (0, 0)),
                pl.BlockSpec((1, width), lambda c, *_: (0, 0)),
                pl.BlockSpec((TS, q2, quarter), lambda c, *_: (0, 0, 0)),
                pl.BlockSpec((TS, q2, quarter), lambda c, *_: (0, 0, 0)),
                pl.BlockSpec((width, SG), lambda c, m, *_: (m[1], 0)),
                pl.BlockSpec((width, SG), lambda c, m, *_: (m[1], 0)),
            ],
            out_specs=[
                pl.BlockSpec(
                    (used, 2, TS, q2, block),
                    lambda c, *_: (0, 0, 0, 0, jnp.minimum(c, blocks - 1)),
                ),
                pl.BlockSpec((1, subs, rows, half), late),
                pl.BlockSpec((1, subs, rows, half), late),
            ],
            scratch_shapes=[
                pltpu.VMEM((blocks, 2, length, block), BF16),
                pltpu.SemaphoreType.DMA((blocks,)),
                pltpu.VMEM((TS, count * 2 * q2, 2 * quarter), BF16),
                pltpu.VMEM((TS, 2 * quarter, block), BF16),
                pltpu.VMEM((length, LANES), F32),
                pltpu.VMEM((count, 2, width), F32),
                pltpu.VMEM((used, 2, TS, q2, width), BF16),
                pltpu.VMEM((2, SG // LANES, SG, LANES), F32),
            ],
        ),
        out_shape=[kept, sent, sent],
        compiler_params=pltpu.CompilerParams(vmem_limit_bytes=VMEM_LIMIT),
        cost_estimate=pl.CostEstimate(
            flops=12_000_000_000, bytes_accessed=16 << 20, transcendentals=0
        ),
        name="forward",
    )(ids, row_off, col_off, strips, row_window, col_window, *row_consts, *col_consts)


def cols_forward_kernel(ids, r_ref, fr_ref, fi_ref, a_ref, b_ref, full):
    columns_out(r_ref[0, 0], r_ref[0, 1], fr_ref[...], fi_ref[...], full)
    send_blocks(full, ids[1], a_ref.shape[1], a_ref, b_ref, 0)


def cols_forward(ids, rows, tables, subs):
    used, _, _, width = rows.shape
    block_rows = 2 * SG // subs
    half = SG // 2
    shape = jax.ShapeDtypeStruct((used, subs, block_rows, half), BF16)
    return pl.pallas_call(
        cols_forward_kernel,
        grid_spec=pltpu.PrefetchScalarGridSpec(
            num_scalar_prefetch=1,
            grid=(used,),
            in_specs=[
                pl.BlockSpec((1, 2, SG, width), lambda j, m: (j, 0, 0, 0)),
                pl.BlockSpec((width, SG), lambda j, m: (m[1], 0)),
                pl.BlockSpec((width, SG), lambda j, m: (m[1], 0)),
            ],
            out_specs=[pl.BlockSpec((1, subs, block_rows, half), lambda j, m: (j, 0, 0, 0))] * 2,
            scratch_shapes=[pltpu.VMEM((2, SG // LANES, SG, LANES), F32)],
        ),
        out_shape=[shape, shape],
        compiler_params=pltpu.CompilerParams(vmem_limit_bytes=VMEM_LIMIT),
        cost_estimate=pl.CostEstimate(
            flops=4_000_000_000, bytes_accessed=6 << 20, transcendentals=0
        ),
        name="cols_forward",
    )(ids, rows, *tables)


def route_kernel(ids, owner_ref, *refs):
    subs = len(refs) - 8
    parts, outs = refs[:4], refs[4 : 4 + subs]
    where_ref, held, slots, counts = refs[4 + subs :]
    chunks = SG // LANES
    tile_rows = held.shape[1] // (2 * TS)
    groups = outs[0].shape[0]
    me = ids[1]
    for h in range(2):
        total = parts[2 * h][...].astype(F32) + parts[2 * h + 1][...].astype(F32)
        for c in range(chunks // 2):
            held[h * (chunks // 2) + c] = total[:, c * LANES : (c + 1) * LANES]

    def clear(g, carry):
        slots[g] = jnp.zeros(slots.shape[1:], F32)
        return carry

    lax.fori_loop(0, slots.shape[0], clear, 0, unroll=8)
    for o in range(subs):
        counts[o] = 0
    lane = lax.broadcasted_iota(jnp.int32, (2 * TS, LANES), 1) % GROUP

    def per_chunk(n, carry):
        value = held[n % chunks, pl.ds(n // chunks, 2 * TS, stride=tile_rows), :]
        for cl in range(GROUP):
            t = n * GROUP + cl
            owner = owner_ref[t]
            rank = counts[owner]
            counts[owner] = rank + 1
            g = jnp.bitwise_xor(owner, me) * groups + rank // GROUP
            sl = rank % GROUP
            where_ref[t] = g * GROUP + sl
            moved = pltpu.roll(value, jnp.bitwise_and(sl - cl, LANES - 1), 1)
            slots[g] = jnp.where(lane == sl, moved, slots[g])
        return carry

    lax.fori_loop(0, tile_rows * chunks, per_chunk, 0, unroll=4)
    for o in range(subs):
        outs[o][...] = slots[o * groups : (o + 1) * groups].astype(BF16)


def route(ids, owners, parts, subs, groups):
    rows = parts[0].shape[0]
    smem = pl.BlockSpec(memory_space=pltpu.SMEM)
    vmem = pl.BlockSpec(memory_space=pltpu.VMEM)
    block = jax.ShapeDtypeStruct((groups, 2 * TS, LANES), BF16)
    return pl.pallas_call(
        route_kernel,
        in_specs=[smem, smem] + [vmem] * 4,
        out_specs=[vmem] * subs + [smem],
        out_shape=[block] * subs + [jax.ShapeDtypeStruct(owners.shape, jnp.int32)],
        scratch_shapes=[
            pltpu.VMEM((SG // LANES, rows, LANES), F32),
            pltpu.VMEM((subs * groups, 2 * TS, LANES), F32),
            pltpu.SMEM((subs,), jnp.int32),
        ],
        compiler_params=pltpu.CompilerParams(vmem_limit_bytes=VMEM_LIMIT),
        name="route",
    )(ids, owners, *parts)


def unroute_kernel(where_ref, *refs):
    subs = len(refs) - 4
    ins, (a_ref, b_ref, slots, held) = refs[:subs], refs[subs:]
    groups = ins[0].shape[0]
    chunks = SG // LANES
    tile_rows = held.shape[1] // (2 * TS)
    for o in range(subs):
        slots[o * groups : (o + 1) * groups] = ins[o][...].astype(F32)
    lane = lax.broadcasted_iota(jnp.int32, (2 * TS, LANES), 1) % GROUP

    def per_row(r2, carry):
        for chunk in range(chunks):
            total = jnp.zeros((2 * TS, LANES), F32)
            for cl in range(GROUP):
                slot = where_ref[(r2 * chunks + chunk) * GROUP + cl]
                moved = pltpu.roll(
                    slots[slot // GROUP], jnp.bitwise_and(cl - slot % GROUP, LANES - 1), 1
                )
                total = jnp.where(lane == cl, moved, total)
            held[chunk, pl.ds(r2, 2 * TS, stride=tile_rows), :] = total
        return carry

    lax.fori_loop(0, tile_rows, per_row, 0, unroll=2 if tile_rows > 1 else 1)
    for chunk in range(chunks):
        out_ref = a_ref if chunk < chunks // 2 else b_ref
        at = (chunk % (chunks // 2)) * LANES
        out_ref[:, at : at + LANES] = held[chunk].astype(BF16)


def unroute(where, blocks, rows):
    groups = blocks[0].shape[0]
    smem = pl.BlockSpec(memory_space=pltpu.SMEM)
    vmem = pl.BlockSpec(memory_space=pltpu.VMEM)
    half = jax.ShapeDtypeStruct((rows, SG // 2), BF16)
    return pl.pallas_call(
        unroute_kernel,
        in_specs=[smem] + [vmem] * len(blocks),
        out_specs=[vmem] * 2,
        out_shape=[half] * 2,
        scratch_shapes=[
            pltpu.VMEM((len(blocks) * groups, 2 * TS, LANES), F32),
            pltpu.VMEM((SG // LANES, rows, LANES), F32),
        ],
        compiler_params=pltpu.CompilerParams(vmem_limit_bytes=VMEM_LIMIT),
        name="unroute",
    )(where, *blocks)


def falloffs(centre):
    spread = kernel_width * kernel_width
    c = centre.astype(F32)
    value = kernel_norm * jnp.exp(c * c * (-1.0 / spread))
    ratio = jnp.exp((2.0 * c - 1.0) * (1.0 / spread))
    out = [value]
    for _ in range(1, TS):
        value = value * ratio
        ratio = ratio * math.exp(-2.0 / spread)
        out.append(value)
    return out


def plane_phases(plane):
    base_r, base_i = wave(plane, TS * TS)
    step_r, step_i = base_r * base_r - base_i * base_i, 2.0 * base_r * base_i
    value_r, value_i, turn_r, turn_i = base_r, base_i, base_r, base_i
    out = [(None, None), (value_r, value_i)]
    for _ in range(2, TS // 2 + 1):
        turn_r, turn_i = (
            turn_r * step_r - turn_i * step_i,
            turn_r * step_i + turn_i * step_r,
        )
        value_r, value_i = (
            value_r * turn_r - value_i * turn_i,
            value_r * turn_i + value_i * turn_r,
        )
        out.append((value_r, value_i))
    return out


def kernels_kernel(pixel_ref, row_ref, col_ref):
    def one(g, carry):
        at = pl.ds(pl.multiple_of(g * GROUP, GROUP), GROUP)
        across, along = falloffs(pixel_ref[0, at, :]), falloffs(pixel_ref[1, at, :])
        phases = plane_phases(pixel_ref[2, at, :])
        zero = jnp.zeros(across[0].shape, F32)

        def times(falls, a, z):
            if a == TS // 2:
                return zero if z else falls[a]
            return falls[a] * phases[abs(a - TS // 2)][z]

        for a in range(0, TS, 2):
            rows = pl.ds(a * GROUP, 2 * GROUP)
            for z in range(2):
                row = jnp.concatenate([times(across, a, z), times(across, a + 1, z)], axis=0)
                col = jnp.concatenate([times(along, a, z), times(along, a + 1, z)], axis=0)
                row_ref[g, z, rows, :] = row.astype(BF16)
                col_ref[g, rows, z * LANES : (z + 1) * LANES] = col.astype(BF16)
        return carry

    lax.fori_loop(0, row_ref.shape[0], one, 0, unroll=2)


def kernels(pixels, steps):
    slots = pixels.shape[1]
    groups = slots // GROUP
    rows = TS * GROUP
    return pl.pallas_call(
        kernels_kernel,
        grid=(steps,),
        in_specs=[pl.BlockSpec((3, slots // steps, LANES), lambda i: (0, i, 0))],
        out_specs=[
            pl.BlockSpec((groups // steps, 2, rows, LANES), lambda i: (i, 0, 0, 0)),
            pl.BlockSpec((groups // steps, rows, 2 * LANES), lambda i: (i, 0, 0)),
        ],
        out_shape=[
            jax.ShapeDtypeStruct((groups, 2, rows, LANES), BF16),
            jax.ShapeDtypeStruct((groups, rows, 2 * LANES), BF16),
        ],
        compiler_params=pltpu.CompilerParams(vmem_limit_bytes=VMEM_LIMIT),
        cost_estimate=pl.CostEstimate(
            flops=6_000_000_000, bytes_accessed=9 << 20, transcendentals=0
        ),
        name="kernels",
    )(pixels)


def visit_kernel(ids, *refs):
    n = (len(refs) - 7) // 2
    ins, outs = refs[:n], refs[n + 5 : 2 * n + 5]
    meas_ref, weight_ref, row_ref, col_ref, mask_ref = refs[n : n + 5]
    held, wide = refs[-2:]
    groups = held.shape[0]
    rows = TS * GROUP
    lane = lax.broadcasted_iota(jnp.int32, (2 * TS, LANES), 1) % GROUP

    def one(g, v):
        at = pl.ds(g * GROUP, GROUP)
        blocks = jnp.concatenate(
            [held[g, pl.ds(k, 1), :] * mask_ref[...] for k in range(2 * TS)], axis=0
        ).astype(BF16)
        col = col_ref[g]
        sums = jnp.dot(blocks, col, preferred_element_type=F32)
        part_r = sums[:rows, :LANES] - sums[rows:, LANES:]
        part_i = sums[:rows, LANES:] + sums[rows:, :LANES]
        row_r, row_i = row_ref[g, 0].astype(F32), row_ref[g, 1].astype(F32)
        pred_r = jnp.sum((row_r * part_r - row_i * part_i).reshape(TS, GROUP, LANES), axis=0)
        pred_i = jnp.sum((row_r * part_i + row_i * part_r).reshape(TS, GROUP, LANES), axis=0)
        weight = weight_ref[at, :]
        res_r = jnp.tile(weight * (meas_ref[0, at, :] - pred_r), (TS, 1))
        res_i = jnp.tile(weight * (meas_ref[1, at, :] - pred_i), (TS, 1))
        s_r = (row_r * res_r + row_i * res_i).astype(BF16)
        s_i = (row_r * res_i - row_i * res_r).astype(BF16)
        both = jnp.concatenate(
            [jnp.concatenate([s_r, s_i], axis=1), jnp.concatenate([s_i, -s_r], axis=1)], axis=0
        )
        wide[v] = lax.dot_general(both, col, (((1,), (1,)), ((), ())), preferred_element_type=F32)
        total = wide[v, pl.ds(0, 2 * TS, stride=GROUP), :]
        for slot in range(1, GROUP):
            total = jnp.where(lane == slot, wide[v, pl.ds(slot, 2 * TS, stride=GROUP), :], total)
        return total.astype(BF16)

    for i in range(n):

        @pl.when(pl.program_id(0) == i)
        def _(i=i):
            held[...] = ins[i][...].astype(F32)
            for g, value in enumerate([one(g, g) for g in range(groups)]):
                outs[i][g] = value


def visit(ids, first, blocks, measured, weight, row, col):
    n = len(blocks)
    shape = blocks[0].shape
    groups = shape[0]
    slots = groups * GROUP
    rows = TS * GROUP
    mask = np.arange(GROUP)[:, None] == np.arange(LANES)[None, :] % GROUP
    whole = pl.BlockSpec(shape, lambda i, m: (0, 0, 0))

    def source(i, m):
        return jnp.bitwise_xor(m[1], first + i)

    return pl.pallas_call(
        visit_kernel,
        grid_spec=pltpu.PrefetchScalarGridSpec(
            num_scalar_prefetch=1,
            grid=(n,),
            in_specs=[whole] * n
            + [
                pl.BlockSpec((2, slots, LANES), lambda i, m: (0, source(i, m), 0)),
                pl.BlockSpec((slots, LANES), lambda i, m: (source(i, m), 0)),
                pl.BlockSpec((groups, 2, rows, LANES), lambda i, m: (source(i, m), 0, 0, 0)),
                pl.BlockSpec((groups, rows, 2 * LANES), lambda i, m: (source(i, m), 0, 0)),
                pl.BlockSpec((GROUP, LANES), lambda i, m: (0, 0)),
            ],
            out_specs=[whole] * n,
            scratch_shapes=[
                pltpu.VMEM((groups, 2 * TS, LANES), F32),
                pltpu.VMEM((groups, 2 * rows, LANES), F32),
            ],
        ),
        out_shape=[jax.ShapeDtypeStruct(b.shape, b.dtype) for b in blocks],
        compiler_params=pltpu.CompilerParams(vmem_limit_bytes=VMEM_LIMIT),
        cost_estimate=pl.CostEstimate(
            flops=1_800_000_000 * n, bytes_accessed=(5 << 18) * n, transcendentals=0
        ),
        name="visit",
    )(ids, *blocks, measured, weight, row, col, jnp.asarray(mask.astype(np.float32)))


def columns_back(ids, jr, col_off, halves, fr_ref, fi_ref, cw_ref, image, length):
    subs, rows, half = halves[0].shape
    width = fr_ref.shape[0]
    block = rows // 2

    def times(left, right):
        return lax.dot_general(left, right, (((1,), (1,)), ((), ())), preferred_element_type=F32)

    real = imag = 0.0
    for h, ref in enumerate(halves):
        p_r = ref[:, :block, :].reshape(subs * block, half)
        p_i = ref[:, block:, :].reshape(subs * block, half)
        f_r = fr_ref[:, h * half : (h + 1) * half]
        f_i = fi_ref[:, h * half : (h + 1) * half]
        real += times(p_r, f_r) + times(p_i, f_i)
        imag += times(p_i, f_r) + times(p_r, -f_i)
    l_r, l_i = col_level(ids, col_off, jr, cw_ref[...], width * subs, length)
    for z, value in enumerate((real * l_r + imag * l_i, imag * l_r - real * l_i)):
        for s in range(subs):
            for chunk in range(width // LANES):
                image[z, chunk, jnp.bitwise_xor(s, ids[1])] = value[
                    s * block : (s + 1) * block, chunk * LANES : (chunk + 1) * LANES
                ]


def sort_rows(image, off, write):
    _, chunks, subs, block, _ = image.shape
    tile_rows = block // TS
    q2 = SG // TS

    def k1_of(q1):
        return jnp.bitwise_and(off + q1, TS - 1)

    if tile_rows == 4:

        def per_pair(pair, carry):
            rows = pl.ds(pl.multiple_of(pair * 8, 8), 8)
            for z in range(2):
                for chunk in range(chunks):
                    for s in range(0, subs, 4):
                        v = [image[z, chunk, s + n, rows, :] for n in range(4)]
                        pairs = [exchange(v[0], v[1]), exchange(v[2], v[3])]
                        for n in range(2):
                            value = jnp.concatenate([pairs[0][n], pairs[1][n]], axis=0)
                            write(k1_of(2 * pair + n), z * q2 + s * tile_rows, chunk, value)
            return carry

        lax.fori_loop(0, TS // 2, per_pair, 0)
    else:
        assert tile_rows == 1
        for q1 in range(TS):
            for z in range(2):
                for chunk in range(chunks):
                    value = jnp.concatenate(
                        [image[z, chunk, s, q1 : q1 + 1, :] for s in range(subs)], axis=0
                    )
                    write(k1_of(q1), z * q2, chunk, value)


def cols_backward_kernel(
    ids, row_off, col_off, a_ref, b_ref, fr_ref, fi_ref, cw_ref, out_ref, image, *, length
):
    jr = 2 * pl.program_id(0)
    columns_back(
        ids, jr, col_off, (a_ref.at[0], b_ref.at[0]), fr_ref, fi_ref, cw_ref, image, length
    )

    def write(k1, row, chunk, value):
        lanes = slice(chunk * LANES, (chunk + 1) * LANES)
        out_ref[k1, row : row + value.shape[0], lanes] = value.astype(BF16)

    sort_rows(image, row_off[jnp.bitwise_xor(ids[0], jr)], write)


def image_scratch(width, subs):
    return pltpu.VMEM((2, width // LANES, subs, SG // subs, LANES), F32)


def cols_backward(ids, row_off, col_off, halves, tables, col_window, length):
    used, subs, rows, half = halves[0].shape
    width = col_window.shape[1]
    part = 2 * (SG // TS)
    return pl.pallas_call(
        partial(cols_backward_kernel, length=length),
        grid_spec=pltpu.PrefetchScalarGridSpec(
            num_scalar_prefetch=3,
            grid=(used,),
            in_specs=[pl.BlockSpec((1, subs, rows, half), lambda j, *_: (j, 0, 0, 0))] * 2
            + [pl.BlockSpec((width, SG), lambda j, m, *_: (m[1], 0))] * 2
            + [pl.BlockSpec((1, width), lambda j, *_: (0, 0))],
            out_specs=pl.BlockSpec((TS, part, width), lambda j, *_: (0, j, 0)),
            scratch_shapes=[image_scratch(width, subs)],
        ),
        out_shape=jax.ShapeDtypeStruct((TS, used * part, width), BF16),
        compiler_params=pltpu.CompilerParams(vmem_limit_bytes=VMEM_LIMIT),
        cost_estimate=pl.CostEstimate(
            flops=5_000_000_000, bytes_accessed=6 << 20, transcendentals=0
        ),
        name="cols_backward",
    )(ids, row_off, col_off, *halves, *tables, col_window)


def adjoint_tables_kernel(ids, row_off, tr_ref, ti_ref, rw_ref, out_ref, spread_ref, mat):
    part = 2 * (SG // TS)

    def write(k1, place, block):
        mat[k1, place * part : (place + 1) * part, :] = block.astype(F32)

    fill_matrix(ids, row_off, (tr_ref, ti_ref), write, row_off.shape[0])

    def per_k1(k1, carry):
        out_ref[k1] = mat[k1].T.astype(BF16)
        return carry

    lax.fori_loop(0, TS, per_k1, 0)
    spread_window(rw_ref, spread_ref)


def adjoint_tables(ids, row_off, tables, row_window):
    count = row_off.shape[0]
    quarter = tables[0].shape[2]
    part = 2 * (SG // TS)
    vmem = pl.BlockSpec(memory_space=pltpu.VMEM)
    smem = pl.BlockSpec(memory_space=pltpu.SMEM)
    return pl.pallas_call(
        adjoint_tables_kernel,
        in_specs=[smem] * 2 + [vmem] * 3,
        out_specs=[vmem] * 2,
        out_shape=[
            jax.ShapeDtypeStruct((TS, 2 * quarter, count * part), BF16),
            jax.ShapeDtypeStruct((row_window.size, LANES), F32),
        ],
        scratch_shapes=[pltpu.VMEM((TS, count * part, 2 * quarter), F32)],
        compiler_params=pltpu.CompilerParams(vmem_limit_bytes=VMEM_LIMIT),
        cost_estimate=pl.CostEstimate(
            flops=7_000_000_000, bytes_accessed=7 << 20, transcendentals=0
        ),
        name="adjoint_tables",
    )(ids, row_off, *tables, row_window)


def backward_kernel(
    ids,
    row_off,
    col_off,
    a_ref,
    b_ref,
    fr_ref,
    fi_ref,
    cw_ref,
    even_ref,
    mat_ref,
    spread_ref,
    out_ref,
    image,
    odd,
    middle,
    mat,
    spread,
    update,
    arrived,
    left,
):
    used = row_off.shape[0] // 2
    quarter = mat.shape[1] // 2
    blocks, _, _, _, block = update.shape
    pieces = left.shape[1]
    piece = quarter // pieces
    part = 2 * (SG // TS)
    step = pl.program_id(0)

    def fetches():
        return (
            pltpu.make_async_copy(mat_ref, mat, arrived.at[0]),
            pltpu.make_async_copy(spread_ref, spread, arrived.at[1]),
        )

    def leave(b, n):
        rows = pl.ds(pl.multiple_of(n * piece, piece), piece)
        lanes = pl.ds(pl.multiple_of(b * block, block), block)
        return pltpu.make_async_copy(
            update.at[b, :, :, rows, :], out_ref.at[:, :, rows, lanes], left.at[b, n]
        )

    @pl.when(step == 0)
    def _():
        for copy in fetches():
            copy.start()

    @pl.when(step < used)
    def _():
        jr = 2 * step + 1
        columns_back(
            ids,
            jr,
            col_off,
            (a_ref.at[0], b_ref.at[0]),
            fr_ref,
            fi_ref,
            cw_ref,
            image,
            quarter * TS,
        )

        def write(k1, row, chunk, value):
            rows = pl.ds(pl.multiple_of(step * part + row, 16), value.shape[0])
            odd[k1, rows, chunk * LANES : (chunk + 1) * LANES] = value.astype(BF16)

        sort_rows(image, row_off[jnp.bitwise_xor(ids[0], jr)], write)

    @pl.when(step == used)
    def _():
        for copy in fetches():
            copy.wait()

    @pl.when(step >= used)
    def _():
        b = step - used
        lanes = pl.ds(pl.multiple_of(b * block, block), block)

        def per_k1(k1, carry):
            rows = jnp.concatenate([even_ref[k1], odd[k1, :, lanes]], axis=0)
            middle[k1] = jnp.dot(mat[k1], rows, preferred_element_type=F32)
            return carry

        lax.fori_loop(0, TS, per_k1, 0, unroll=4)

        def butterfly(chunk, carry):
            n2 = pl.multiple_of(chunk * 16, 16)
            for lane in range(0, block, LANES):
                values = [
                    tuple(
                        middle[
                            k1,
                            pl.ds(pl.multiple_of(z * quarter + n2, 16), 16),
                            lane : lane + LANES,
                        ]
                        for z in range(2)
                    )
                    for k1 in range(TS)
                ]
                for n1, pair in enumerate(dft16(values, 1)):
                    window = spread[pl.ds(pl.multiple_of(n1 * quarter + n2, 16), 16), :]
                    for z in range(2):
                        update[b, z, n1, pl.ds(n2, 16), lane : lane + LANES] = (
                            pair[z] * window
                        ).astype(BF16)
            return carry

        def per_piece(n, carry):
            chunks = piece // 16
            lax.fori_loop(n * chunks, (n + 1) * chunks, butterfly, 0)
            leave(b, n).start()
            return carry

        lax.fori_loop(0, pieces, per_piece, 0)

    @pl.when(step == used + blocks - 1)
    def _():
        for b in range(blocks):
            for n in range(pieces):
                leave(b, n).wait()


def backward(ids, row_off, col_off, halves, tables, col_window, even, matrix, spread):
    used, subs, rows, half = halves[0].shape
    _, depth, width = even.shape
    length = spread.shape[0]
    quarter = length // TS
    block = min(2 * LANES, width)
    blocks = width // block
    pieces = 4

    def early(c, *_):
        return (jnp.minimum(c, used - 1), 0, 0, 0)

    update = pl.pallas_call(
        backward_kernel,
        grid_spec=pltpu.PrefetchScalarGridSpec(
            num_scalar_prefetch=3,
            grid=(used + blocks,),
            in_specs=[pl.BlockSpec((1, subs, rows, half), early)] * 2
            + [pl.BlockSpec((width, SG), lambda c, m, *_: (m[1], 0))] * 2
            + [
                pl.BlockSpec((1, width), lambda c, *_: (0, 0)),
                pl.BlockSpec((TS, depth, block), lambda c, *_: (0, 0, jnp.maximum(c - used, 0))),
                pl.BlockSpec(memory_space=pl.ANY),
                pl.BlockSpec(memory_space=pl.ANY),
            ],
            out_specs=pl.BlockSpec(memory_space=pl.ANY),
            scratch_shapes=[
                image_scratch(width, subs),
                pltpu.VMEM((TS, depth, width), BF16),
                pltpu.VMEM((TS, 2 * quarter, block), F32),
                pltpu.VMEM(matrix.shape, BF16),
                pltpu.VMEM(spread.shape, F32),
                pltpu.VMEM((blocks, 2, TS, quarter, block), BF16),
                pltpu.SemaphoreType.DMA((2,)),
                pltpu.SemaphoreType.DMA((blocks, pieces)),
            ],
        ),
        out_shape=jax.ShapeDtypeStruct((2, TS, quarter, width), BF16),
        compiler_params=pltpu.CompilerParams(vmem_limit_bytes=VMEM_LIMIT),
        name="backward",
    )(ids, row_off, col_off, *halves, *tables, col_window, even, matrix, spread)
    return update.reshape(2, length, width)


def swap(value, axis, bit):
    return lax.ppermute(value, axis, [(i, i ^ bit) for i in range(lax.axis_size(axis))])


def bits_of(axis):
    return [(axis, 1 << n) for n in range(lax.axis_size(axis).bit_length() - 1)]


def orders():
    facet, sub = bits_of("facet")[1:], bits_of("sub")
    rest = facet[1:] + sub[1:]
    return facet[:1] + sub[:1] + rest, sub[:1] + facet[:1] + rest


def dimensions():
    return bits_of("facet")[:0:-1] + bits_of("sub")[::-1]


def sum_blocks(kept, sent, beside, operand):
    values = [k + swap(s, "facet", 1) for k, s in zip(kept, sent)]
    values[0], operand = lax.optimization_barrier((values[0], operand))
    extra = beside(operand)
    left = [dimensions(), dimensions()]
    values = [value.reshape((2,) * len(left[0]) + value.shape[2:]) for value in values]

    def halve(n, step):
        at = left[n].index(step)
        left[n].remove(step)
        mine = lax.index_in_dim(values[n], 0, at, keepdims=False)
        return mine, swap(lax.index_in_dim(values[n], 1, at, keepdims=False), *step)

    steps = list(zip(*orders()))
    for pair in steps[:-1]:
        halved = [halve(n, step) for n, step in enumerate(pair)]
        if pair is steps[0]:
            halved, extra = lax.optimization_barrier((halved, extra))
        values = [mine + arrived for mine, arrived in halved]
    last = [halve(n, step) for n, step in enumerate(steps[-1])]
    return last[0] + last[1], extra


def gather_blocks(halves, facet_count, sub_count, beside, operand):
    shape = halves[0].shape
    every = dimensions()
    have = [[], []]
    values = list(halves)

    def grow(n, step):
        at = len([d for d in every if d in have[n] and every.index(d) < every.index(step)])
        have[n].append(step)
        values[n] = jnp.stack([values[n], swap(values[n], *step)], axis=at)

    steps = list(zip(*[order[::-1] for order in orders()]))
    for pair in steps[:-1]:
        for n, step in enumerate(pair):
            grow(n, step)
    values, operand = lax.optimization_barrier((values, operand))
    extra = beside(operand)
    for n, step in enumerate(steps[-1]):
        grow(n, step)
    values, extra = lax.optimization_barrier((values, extra))
    result = []
    for value in values:
        value = value.reshape((facet_count // 2, sub_count) + shape)
        result.append((value, swap(value, "facet", 1)))
    return result, extra


def per_device(
    facet_strips,
    row_window,
    col_window,
    row_offsets,
    col_offsets,
    tile_owner,
    measured,
    vis_weight,
    uvw_pixels,
    vis_count,
):
    sub_count = lax.axis_size("sub")
    facet_count = lax.axis_size("facet")
    _, length, strip_width = facet_strips.shape
    full_width = strip_width * sub_count
    ids = jnp.stack([lax.axis_index("facet"), lax.axis_index("sub")]).astype(jnp.int32)
    row_win = row_window.reshape(length // LANES, LANES)
    col_win = col_window.reshape(1, strip_width)
    row_consts = row_tables(length)
    col_consts = column_tables(full_width)

    spectrum, *sent = forward(
        ids,
        row_offsets,
        col_offsets,
        facet_strips,
        row_win,
        col_win,
        row_consts,
        col_consts,
        sub_count,
    )
    spectrum = spectrum.reshape(facet_count // 2, 2, SG, strip_width)
    kept = cols_forward(ids, spectrum, col_consts, sub_count)

    owners = tile_owner.reshape(-1)
    slots = measured.shape[2]
    capacity = slots // sub_count
    padded = -(-capacity // GROUP) * GROUP
    groups = padded // GROUP

    def per_slot(value):
        if padded == capacity:
            return value
        value = value.reshape((sub_count, capacity) + value.shape[1:])
        value = jnp.pad(value, ((0, 0), (0, padded - capacity)) + ((0, 0),) * (value.ndim - 2))
        return value.reshape((sub_count * padded,) + value.shape[2:])

    def prepare(operand):
        pixels, values, weights, counts = operand
        live = jnp.arange(weights.shape[1], dtype=jnp.int32)[None, :] < counts[:, None]
        weights = per_slot(jnp.where(live, weights, 0.0))
        values = jnp.transpose(per_slot(values), (1, 0, 2))
        pixels = jnp.transpose(per_slot(pixels), (1, 0, 2))
        return values, weights, kernels(pixels, 4)

    parts, (values, weights, (row_kernels, col_kernels)) = sum_blocks(
        kept,
        sent,
        prepare,
        (uvw_pixels[0, 0], measured[0, 0], vis_weight[0, 0], vis_count[0, 0]),
    )
    routed = route(ids, owners, parts, sub_count, groups)
    outgoing, where = routed[:-1], routed[-1]
    arrived = [outgoing[0]] + [swap(outgoing[r], "sub", r) for r in range(1, sub_count)]
    returned = []
    for first in range(0, sub_count, sub_count // 2):
        chosen = arrived[first : first + sub_count // 2]
        answered = visit(ids, first, chosen, values, weights, row_kernels, col_kernels)
        returned += [
            swap(value, "sub", first + n) if first + n else value
            for n, value in enumerate(answered)
        ]
    halves = unroute(where, returned, 2 * SG // sub_count)

    ((a_own, a_other), (b_own, b_other)), (matrix, spread) = gather_blocks(
        halves,
        facet_count,
        sub_count,
        lambda window: adjoint_tables(ids, row_offsets, row_consts, window),
        row_win,
    )
    even = cols_backward(
        ids, row_offsets, col_offsets, (a_own, b_own), col_consts, col_win, length
    )
    return backward(
        ids,
        row_offsets,
        col_offsets,
        (a_other, b_other),
        col_consts,
        col_win,
        even,
        matrix,
        spread,
    )


def solution(mesh):
    in_specs = (
        P(None, "facet", "sub"),
        P(),
        P("sub"),
        P(),
        P(),
        P("sub", "facet", None, None),
        P("facet", "sub", None, None, None),
        P("facet", "sub", None, None),
        P("facet", "sub", None, None, None),
        P("facet", "sub", None),
    )
    out_specs = P(None, "facet", "sub")
    return jax.shard_map(
        per_device, mesh=mesh, in_specs=in_specs, out_specs=out_specs, check_vma=False
    )
```

```python
from functools import partial
import math

import jax
import jax.numpy as jnp
import numpy as np
from jax import lax
from jax.experimental import pallas as pl
from jax.experimental.pallas import tpu as pltpu
from jax.sharding import PartitionSpec as P

SG = 512
TS = 16
LANES = 128
GROUP = LANES // TS

kernel_width = 2.5
kernel_norm = 0.565

VMEM_LIMIT = 56 * 1024 * 1024
F32 = jnp.float32
BF16 = jnp.bfloat16


def column_order():
    lane = np.arange(SG)
    chunk, b, cl = lane // LANES, (lane % LANES) // GROUP, lane % GROUP
    return TS * (GROUP * chunk + cl) + b


def column_tables(full_width):
    turns = np.outer(np.arange(full_width, dtype=np.int64), column_order()) % full_width
    angles = turns * (2.0 * np.pi / full_width)
    return (
        jnp.asarray(np.cos(angles).astype(BF16)),
        jnp.asarray((-np.sin(angles)).astype(BF16)),
    )


def row_tables(length):
    q = np.arange(TS)[:, None] + TS * np.arange(SG // TS)[None, :]
    turns = (q[:, :, None] * np.arange(length // TS)[None, None, :]) % length
    angles = turns * (2.0 * np.pi / length)
    return (
        jnp.asarray(np.cos(angles).astype(np.float32)),
        jnp.asarray((-np.sin(angles)).astype(np.float32)),
    )


def radix4(x, direction):
    (r0, i0), (r1, i1), (r2, i2), (r3, i3) = x
    sr, si, dr, di = r0 + r2, i0 + i2, r0 - r2, i0 - i2
    tr, ti, er, ei = r1 + r3, i1 + i3, r1 - r3, i1 - i3
    if direction < 0:
        fr, fi = ei, -er
    else:
        fr, fi = -ei, er
    return [(sr + tr, si + ti), (dr + fr, di + fi), (sr - tr, si - ti), (dr - fr, di - fi)]


def turn(value, step, direction):
    r, i = value
    step = step % TS
    if step == 0:
        return value
    if step == 4:
        return (-i, r) if direction > 0 else (i, -r)
    angle = direction * 2.0 * math.pi * step / TS
    if step == 2:
        h = math.sqrt(0.5)
        return (h * (r - i), h * (r + i)) if direction > 0 else (h * (r + i), h * (i - r))
    if step == 6:
        h = math.sqrt(0.5)
        return (-h * (r + i), h * (r - i)) if direction > 0 else (h * (i - r), -h * (r + i))
    c, s = math.cos(angle), math.sin(angle)
    return (c * r - s * i, s * r + c * i)


def dft16(x, direction):
    inner = [radix4([x[4 * a + b] for a in range(4)], direction) for b in range(4)]
    out = [None] * 16
    for c in range(4):
        column = radix4([turn(inner[b][c], b * c, direction) for b in range(4)], direction)
        for d in range(4):
            out[c + 4 * d] = column[d]
    return out


def wave(turns, length):
    angles = turns.astype(F32) * (2.0 * math.pi / length)
    return jnp.cos(angles), -jnp.sin(angles)


def row_phase(ids, row_off, jr, quarter, facets):
    length = quarter * TS
    off = row_off[jnp.bitwise_xor(ids[0], jr)]
    theta = jnp.bitwise_and(ids[0] * off, facets - 1) * (length // facets)
    n2 = lax.broadcasted_iota(jnp.int32, (1, quarter), 1)
    return wave(jnp.bitwise_and(n2 * off + theta, length - 1), length)


def col_level(ids, col_off, jr, window, full_width, length):
    width = window.shape[1]
    off = col_off[jnp.bitwise_xor(ids[0], jr)]
    c = ids[1] * width + lax.broadcasted_iota(jnp.int32, (1, width), 1)
    cosine, sine = wave(jnp.bitwise_and(c * off, full_width - 1), full_width)
    level = window * (1.0 / math.sqrt(length * full_width))
    return level * cosine, level * sine


def spread_window(window_ref, spread):
    def one(i, carry):
        row = jnp.broadcast_to(window_ref[pl.ds(i, 1), :], (LANES, LANES))
        spread[pl.ds(pl.multiple_of(i * LANES, LANES), LANES), :] = row.T
        return carry

    lax.fori_loop(0, window_ref.shape[0], one, 0, unroll=16)


def place_of(jr, count):
    return (jr % 2) * (count // 2) + jr // 2


def fill_matrix(ids, row_off, tables, write, count):
    t_r, t_i = tables
    quarter = t_r.shape[2]
    phases = [row_phase(ids, row_off, jr, quarter, count) for jr in range(count)]

    def per_q1(q1, carry):
        a_r, a_i = t_r[q1], t_i[q1]
        for jr, (d_r, d_i) in enumerate(phases):
            m_r = a_r * d_r - a_i * d_i
            m_i = a_r * d_i + a_i * d_r
            upper = jnp.concatenate([m_r, -m_i], axis=1)
            lower = jnp.concatenate([m_i, m_r], axis=1)
            block = jnp.concatenate([upper, lower], axis=0).astype(BF16)
            off = row_off[jnp.bitwise_xor(ids[0], jr)]
            write(jnp.bitwise_and(off + q1, TS - 1), place_of(jr, count), block)
        return carry

    lax.fori_loop(0, TS, per_q1, 0, unroll=4)


def exchange(first, second):
    upper = lax.broadcasted_iota(jnp.int32, first.shape, 0) < 4
    return (
        jnp.where(upper, first, pltpu.roll(second, 4, 0)),
        jnp.where(upper, pltpu.roll(first, 4, 0), second),
    )


def columns_out(real, imag, f_r, f_i, full):
    for z, (u, v) in enumerate(((f_r, -f_i), (f_i, f_r))):
        sums = jnp.dot(real, u, preferred_element_type=F32)
        sums += jnp.dot(imag, v, preferred_element_type=F32)
        for chunk in range(SG // LANES):
            full[z, chunk] = sums[:, chunk * LANES : (chunk + 1) * LANES]


def send_blocks(full, me, subs, a_ref, b_ref, at):
    tile_rows = SG // TS // subs
    q2 = SG // TS
    chunks = SG // LANES

    def store(place, row, chunk, value):
        out_ref = a_ref if chunk < chunks // 2 else b_ref
        lane = (chunk % (chunks // 2)) * LANES
        out_ref[at, place, row : row + TS, lane : lane + LANES] = value.astype(BF16)

    if tile_rows == 4:

        def per_pair(m, carry):
            for z in range(2):
                for chunk in range(chunks):
                    for quad in range(0, TS, 4):
                        v = [
                            full[z, chunk, pl.ds(pl.multiple_of((quad + n) * q2 + m * 8, 8), 8), :]
                            for n in range(4)
                        ]
                        pairs = [exchange(v[0], v[1]), exchange(v[2], v[3])]
                        for n in range(2):
                            value = jnp.concatenate([pairs[0][n], pairs[1][n]], axis=0)
                            place = jnp.bitwise_xor(2 * m + n, me)
                            store(place, z * TS * tile_rows + quad * tile_rows, chunk, value)
            return carry

        lax.fori_loop(0, subs // 2, per_pair, 0, unroll=True)
    else:
        assert tile_rows == 1

        def per_block(s, carry):
            for z in range(2):
                for chunk in range(chunks):
                    value = full[z, chunk, pl.ds(s, TS, stride=q2), :]
                    store(jnp.bitwise_xor(s, me), z * TS, chunk, value)
            return carry

        lax.fori_loop(0, subs, per_block, 0)


def forward_kernel(
    ids,
    row_off,
    col_off,
    x_ref,
    rw_ref,
    cw_ref,
    tr_ref,
    ti_ref,
    fr_ref,
    fi_ref,
    kept_ref,
    a_ref,
    b_ref,
    strips,
    arrived,
    mat,
    inner,
    spread,
    level,
    odd,
    full,
):
    count = level.shape[0]
    quarter = tr_ref.shape[2]
    length = quarter * TS
    blocks, _, _, block = strips.shape
    width = fr_ref.shape[0]
    subs = a_ref.shape[1]
    part = 2 * (SG // TS)
    step = pl.program_id(0)

    def fetch(b):
        lanes = pl.ds(pl.multiple_of(b * block, block), block)
        return pltpu.make_async_copy(x_ref.at[:, :, lanes], strips.at[b], arrived.at[b])

    @pl.when(step == 0)
    def _():
        for b in range(blocks):
            fetch(b).start()

        def write(k1, place, value):
            mat[k1, place * part : (place + 1) * part, :] = value

        fill_matrix(ids, row_off, (tr_ref, ti_ref), write, count)
        spread_window(rw_ref, spread)
        for jr in range(count):
            l_r, l_i = col_level(ids, col_off, jr, cw_ref[...], width * subs, length)
            level[jr, 0:1, :] = l_r
            level[jr, 1:2, :] = l_i

    @pl.when(step < blocks)
    def _():
        fetch(step).wait()

        def butterfly(chunk, carry):
            n2 = pl.multiple_of(chunk * 16, 16)
            for lane in range(0, block, LANES):
                values = []
                for n1 in range(TS):
                    rows = pl.ds(pl.multiple_of(n1 * quarter + n2, 16), 16)
                    window = spread[rows, :]
                    values.append(
                        tuple(
                            strips[step, z, rows, lane : lane + LANES].astype(F32) * window
                            for z in range(2)
                        )
                    )
                for k1, pair in enumerate(dft16(values, -1)):
                    for z in range(2):
                        rows = pl.ds(pl.multiple_of(z * quarter + n2, 16), 16)
                        inner[k1, rows, lane : lane + LANES] = pair[z].astype(BF16)
            return carry

        lax.fori_loop(0, quarter // 16, butterfly, 0)
        lanes = pl.ds(pl.multiple_of(step * block, block), block)

        def per_k1(k1, carry):
            sums = jnp.dot(mat[k1], inner[k1], preferred_element_type=F32)
            for jr in range(count):
                off = row_off[jnp.bitwise_xor(ids[0], jr)]
                q1 = jnp.bitwise_and(k1 - off, TS - 1)
                at = place_of(jr, count) * part
                real = sums[at : at + part // 2]
                imag = sums[at + part // 2 : at + part]
                l_r, l_i = level[jr, 0:1, lanes], level[jr, 1:2, lanes]
                out_r = (real * l_r - imag * l_i).astype(BF16)
                out_i = (real * l_i + imag * l_r).astype(BF16)
                if jr % 2:
                    odd[jr // 2, 0, q1, :, lanes] = out_r
                    odd[jr // 2, 1, q1, :, lanes] = out_i
                else:
                    kept_ref[jr // 2, 0, q1] = out_r
                    kept_ref[jr // 2, 1, q1] = out_i
            return carry

        lax.fori_loop(0, TS, per_k1, 0, unroll=16)

    @pl.when(step >= blocks)
    def _():
        j = step - blocks
        columns_out(
            odd[j, 0].reshape(SG, width),
            odd[j, 1].reshape(SG, width),
            fr_ref[...],
            fi_ref[...],
            full,
        )
        send_blocks(full, ids[1], subs, a_ref, b_ref, 0)


def forward(ids, row_off, col_off, strips, row_window, col_window, row_consts, col_consts, subs):
    _, length, width = strips.shape
    count = row_off.shape[0]
    quarter = length // TS
    q2 = SG // TS
    block = min(2 * LANES, width)
    blocks = width // block
    half = SG // 2
    used = count // 2
    rows = 2 * SG // subs
    sent = jax.ShapeDtypeStruct((used, subs, rows, half), BF16)
    kept = jax.ShapeDtypeStruct((used, 2, TS, q2, width), BF16)

    def late(c, *_):
        return (jnp.maximum(c - blocks, 0), 0, 0, 0)

    return pl.pallas_call(
        forward_kernel,
        grid_spec=pltpu.PrefetchScalarGridSpec(
            num_scalar_prefetch=3,
            grid=(blocks + used,),
            in_specs=[
                pl.BlockSpec(memory_space=pl.ANY),
                pl.BlockSpec((length // LANES, LANES), lambda c, *_: (0, 0)),
                pl.BlockSpec((1, width), lambda c, *_: (0, 0)),
                pl.BlockSpec((TS, q2, quarter), lambda c, *_: (0, 0, 0)),
                pl.BlockSpec((TS, q2, quarter), lambda c, *_: (0, 0, 0)),
                pl.BlockSpec((width, SG), lambda c, m, *_: (m[1], 0)),
                pl.BlockSpec((width, SG), lambda c, m, *_: (m[1], 0)),
            ],
            out_specs=[
                pl.BlockSpec(
                    (used, 2, TS, q2, block),
                    lambda c, *_: (0, 0, 0, 0, jnp.minimum(c, blocks - 1)),
                ),
                pl.BlockSpec((1, subs, rows, half), late),
                pl.BlockSpec((1, subs, rows, half), late),
            ],
            scratch_shapes=[
                pltpu.VMEM((blocks, 2, length, block), BF16),
                pltpu.SemaphoreType.DMA((blocks,)),
                pltpu.VMEM((TS, count * 2 * q2, 2 * quarter), BF16),
                pltpu.VMEM((TS, 2 * quarter, block), BF16),
                pltpu.VMEM((length, LANES), F32),
                pltpu.VMEM((count, 2, width), F32),
                pltpu.VMEM((used, 2, TS, q2, width), BF16),
                pltpu.VMEM((2, SG // LANES, SG, LANES), F32),
            ],
        ),
        out_shape=[kept, sent, sent],
        compiler_params=pltpu.CompilerParams(vmem_limit_bytes=VMEM_LIMIT),
        cost_estimate=pl.CostEstimate(
            flops=12_000_000_000, bytes_accessed=16 << 20, transcendentals=0
        ),
        name="forward",
    )(ids, row_off, col_off, strips, row_window, col_window, *row_consts, *col_consts)


def cols_forward_kernel(ids, r_ref, fr_ref, fi_ref, a_ref, b_ref, full):
    columns_out(r_ref[0, 0], r_ref[0, 1], fr_ref[...], fi_ref[...], full)
    send_blocks(full, ids[1], a_ref.shape[1], a_ref, b_ref, 0)


def cols_forward(ids, rows, tables, subs):
    used, _, _, width = rows.shape
    block_rows = 2 * SG // subs
    half = SG // 2
    shape = jax.ShapeDtypeStruct((used, subs, block_rows, half), BF16)
    return pl.pallas_call(
        cols_forward_kernel,
        grid_spec=pltpu.PrefetchScalarGridSpec(
            num_scalar_prefetch=1,
            grid=(used,),
            in_specs=[
                pl.BlockSpec((1, 2, SG, width), lambda j, m: (j, 0, 0, 0)),
                pl.BlockSpec((width, SG), lambda j, m: (m[1], 0)),
                pl.BlockSpec((width, SG), lambda j, m: (m[1], 0)),
            ],
            out_specs=[pl.BlockSpec((1, subs, block_rows, half), lambda j, m: (j, 0, 0, 0))] * 2,
            scratch_shapes=[pltpu.VMEM((2, SG // LANES, SG, LANES), F32)],
        ),
        out_shape=[shape, shape],
        compiler_params=pltpu.CompilerParams(vmem_limit_bytes=VMEM_LIMIT),
        cost_estimate=pl.CostEstimate(
            flops=4_000_000_000, bytes_accessed=6 << 20, transcendentals=0
        ),
        name="cols_forward",
    )(ids, rows, *tables)


def route_kernel(ids, owner_ref, *refs):
    subs = len(refs) - 8
    parts, outs = refs[:4], refs[4 : 4 + subs]
    where_ref, held, slots, counts = refs[4 + subs :]
    chunks = SG // LANES
    tile_rows = held.shape[1] // (2 * TS)
    groups = outs[0].shape[0]
    me = ids[1]
    for h in range(2):
        total = parts[2 * h][...].astype(F32) + parts[2 * h + 1][...].astype(F32)
        for c in range(chunks // 2):
            held[h * (chunks // 2) + c] = total[:, c * LANES : (c + 1) * LANES]

    def clear(g, carry):
        slots[g] = jnp.zeros(slots.shape[1:], F32)
        return carry

    lax.fori_loop(0, slots.shape[0], clear, 0, unroll=8)
    for o in range(subs):
        counts[o] = 0
    lane = lax.broadcasted_iota(jnp.int32, (2 * TS, LANES), 1) % GROUP

    def per_chunk(n, carry):
        value = held[n % chunks, pl.ds(n // chunks, 2 * TS, stride=tile_rows), :]
        for cl in range(GROUP):
            t = n * GROUP + cl
            owner = owner_ref[t]
            rank = counts[owner]
            counts[owner] = rank + 1
            g = jnp.bitwise_xor(owner, me) * groups + rank // GROUP
            sl = rank % GROUP
            where_ref[t] = g * GROUP + sl
            moved = pltpu.roll(value, jnp.bitwise_and(sl - cl, LANES - 1), 1)
            slots[g] = jnp.where(lane == sl, moved, slots[g])
        return carry

    lax.fori_loop(0, tile_rows * chunks, per_chunk, 0, unroll=4)
    for o in range(subs):
        outs[o][...] = slots[o * groups : (o + 1) * groups].astype(BF16)


def route(ids, owners, parts, subs, groups):
    rows = parts[0].shape[0]
    smem = pl.BlockSpec(memory_space=pltpu.SMEM)
    vmem = pl.BlockSpec(memory_space=pltpu.VMEM)
    block = jax.ShapeDtypeStruct((groups, 2 * TS, LANES), BF16)
    return pl.pallas_call(
        route_kernel,
        in_specs=[smem, smem] + [vmem] * 4,
        out_specs=[vmem] * subs + [smem],
        out_shape=[block] * subs + [jax.ShapeDtypeStruct(owners.shape, jnp.int32)],
        scratch_shapes=[
            pltpu.VMEM((SG // LANES, rows, LANES), F32),
            pltpu.VMEM((subs * groups, 2 * TS, LANES), F32),
            pltpu.SMEM((subs,), jnp.int32),
        ],
        compiler_params=pltpu.CompilerParams(vmem_limit_bytes=VMEM_LIMIT),
        name="route",
    )(ids, owners, *parts)


def unroute_kernel(where_ref, *refs):
    subs = len(refs) - 4
    ins, (a_ref, b_ref, slots, held) = refs[:subs], refs[subs:]
    groups = ins[0].shape[0]
    chunks = SG // LANES
    tile_rows = held.shape[1] // (2 * TS)
    for o in range(subs):
        slots[o * groups : (o + 1) * groups] = ins[o][...].astype(F32)
    lane = lax.broadcasted_iota(jnp.int32, (2 * TS, LANES), 1) % GROUP

    def per_row(r2, carry):
        for chunk in range(chunks):
            total = jnp.zeros((2 * TS, LANES), F32)
            for cl in range(GROUP):
                slot = where_ref[(r2 * chunks + chunk) * GROUP + cl]
                moved = pltpu.roll(
                    slots[slot // GROUP], jnp.bitwise_and(cl - slot % GROUP, LANES - 1), 1
                )
                total = jnp.where(lane == cl, moved, total)
            held[chunk, pl.ds(r2, 2 * TS, stride=tile_rows), :] = total
        return carry

    lax.fori_loop(0, tile_rows, per_row, 0, unroll=2 if tile_rows > 1 else 1)
    for chunk in range(chunks):
        out_ref = a_ref if chunk < chunks // 2 else b_ref
        at = (chunk % (chunks // 2)) * LANES
        out_ref[:, at : at + LANES] = held[chunk].astype(BF16)


def unroute(where, blocks, rows):
    groups = blocks[0].shape[0]
    smem = pl.BlockSpec(memory_space=pltpu.SMEM)
    vmem = pl.BlockSpec(memory_space=pltpu.VMEM)
    half = jax.ShapeDtypeStruct((rows, SG // 2), BF16)
    return pl.pallas_call(
        unroute_kernel,
        in_specs=[smem] + [vmem] * len(blocks),
        out_specs=[vmem] * 2,
        out_shape=[half] * 2,
        scratch_shapes=[
            pltpu.VMEM((len(blocks) * groups, 2 * TS, LANES), F32),
            pltpu.VMEM((SG // LANES, rows, LANES), F32),
        ],
        compiler_params=pltpu.CompilerParams(vmem_limit_bytes=VMEM_LIMIT),
        name="unroute",
    )(where, *blocks)


def falloffs(centre):
    spread = kernel_width * kernel_width
    c = centre.astype(F32)
    value = kernel_norm * jnp.exp(c * c * (-1.0 / spread))
    ratio = jnp.exp((2.0 * c - 1.0) * (1.0 / spread))
    out = [value]
    for _ in range(1, TS):
        value = value * ratio
        ratio = ratio * math.exp(-2.0 / spread)
        out.append(value)
    return out


def plane_phases(plane):
    base_r, base_i = wave(plane, TS * TS)
    step_r, step_i = base_r * base_r - base_i * base_i, 2.0 * base_r * base_i
    value_r, value_i, turn_r, turn_i = base_r, base_i, base_r, base_i
    out = [(None, None), (value_r, value_i)]
    for _ in range(2, TS // 2 + 1):
        turn_r, turn_i = (
            turn_r * step_r - turn_i * step_i,
            turn_r * step_i + turn_i * step_r,
        )
        value_r, value_i = (
            value_r * turn_r - value_i * turn_i,
            value_r * turn_i + value_i * turn_r,
        )
        out.append((value_r, value_i))
    return out


def kernels_kernel(pixel_ref, row_ref, col_ref):
    def one(g, carry):
        at = pl.ds(pl.multiple_of(g * GROUP, GROUP), GROUP)
        across, along = falloffs(pixel_ref[0, at, :]), falloffs(pixel_ref[1, at, :])
        phases = plane_phases(pixel_ref[2, at, :])
        zero = jnp.zeros(across[0].shape, F32)

        def times(falls, a, z):
            if a == TS // 2:
                return zero if z else falls[a]
            return falls[a] * phases[abs(a - TS // 2)][z]

        for a in range(0, TS, 2):
            rows = pl.ds(a * GROUP, 2 * GROUP)
            for z in range(2):
                row = jnp.concatenate([times(across, a, z), times(across, a + 1, z)], axis=0)
                col = jnp.concatenate([times(along, a, z), times(along, a + 1, z)], axis=0)
                row_ref[g, z, rows, :] = row.astype(BF16)
                col_ref[g, rows, z * LANES : (z + 1) * LANES] = col.astype(BF16)
        return carry

    lax.fori_loop(0, row_ref.shape[0], one, 0, unroll=2)


def kernels(pixels, steps):
    slots = pixels.shape[1]
    groups = slots // GROUP
    rows = TS * GROUP
    return pl.pallas_call(
        kernels_kernel,
        grid=(steps,),
        in_specs=[pl.BlockSpec((3, slots // steps, LANES), lambda i: (0, i, 0))],
        out_specs=[
            pl.BlockSpec((groups // steps, 2, rows, LANES), lambda i: (i, 0, 0, 0)),
            pl.BlockSpec((groups // steps, rows, 2 * LANES), lambda i: (i, 0, 0)),
        ],
        out_shape=[
            jax.ShapeDtypeStruct((groups, 2, rows, LANES), BF16),
            jax.ShapeDtypeStruct((groups, rows, 2 * LANES), BF16),
        ],
        compiler_params=pltpu.CompilerParams(vmem_limit_bytes=VMEM_LIMIT),
        cost_estimate=pl.CostEstimate(
            flops=6_000_000_000, bytes_accessed=9 << 20, transcendentals=0
        ),
        name="kernels",
    )(pixels)


def visit_kernel(ids, *refs):
    n = (len(refs) - 7) // 2
    ins, outs = refs[:n], refs[n + 5 : 2 * n + 5]
    meas_ref, weight_ref, row_ref, col_ref, mask_ref = refs[n : n + 5]
    held, wide = refs[-2:]
    groups = held.shape[0]
    rows = TS * GROUP
    lane = lax.broadcasted_iota(jnp.int32, (2 * TS, LANES), 1) % GROUP

    def one(g, v):
        at = pl.ds(g * GROUP, GROUP)
        blocks = jnp.concatenate(
            [held[g, pl.ds(k, 1), :] * mask_ref[...] for k in range(2 * TS)], axis=0
        ).astype(BF16)
        col = col_ref[g]
        sums = jnp.dot(blocks, col, preferred_element_type=F32)
        part_r = sums[:rows, :LANES] - sums[rows:, LANES:]
        part_i = sums[:rows, LANES:] + sums[rows:, :LANES]
        row_r, row_i = row_ref[g, 0].astype(F32), row_ref[g, 1].astype(F32)
        pred_r = jnp.sum((row_r * part_r - row_i * part_i).reshape(TS, GROUP, LANES), axis=0)
        pred_i = jnp.sum((row_r * part_i + row_i * part_r).reshape(TS, GROUP, LANES), axis=0)
        weight = weight_ref[at, :]
        res_r = jnp.tile(weight * (meas_ref[0, at, :] - pred_r), (TS, 1))
        res_i = jnp.tile(weight * (meas_ref[1, at, :] - pred_i), (TS, 1))
        s_r = (row_r * res_r + row_i * res_i).astype(BF16)
        s_i = (row_r * res_i - row_i * res_r).astype(BF16)
        both = jnp.concatenate(
            [jnp.concatenate([s_r, s_i], axis=1), jnp.concatenate([s_i, -s_r], axis=1)], axis=0
        )
        wide[v] = lax.dot_general(both, col, (((1,), (1,)), ((), ())), preferred_element_type=F32)
        total = wide[v, pl.ds(0, 2 * TS, stride=GROUP), :]
        for slot in range(1, GROUP):
            total = jnp.where(lane == slot, wide[v, pl.ds(slot, 2 * TS, stride=GROUP), :], total)
        return total.astype(BF16)

    for i in range(n):

        @pl.when(pl.program_id(0) == i)
        def _(i=i):
            held[...] = ins[i][...].astype(F32)
            for g, value in enumerate([one(g, g) for g in range(groups)]):
                outs[i][g] = value


def visit(ids, first, blocks, measured, weight, row, col):
    n = len(blocks)
    shape = blocks[0].shape
    groups = shape[0]
    slots = groups * GROUP
    rows = TS * GROUP
    mask = np.arange(GROUP)[:, None] == np.arange(LANES)[None, :] % GROUP
    whole = pl.BlockSpec(shape, lambda i, m: (0, 0, 0))

    def source(i, m):
        return jnp.bitwise_xor(m[1], first + i)

    return pl.pallas_call(
        visit_kernel,
        grid_spec=pltpu.PrefetchScalarGridSpec(
            num_scalar_prefetch=1,
            grid=(n,),
            in_specs=[whole] * n
            + [
                pl.BlockSpec((2, slots, LANES), lambda i, m: (0, source(i, m), 0)),
                pl.BlockSpec((slots, LANES), lambda i, m: (source(i, m), 0)),
                pl.BlockSpec((groups, 2, rows, LANES), lambda i, m: (source(i, m), 0, 0, 0)),
                pl.BlockSpec((groups, rows, 2 * LANES), lambda i, m: (source(i, m), 0, 0)),
                pl.BlockSpec((GROUP, LANES), lambda i, m: (0, 0)),
            ],
            out_specs=[whole] * n,
            scratch_shapes=[
                pltpu.VMEM((groups, 2 * TS, LANES), F32),
                pltpu.VMEM((groups, 2 * rows, LANES), F32),
            ],
        ),
        out_shape=[jax.ShapeDtypeStruct(b.shape, b.dtype) for b in blocks],
        compiler_params=pltpu.CompilerParams(vmem_limit_bytes=VMEM_LIMIT),
        cost_estimate=pl.CostEstimate(
            flops=1_800_000_000 * n, bytes_accessed=(5 << 18) * n, transcendentals=0
        ),
        name="visit",
    )(ids, *blocks, measured, weight, row, col, jnp.asarray(mask.astype(np.float32)))


def columns_back(ids, jr, col_off, halves, fr_ref, fi_ref, cw_ref, image, length):
    subs, rows, half = halves[0].shape
    width = fr_ref.shape[0]
    block = rows // 2

    def times(left, right):
        return lax.dot_general(left, right, (((1,), (1,)), ((), ())), preferred_element_type=F32)

    real = imag = 0.0
    for h, ref in enumerate(halves):
        p_r = ref[:, :block, :].reshape(subs * block, half)
        p_i = ref[:, block:, :].reshape(subs * block, half)
        f_r = fr_ref[:, h * half : (h + 1) * half]
        f_i = fi_ref[:, h * half : (h + 1) * half]
        real += times(p_r, f_r) + times(p_i, f_i)
        imag += times(p_i, f_r) + times(p_r, -f_i)
    l_r, l_i = col_level(ids, col_off, jr, cw_ref[...], width * subs, length)
    for z, value in enumerate((real * l_r + imag * l_i, imag * l_r - real * l_i)):
        for s in range(subs):
            for chunk in range(width // LANES):
                image[z, chunk, jnp.bitwise_xor(s, ids[1])] = value[
                    s * block : (s + 1) * block, chunk * LANES : (chunk + 1) * LANES
                ]


def sort_rows(image, off, write):
    _, chunks, subs, block, _ = image.shape
    tile_rows = block // TS
    q2 = SG // TS

    def k1_of(q1):
        return jnp.bitwise_and(off + q1, TS - 1)

    if tile_rows == 4:

        def per_pair(pair, carry):
            rows = pl.ds(pl.multiple_of(pair * 8, 8), 8)
            for z in range(2):
                for chunk in range(chunks):
                    for s in range(0, subs, 4):
                        v = [image[z, chunk, s + n, rows, :] for n in range(4)]
                        pairs = [exchange(v[0], v[1]), exchange(v[2], v[3])]
                        for n in range(2):
                            value = jnp.concatenate([pairs[0][n], pairs[1][n]], axis=0)
                            write(k1_of(2 * pair + n), z * q2 + s * tile_rows, chunk, value)
            return carry

        lax.fori_loop(0, TS // 2, per_pair, 0, unroll=4)
    else:
        assert tile_rows == 1
        for q1 in range(TS):
            for z in range(2):
                for chunk in range(chunks):
                    value = jnp.concatenate(
                        [image[z, chunk, s, q1 : q1 + 1, :] for s in range(subs)], axis=0
                    )
                    write(k1_of(q1), z * q2, chunk, value)


def cols_backward_kernel(
    ids, row_off, col_off, a_ref, b_ref, fr_ref, fi_ref, cw_ref, out_ref, image, *, length
):
    jr = 2 * pl.program_id(0)
    columns_back(
        ids, jr, col_off, (a_ref.at[0], b_ref.at[0]), fr_ref, fi_ref, cw_ref, image, length
    )

    def write(k1, row, chunk, value):
        lanes = slice(chunk * LANES, (chunk + 1) * LANES)
        out_ref[k1, row : row + value.shape[0], lanes] = value.astype(BF16)

    sort_rows(image, row_off[jnp.bitwise_xor(ids[0], jr)], write)


def image_scratch(width, subs):
    return pltpu.VMEM((2, width // LANES, subs, SG // subs, LANES), F32)


def cols_backward(ids, row_off, col_off, halves, tables, col_window, length):
    used, subs, rows, half = halves[0].shape
    width = col_window.shape[1]
    part = 2 * (SG // TS)
    return pl.pallas_call(
        partial(cols_backward_kernel, length=length),
        grid_spec=pltpu.PrefetchScalarGridSpec(
            num_scalar_prefetch=3,
            grid=(used,),
            in_specs=[pl.BlockSpec((1, subs, rows, half), lambda j, *_: (j, 0, 0, 0))] * 2
            + [pl.BlockSpec((width, SG), lambda j, m, *_: (m[1], 0))] * 2
            + [pl.BlockSpec((1, width), lambda j, *_: (0, 0))],
            out_specs=pl.BlockSpec((TS, part, width), lambda j, *_: (0, j, 0)),
            scratch_shapes=[image_scratch(width, subs)],
        ),
        out_shape=jax.ShapeDtypeStruct((TS, used * part, width), BF16),
        compiler_params=pltpu.CompilerParams(vmem_limit_bytes=VMEM_LIMIT),
        cost_estimate=pl.CostEstimate(
            flops=5_000_000_000, bytes_accessed=6 << 20, transcendentals=0
        ),
        name="cols_backward",
    )(ids, row_off, col_off, *halves, *tables, col_window)


def adjoint_tables_kernel(ids, row_off, tr_ref, ti_ref, rw_ref, out_ref, spread_ref, mat):
    part = 2 * (SG // TS)

    def write(k1, place, block):
        mat[k1, place * part : (place + 1) * part, :] = block.astype(F32)

    fill_matrix(ids, row_off, (tr_ref, ti_ref), write, row_off.shape[0])

    def per_k1(k1, carry):
        out_ref[k1] = mat[k1].T.astype(BF16)
        return carry

    lax.fori_loop(0, TS, per_k1, 0, unroll=4)
    spread_window(rw_ref, spread_ref)


def adjoint_tables(ids, row_off, tables, row_window):
    count = row_off.shape[0]
    quarter = tables[0].shape[2]
    part = 2 * (SG // TS)
    vmem = pl.BlockSpec(memory_space=pltpu.VMEM)
    smem = pl.BlockSpec(memory_space=pltpu.SMEM)
    return pl.pallas_call(
        adjoint_tables_kernel,
        in_specs=[smem] * 2 + [vmem] * 3,
        out_specs=[vmem] * 2,
        out_shape=[
            jax.ShapeDtypeStruct((TS, 2 * quarter, count * part), BF16),
            jax.ShapeDtypeStruct((row_window.size, LANES), F32),
        ],
        scratch_shapes=[pltpu.VMEM((TS, count * part, 2 * quarter), F32)],
        compiler_params=pltpu.CompilerParams(vmem_limit_bytes=VMEM_LIMIT),
        cost_estimate=pl.CostEstimate(
            flops=7_000_000_000, bytes_accessed=7 << 20, transcendentals=0
        ),
        name="adjoint_tables",
    )(ids, row_off, *tables, row_window)


def backward_kernel(
    ids,
    row_off,
    col_off,
    a_ref,
    b_ref,
    fr_ref,
    fi_ref,
    cw_ref,
    even_ref,
    mat_ref,
    spread_ref,
    out_ref,
    image,
    odd,
    middle,
    mat,
    spread,
    update,
    arrived,
    left,
):
    used = row_off.shape[0] // 2
    quarter = mat.shape[1] // 2
    blocks, _, _, _, block = update.shape
    pieces = left.shape[1]
    piece = quarter // pieces
    part = 2 * (SG // TS)
    step = pl.program_id(0)

    def fetches():
        return (
            pltpu.make_async_copy(mat_ref, mat, arrived.at[0]),
            pltpu.make_async_copy(spread_ref, spread, arrived.at[1]),
        )

    def leave(b, n):
        rows = pl.ds(pl.multiple_of(n * piece, piece), piece)
        lanes = pl.ds(pl.multiple_of(b * block, block), block)
        return pltpu.make_async_copy(
            update.at[b, :, :, rows, :], out_ref.at[:, :, rows, lanes], left.at[b, n]
        )

    @pl.when(step == 0)
    def _():
        for copy in fetches():
            copy.start()

    @pl.when(step < used)
    def _():
        jr = 2 * step + 1
        columns_back(
            ids,
            jr,
            col_off,
            (a_ref.at[0], b_ref.at[0]),
            fr_ref,
            fi_ref,
            cw_ref,
            image,
            quarter * TS,
        )

        def write(k1, row, chunk, value):
            rows = pl.ds(pl.multiple_of(step * part + row, 16), value.shape[0])
            odd[k1, rows, chunk * LANES : (chunk + 1) * LANES] = value.astype(BF16)

        sort_rows(image, row_off[jnp.bitwise_xor(ids[0], jr)], write)

    @pl.when(step == used)
    def _():
        for copy in fetches():
            copy.wait()

    @pl.when(step >= used)
    def _():
        b = step - used
        lanes = pl.ds(pl.multiple_of(b * block, block), block)

        def per_k1(k1, carry):
            rows = jnp.concatenate([even_ref[k1], odd[k1, :, lanes]], axis=0)
            middle[k1] = jnp.dot(mat[k1], rows, preferred_element_type=F32)
            return carry

        lax.fori_loop(0, TS, per_k1, 0, unroll=16)

        def butterfly(chunk, carry):
            n2 = pl.multiple_of(chunk * 16, 16)
            for lane in range(0, block, LANES):
                values = [
                    tuple(
                        middle[
                            k1,
                            pl.ds(pl.multiple_of(z * quarter + n2, 16), 16),
                            lane : lane + LANES,
                        ]
                        for z in range(2)
                    )
                    for k1 in range(TS)
                ]
                for n1, pair in enumerate(dft16(values, 1)):
                    window = spread[pl.ds(pl.multiple_of(n1 * quarter + n2, 16), 16), :]
                    for z in range(2):
                        update[b, z, n1, pl.ds(n2, 16), lane : lane + LANES] = (
                            pair[z] * window
                        ).astype(BF16)
            return carry

        def per_piece(n, carry):
            chunks = piece // 16
            lax.fori_loop(n * chunks, (n + 1) * chunks, butterfly, 0)
            leave(b, n).start()
            return carry

        lax.fori_loop(0, pieces, per_piece, 0)

    @pl.when(step == used + blocks - 1)
    def _():
        for b in range(blocks):
            for n in range(pieces):
                leave(b, n).wait()


def backward(ids, row_off, col_off, halves, tables, col_window, even, matrix, spread):
    used, subs, rows, half = halves[0].shape
    _, depth, width = even.shape
    length = spread.shape[0]
    quarter = length // TS
    block = min(2 * LANES, width)
    blocks = width // block
    pieces = 4

    def early(c, *_):
        return (jnp.minimum(c, used - 1), 0, 0, 0)

    update = pl.pallas_call(
        backward_kernel,
        grid_spec=pltpu.PrefetchScalarGridSpec(
            num_scalar_prefetch=3,
            grid=(used + blocks,),
            in_specs=[pl.BlockSpec((1, subs, rows, half), early)] * 2
            + [pl.BlockSpec((width, SG), lambda c, m, *_: (m[1], 0))] * 2
            + [
                pl.BlockSpec((1, width), lambda c, *_: (0, 0)),
                pl.BlockSpec((TS, depth, block), lambda c, *_: (0, 0, jnp.maximum(c - used, 0))),
                pl.BlockSpec(memory_space=pl.ANY),
                pl.BlockSpec(memory_space=pl.ANY),
            ],
            out_specs=pl.BlockSpec(memory_space=pl.ANY),
            scratch_shapes=[
                image_scratch(width, subs),
                pltpu.VMEM((TS, depth, width), BF16),
                pltpu.VMEM((TS, 2 * quarter, block), F32),
                pltpu.VMEM(matrix.shape, BF16),
                pltpu.VMEM(spread.shape, F32),
                pltpu.VMEM((blocks, 2, TS, quarter, block), BF16),
                pltpu.SemaphoreType.DMA((2,)),
                pltpu.SemaphoreType.DMA((blocks, pieces)),
            ],
        ),
        out_shape=jax.ShapeDtypeStruct((2, TS, quarter, width), BF16),
        compiler_params=pltpu.CompilerParams(vmem_limit_bytes=VMEM_LIMIT),
        name="backward",
    )(ids, row_off, col_off, *halves, *tables, col_window, even, matrix, spread)
    return update.reshape(2, length, width)


def swap(value, axis, bit):
    return lax.ppermute(value, axis, [(i, i ^ bit) for i in range(lax.axis_size(axis))])


def bits_of(axis):
    return [(axis, 1 << n) for n in range(lax.axis_size(axis).bit_length() - 1)]


def orders():
    facet, sub = bits_of("facet")[1:], bits_of("sub")
    rest = facet[1:] + sub[1:]
    return facet[:1] + sub[:1] + rest, sub[:1] + facet[:1] + rest


def dimensions():
    return bits_of("facet")[:0:-1] + bits_of("sub")[::-1]


def sum_blocks(kept, sent, beside, operand):
    values = [k + swap(s, "facet", 1) for k, s in zip(kept, sent)]
    values[0], operand = lax.optimization_barrier((values[0], operand))
    extra = beside(operand)
    left = [dimensions(), dimensions()]
    values = [value.reshape((2,) * len(left[0]) + value.shape[2:]) for value in values]

    def halve(n, step):
        at = left[n].index(step)
        left[n].remove(step)
        mine = lax.index_in_dim(values[n], 0, at, keepdims=False)
        return mine, swap(lax.index_in_dim(values[n], 1, at, keepdims=False), *step)

    steps = list(zip(*orders()))
    for pair in steps[:-1]:
        halved = [halve(n, step) for n, step in enumerate(pair)]
        if pair is steps[0]:
            halved, extra = lax.optimization_barrier((halved, extra))
        values = [mine + arrived for mine, arrived in halved]
    last = [halve(n, step) for n, step in enumerate(steps[-1])]
    return last[0] + last[1], extra


def gather_blocks(halves, facet_count, sub_count, beside, operand):
    shape = halves[0].shape
    every = dimensions()
    have = [[], []]
    values = list(halves)

    def grow(n, step):
        at = len([d for d in every if d in have[n] and every.index(d) < every.index(step)])
        have[n].append(step)
        values[n] = jnp.stack([values[n], swap(values[n], *step)], axis=at)

    steps = list(zip(*[order[::-1] for order in orders()]))
    for pair in steps[:-1]:
        for n, step in enumerate(pair):
            grow(n, step)
    values, operand = lax.optimization_barrier((values, operand))
    extra = beside(operand)
    for n, step in enumerate(steps[-1]):
        grow(n, step)
    values, extra = lax.optimization_barrier((values, extra))
    result = []
    for value in values:
        value = value.reshape((facet_count // 2, sub_count) + shape)
        result.append((value, swap(value, "facet", 1)))
    return result, extra


def per_device(
    facet_strips,
    row_window,
    col_window,
    row_offsets,
    col_offsets,
    tile_owner,
    measured,
    vis_weight,
    uvw_pixels,
    vis_count,
):
    sub_count = lax.axis_size("sub")
    facet_count = lax.axis_size("facet")
    _, length, strip_width = facet_strips.shape
    full_width = strip_width * sub_count
    ids = jnp.stack([lax.axis_index("facet"), lax.axis_index("sub")]).astype(jnp.int32)
    row_win = row_window.reshape(length // LANES, LANES)
    col_win = col_window.reshape(1, strip_width)
    row_consts = row_tables(length)
    col_consts = column_tables(full_width)

    spectrum, *sent = forward(
        ids,
        row_offsets,
        col_offsets,
        facet_strips,
        row_win,
        col_win,
        row_consts,
        col_consts,
        sub_count,
    )
    spectrum = spectrum.reshape(facet_count // 2, 2, SG, strip_width)
    kept = cols_forward(ids, spectrum, col_consts, sub_count)

    owners = tile_owner.reshape(-1)
    slots = measured.shape[2]
    capacity = slots // sub_count
    padded = -(-capacity // GROUP) * GROUP
    groups = padded // GROUP

    def per_slot(value):
        if padded == capacity:
            return value
        value = value.reshape((sub_count, capacity) + value.shape[1:])
        value = jnp.pad(value, ((0, 0), (0, padded - capacity)) + ((0, 0),) * (value.ndim - 2))
        return value.reshape((sub_count * padded,) + value.shape[2:])

    def prepare(operand):
        pixels, values, weights, counts = operand
        live = jnp.arange(weights.shape[1], dtype=jnp.int32)[None, :] < counts[:, None]
        weights = per_slot(jnp.where(live, weights, 0.0))
        values = jnp.transpose(per_slot(values), (1, 0, 2))
        pixels = jnp.transpose(per_slot(pixels), (1, 0, 2))
        return values, weights, kernels(pixels, 4)

    parts, (values, weights, (row_kernels, col_kernels)) = sum_blocks(
        kept,
        sent,
        prepare,
        (uvw_pixels[0, 0], measured[0, 0], vis_weight[0, 0], vis_count[0, 0]),
    )
    routed = route(ids, owners, parts, sub_count, groups)
    outgoing, where = routed[:-1], routed[-1]
    arrived = [outgoing[0]] + [swap(outgoing[r], "sub", r) for r in range(1, sub_count)]
    returned = []
    for first in range(0, sub_count, sub_count // 2):
        chosen = arrived[first : first + sub_count // 2]
        answered = visit(ids, first, chosen, values, weights, row_kernels, col_kernels)
        returned += [
            swap(value, "sub", first + n) if first + n else value
            for n, value in enumerate(answered)
        ]
    halves = unroute(where, returned, 2 * SG // sub_count)

    ((a_own, a_other), (b_own, b_other)), (matrix, spread) = gather_blocks(
        halves,
        facet_count,
        sub_count,
        lambda window: adjoint_tables(ids, row_offsets, row_consts, window),
        row_win,
    )
    even = cols_backward(
        ids, row_offsets, col_offsets, (a_own, b_own), col_consts, col_win, length
    )
    return backward(
        ids,
        row_offsets,
        col_offsets,
        (a_other, b_other),
        col_consts,
        col_win,
        even,
        matrix,
        spread,
    )


def solution(mesh):
    in_specs = (
        P(None, "facet", "sub"),
        P(),
        P("sub"),
        P(),
        P(),
        P("sub", "facet", None, None),
        P("facet", "sub", None, None, None),
        P("facet", "sub", None, None),
        P("facet", "sub", None, None, None),
        P("facet", "sub", None),
    )
    out_specs = P(None, "facet", "sub")
    return jax.shard_map(
        per_device, mesh=mesh, in_specs=in_specs, out_specs=out_specs, check_vma=False
    )
```

```python
from functools import partial
import math

import jax
import jax.numpy as jnp
import numpy as np
from jax import lax
from jax.experimental import pallas as pl
from jax.experimental.pallas import tpu as pltpu
from jax.sharding import PartitionSpec as P

SG = 512
TS = 16
LANES = 128
GROUP = LANES // TS

kernel_width = 2.5
kernel_norm = 0.565

VMEM_LIMIT = 56 * 1024 * 1024
F32 = jnp.float32
BF16 = jnp.bfloat16


def column_order():
    lane = np.arange(SG)
    chunk, b, cl = lane // LANES, (lane % LANES) // GROUP, lane % GROUP
    return TS * (GROUP * chunk + cl) + b


def column_tables(full_width):
    turns = np.outer(np.arange(full_width, dtype=np.int64), column_order()) % full_width
    angles = turns * (2.0 * np.pi / full_width)
    return (
        jnp.asarray(np.cos(angles).astype(BF16)),
        jnp.asarray((-np.sin(angles)).astype(BF16)),
    )


def row_tables(length):
    q = np.arange(TS)[:, None] + TS * np.arange(SG // TS)[None, :]
    turns = (q[:, :, None] * np.arange(length // TS)[None, None, :]) % length
    angles = turns * (2.0 * np.pi / length)
    return (
        jnp.asarray(np.cos(angles).astype(np.float32)),
        jnp.asarray((-np.sin(angles)).astype(np.float32)),
    )


def radix4(x, direction):
    (r0, i0), (r1, i1), (r2, i2), (r3, i3) = x
    sr, si, dr, di = r0 + r2, i0 + i2, r0 - r2, i0 - i2
    tr, ti, er, ei = r1 + r3, i1 + i3, r1 - r3, i1 - i3
    if direction < 0:
        fr, fi = ei, -er
    else:
        fr, fi = -ei, er
    return [(sr + tr, si + ti), (dr + fr, di + fi), (sr - tr, si - ti), (dr - fr, di - fi)]


def turn(value, step, direction):
    r, i = value
    step = step % TS
    if step == 0:
        return value
    if step == 4:
        return (-i, r) if direction > 0 else (i, -r)
    angle = direction * 2.0 * math.pi * step / TS
    if step == 2:
        h = math.sqrt(0.5)
        return (h * (r - i), h * (r + i)) if direction > 0 else (h * (r + i), h * (i - r))
    if step == 6:
        h = math.sqrt(0.5)
        return (-h * (r + i), h * (r - i)) if direction > 0 else (h * (i - r), -h * (r + i))
    c, s = math.cos(angle), math.sin(angle)
    return (c * r - s * i, s * r + c * i)


def dft16(x, direction):
    inner = [radix4([x[4 * a + b] for a in range(4)], direction) for b in range(4)]
    out = [None] * 16
    for c in range(4):
        column = radix4([turn(inner[b][c], b * c, direction) for b in range(4)], direction)
        for d in range(4):
            out[c + 4 * d] = column[d]
    return out


def wave(turns, length):
    angles = turns.astype(F32) * (2.0 * math.pi / length)
    return jnp.cos(angles), -jnp.sin(angles)


def row_phase(ids, row_off, jr, quarter, facets):
    length = quarter * TS
    off = row_off[jnp.bitwise_xor(ids[0], jr)]
    theta = jnp.bitwise_and(ids[0] * off, facets - 1) * (length // facets)
    n2 = lax.broadcasted_iota(jnp.int32, (1, quarter), 1)
    return wave(jnp.bitwise_and(n2 * off + theta, length - 1), length)


def col_level(ids, col_off, jr, window, full_width, length):
    width = window.shape[1]
    off = col_off[jnp.bitwise_xor(ids[0], jr)]
    c = ids[1] * width + lax.broadcasted_iota(jnp.int32, (1, width), 1)
    cosine, sine = wave(jnp.bitwise_and(c * off, full_width - 1), full_width)
    level = window * (1.0 / math.sqrt(length * full_width))
    return level * cosine, level * sine


def spread_window(window_ref, spread):
    def one(i, carry):
        row = jnp.broadcast_to(window_ref[pl.ds(i, 1), :], (LANES, LANES))
        spread[pl.ds(pl.multiple_of(i * LANES, LANES), LANES), :] = row.T
        return carry

    lax.fori_loop(0, window_ref.shape[0], one, 0, unroll=16)


def place_of(jr, count):
    return (jr % 2) * (count // 2) + jr // 2


def fill_matrix(ids, row_off, tables, write, count):
    t_r, t_i = tables
    quarter = t_r.shape[2]
    phases = [row_phase(ids, row_off, jr, quarter, count) for jr in range(count)]

    def per_q1(q1, carry):
        a_r, a_i = t_r[q1], t_i[q1]
        for jr, (d_r, d_i) in enumerate(phases):
            m_r = a_r * d_r - a_i * d_i
            m_i = a_r * d_i + a_i * d_r
            upper = jnp.concatenate([m_r, -m_i], axis=1)
            lower = jnp.concatenate([m_i, m_r], axis=1)
            block = jnp.concatenate([upper, lower], axis=0).astype(BF16)
            off = row_off[jnp.bitwise_xor(ids[0], jr)]
            write(jnp.bitwise_and(off + q1, TS - 1), place_of(jr, count), block)
        return carry

    lax.fori_loop(0, TS, per_q1, 0, unroll=4)


def exchange(first, second):
    upper = lax.broadcasted_iota(jnp.int32, first.shape, 0) < 4
    return (
        jnp.where(upper, first, pltpu.roll(second, 4, 0)),
        jnp.where(upper, pltpu.roll(first, 4, 0), second),
    )


def columns_out(real, imag, f_r, f_i, full):
    for z, (u, v) in enumerate(((f_r, -f_i), (f_i, f_r))):
        sums = jnp.dot(real, u, preferred_element_type=F32)
        sums += jnp.dot(imag, v, preferred_element_type=F32)
        for chunk in range(SG // LANES):
            full[z, chunk] = sums[:, chunk * LANES : (chunk + 1) * LANES]


def send_blocks(full, me, subs, a_ref, b_ref, at):
    tile_rows = SG // TS // subs
    q2 = SG // TS
    chunks = SG // LANES

    def store(place, row, chunk, value):
        out_ref = a_ref if chunk < chunks // 2 else b_ref
        lane = (chunk % (chunks // 2)) * LANES
        out_ref[at, place, row : row + TS, lane : lane + LANES] = value.astype(BF16)

    if tile_rows == 4:

        def per_pair(m, carry):
            for z in range(2):
                for chunk in range(chunks):
                    for quad in range(0, TS, 4):
                        v = [
                            full[z, chunk, pl.ds(pl.multiple_of((quad + n) * q2 + m * 8, 8), 8), :]
                            for n in range(4)
                        ]
                        pairs = [exchange(v[0], v[1]), exchange(v[2], v[3])]
                        for n in range(2):
                            value = jnp.concatenate([pairs[0][n], pairs[1][n]], axis=0)
                            place = jnp.bitwise_xor(2 * m + n, me)
                            store(place, z * TS * tile_rows + quad * tile_rows, chunk, value)
            return carry

        lax.fori_loop(0, subs // 2, per_pair, 0, unroll=True)
    else:
        assert tile_rows == 1

        def per_block(s, carry):
            for z in range(2):
                for chunk in range(chunks):
                    value = full[z, chunk, pl.ds(s, TS, stride=q2), :]
                    store(jnp.bitwise_xor(s, me), z * TS, chunk, value)
            return carry

        lax.fori_loop(0, subs, per_block, 0)


def forward_kernel(
    ids,
    row_off,
    col_off,
    x_ref,
    rw_ref,
    cw_ref,
    tr_ref,
    ti_ref,
    fr_ref,
    fi_ref,
    kept_ref,
    a_ref,
    b_ref,
    strips,
    arrived,
    mat,
    inner,
    spread,
    level,
    odd,
    full,
):
    count = level.shape[0]
    quarter = tr_ref.shape[2]
    length = quarter * TS
    blocks, _, _, block = strips.shape
    width = fr_ref.shape[0]
    subs = a_ref.shape[1]
    part = 2 * (SG // TS)
    step = pl.program_id(0)

    def fetch(b):
        lanes = pl.ds(pl.multiple_of(b * block, block), block)
        return pltpu.make_async_copy(x_ref.at[:, :, lanes], strips.at[b], arrived.at[b])

    @pl.when(step == 0)
    def _():
        for b in range(blocks):
            fetch(b).start()

        def write(k1, place, value):
            mat[k1, place * part : (place + 1) * part, :] = value

        fill_matrix(ids, row_off, (tr_ref, ti_ref), write, count)
        spread_window(rw_ref, spread)
        for jr in range(count):
            l_r, l_i = col_level(ids, col_off, jr, cw_ref[...], width * subs, length)
            level[jr, 0:1, :] = l_r
            level[jr, 1:2, :] = l_i

    @pl.when(step < blocks)
    def _():
        fetch(step).wait()

        def butterfly(chunk, carry):
            n2 = pl.multiple_of(chunk * 16, 16)
            for lane in range(0, block, LANES):
                values = []
                for n1 in range(TS):
                    rows = pl.ds(pl.multiple_of(n1 * quarter + n2, 16), 16)
                    window = spread[rows, :]
                    values.append(
                        tuple(
                            strips[step, z, rows, lane : lane + LANES].astype(F32) * window
                            for z in range(2)
                        )
                    )
                for k1, pair in enumerate(dft16(values, -1)):
                    for z in range(2):
                        rows = pl.ds(pl.multiple_of(z * quarter + n2, 16), 16)
                        inner[k1, rows, lane : lane + LANES] = pair[z].astype(BF16)
            return carry

        lax.fori_loop(0, quarter // 16, butterfly, 0)
        lanes = pl.ds(pl.multiple_of(step * block, block), block)

        def per_k1(k1, carry):
            sums = jnp.dot(mat[k1], inner[k1], preferred_element_type=F32)
            for jr in range(count):
                off = row_off[jnp.bitwise_xor(ids[0], jr)]
                q1 = jnp.bitwise_and(k1 - off, TS - 1)
                at = place_of(jr, count) * part
                real = sums[at : at + part // 2]
                imag = sums[at + part // 2 : at + part]
                l_r, l_i = level[jr, 0:1, lanes], level[jr, 1:2, lanes]
                out_r = (real * l_r - imag * l_i).astype(BF16)
                out_i = (real * l_i + imag * l_r).astype(BF16)
                if jr % 2:
                    odd[jr // 2, 0, q1, :, lanes] = out_r
                    odd[jr // 2, 1, q1, :, lanes] = out_i
                else:
                    kept_ref[jr // 2, 0, q1] = out_r
                    kept_ref[jr // 2, 1, q1] = out_i
            return carry

        lax.fori_loop(0, TS, per_k1, 0, unroll=16)

    @pl.when(step >= blocks)
    def _():
        j = step - blocks
        columns_out(
            odd[j, 0].reshape(SG, width),
            odd[j, 1].reshape(SG, width),
            fr_ref[...],
            fi_ref[...],
            full,
        )
        send_blocks(full, ids[1], subs, a_ref, b_ref, 0)


def forward(ids, row_off, col_off, strips, row_window, col_window, row_consts, col_consts, subs):
    _, length, width = strips.shape
    count = row_off.shape[0]
    quarter = length // TS
    q2 = SG // TS
    block = min(2 * LANES, width)
    blocks = width // block
    half = SG // 2
    used = count // 2
    rows = 2 * SG // subs
    sent = jax.ShapeDtypeStruct((used, subs, rows, half), BF16)
    kept = jax.ShapeDtypeStruct((used, 2, TS, q2, width), BF16)

    def late(c, *_):
        return (jnp.maximum(c - blocks, 0), 0, 0, 0)

    return pl.pallas_call(
        forward_kernel,
        grid_spec=pltpu.PrefetchScalarGridSpec(
            num_scalar_prefetch=3,
            grid=(blocks + used,),
            in_specs=[
                pl.BlockSpec(memory_space=pl.ANY),
                pl.BlockSpec((length // LANES, LANES), lambda c, *_: (0, 0)),
                pl.BlockSpec((1, width), lambda c, *_: (0, 0)),
                pl.BlockSpec((TS, q2, quarter), lambda c, *_: (0, 0, 0)),
                pl.BlockSpec((TS, q2, quarter), lambda c, *_: (0, 0, 0)),
                pl.BlockSpec((width, SG), lambda c, m, *_: (m[1], 0)),
                pl.BlockSpec((width, SG), lambda c, m, *_: (m[1], 0)),
            ],
            out_specs=[
                pl.BlockSpec(
                    (used, 2, TS, q2, block),
                    lambda c, *_: (0, 0, 0, 0, jnp.minimum(c, blocks - 1)),
                ),
                pl.BlockSpec((1, subs, rows, half), late),
                pl.BlockSpec((1, subs, rows, half), late),
            ],
            scratch_shapes=[
                pltpu.VMEM((blocks, 2, length, block), BF16),
                pltpu.SemaphoreType.DMA((blocks,)),
                pltpu.VMEM((TS, count * 2 * q2, 2 * quarter), BF16),
                pltpu.VMEM((TS, 2 * quarter, block), BF16),
                pltpu.VMEM((length, LANES), F32),
                pltpu.VMEM((count, 2, width), F32),
                pltpu.VMEM((used, 2, TS, q2, width), BF16),
                pltpu.VMEM((2, SG // LANES, SG, LANES), F32),
            ],
        ),
        out_shape=[kept, sent, sent],
        compiler_params=pltpu.CompilerParams(vmem_limit_bytes=VMEM_LIMIT),
        cost_estimate=pl.CostEstimate(
            flops=12_000_000_000, bytes_accessed=16 << 20, transcendentals=0
        ),
        name="forward",
    )(ids, row_off, col_off, strips, row_window, col_window, *row_consts, *col_consts)


def cols_forward_kernel(ids, r_ref, fr_ref, fi_ref, a_ref, b_ref, full):
    columns_out(r_ref[0, 0], r_ref[0, 1], fr_ref[...], fi_ref[...], full)
    send_blocks(full, ids[1], a_ref.shape[1], a_ref, b_ref, 0)


def cols_forward(ids, rows, tables, subs):
    used, _, _, width = rows.shape
    block_rows = 2 * SG // subs
    half = SG // 2
    shape = jax.ShapeDtypeStruct((used, subs, block_rows, half), BF16)
    return pl.pallas_call(
        cols_forward_kernel,
        grid_spec=pltpu.PrefetchScalarGridSpec(
            num_scalar_prefetch=1,
            grid=(used,),
            in_specs=[
                pl.BlockSpec((1, 2, SG, width), lambda j, m: (j, 0, 0, 0)),
                pl.BlockSpec((width, SG), lambda j, m: (m[1], 0)),
                pl.BlockSpec((width, SG), lambda j, m: (m[1], 0)),
            ],
            out_specs=[pl.BlockSpec((1, subs, block_rows, half), lambda j, m: (j, 0, 0, 0))] * 2,
            scratch_shapes=[pltpu.VMEM((2, SG // LANES, SG, LANES), F32)],
        ),
        out_shape=[shape, shape],
        compiler_params=pltpu.CompilerParams(vmem_limit_bytes=VMEM_LIMIT),
        cost_estimate=pl.CostEstimate(
            flops=4_000_000_000, bytes_accessed=6 << 20, transcendentals=0
        ),
        name="cols_forward",
    )(ids, rows, *tables)


def route_kernel(ids, owner_ref, *refs):
    subs = len(refs) - 8
    parts, outs = refs[:4], refs[4 : 4 + subs]
    where_ref, held, slots, counts = refs[4 + subs :]
    chunks = SG // LANES
    tile_rows = held.shape[1] // (2 * TS)
    groups = outs[0].shape[0]
    me = ids[1]
    for h in range(2):
        total = parts[2 * h][...].astype(F32) + parts[2 * h + 1][...].astype(F32)
        for c in range(chunks // 2):
            held[h * (chunks // 2) + c] = total[:, c * LANES : (c + 1) * LANES]

    def clear(g, carry):
        slots[g] = jnp.zeros(slots.shape[1:], F32)
        return carry

    lax.fori_loop(0, slots.shape[0], clear, 0, unroll=8)
    for o in range(subs):
        counts[o] = 0
    lane = lax.broadcasted_iota(jnp.int32, (2 * TS, LANES), 1) % GROUP

    def per_chunk(n, carry):
        value = held[n % chunks, pl.ds(n // chunks, 2 * TS, stride=tile_rows), :]
        for cl in range(GROUP):
            t = n * GROUP + cl
            owner = owner_ref[t]
            rank = counts[owner]
            counts[owner] = rank + 1
            g = jnp.bitwise_xor(owner, me) * groups + rank // GROUP
            sl = rank % GROUP
            where_ref[t] = g * GROUP + sl
            moved = pltpu.roll(value, jnp.bitwise_and(sl - cl, LANES - 1), 1)
            slots[g] = jnp.where(lane == sl, moved, slots[g])
        return carry

    lax.fori_loop(0, tile_rows * chunks, per_chunk, 0, unroll=4)
    for o in range(subs):
        outs[o][...] = slots[o * groups : (o + 1) * groups].astype(BF16)


def route(ids, owners, parts, subs, groups):
    rows = parts[0].shape[0]
    smem = pl.BlockSpec(memory_space=pltpu.SMEM)
    vmem = pl.BlockSpec(memory_space=pltpu.VMEM)
    block = jax.ShapeDtypeStruct((groups, 2 * TS, LANES), BF16)
    return pl.pallas_call(
        route_kernel,
        in_specs=[smem, smem] + [vmem] * 4,
        out_specs=[vmem] * subs + [smem],
        out_shape=[block] * subs + [jax.ShapeDtypeStruct(owners.shape, jnp.int32)],
        scratch_shapes=[
            pltpu.VMEM((SG // LANES, rows, LANES), F32),
            pltpu.VMEM((subs * groups, 2 * TS, LANES), F32),
            pltpu.SMEM((subs,), jnp.int32),
        ],
        compiler_params=pltpu.CompilerParams(vmem_limit_bytes=VMEM_LIMIT),
        name="route",
    )(ids, owners, *parts)


def unroute_kernel(where_ref, *refs):
    subs = len(refs) - 4
    ins, (a_ref, b_ref, slots, held) = refs[:subs], refs[subs:]
    groups = ins[0].shape[0]
    chunks = SG // LANES
    tile_rows = held.shape[1] // (2 * TS)
    for o in range(subs):
        slots[o * groups : (o + 1) * groups] = ins[o][...].astype(F32)
    lane = lax.broadcasted_iota(jnp.int32, (2 * TS, LANES), 1) % GROUP

    def per_row(r2, carry):
        for chunk in range(chunks):
            total = jnp.zeros((2 * TS, LANES), F32)
            for cl in range(GROUP):
                slot = where_ref[(r2 * chunks + chunk) * GROUP + cl]
                moved = pltpu.roll(
                    slots[slot // GROUP], jnp.bitwise_and(cl - slot % GROUP, LANES - 1), 1
                )
                total = jnp.where(lane == cl, moved, total)
            held[chunk, pl.ds(r2, 2 * TS, stride=tile_rows), :] = total
        return carry

    lax.fori_loop(0, tile_rows, per_row, 0, unroll=2 if tile_rows > 1 else 1)
    for chunk in range(chunks):
        out_ref = a_ref if chunk < chunks // 2 else b_ref
        at = (chunk % (chunks // 2)) * LANES
        out_ref[:, at : at + LANES] = held[chunk].astype(BF16)


def unroute(where, blocks, rows):
    groups = blocks[0].shape[0]
    smem = pl.BlockSpec(memory_space=pltpu.SMEM)
    vmem = pl.BlockSpec(memory_space=pltpu.VMEM)
    half = jax.ShapeDtypeStruct((rows, SG // 2), BF16)
    return pl.pallas_call(
        unroute_kernel,
        in_specs=[smem] + [vmem] * len(blocks),
        out_specs=[vmem] * 2,
        out_shape=[half] * 2,
        scratch_shapes=[
            pltpu.VMEM((len(blocks) * groups, 2 * TS, LANES), F32),
            pltpu.VMEM((SG // LANES, rows, LANES), F32),
        ],
        compiler_params=pltpu.CompilerParams(vmem_limit_bytes=VMEM_LIMIT),
        name="unroute",
    )(where, *blocks)


def falloffs(centre):
    spread = kernel_width * kernel_width
    c = centre.astype(F32)
    value = kernel_norm * jnp.exp(c * c * (-1.0 / spread))
    ratio = jnp.exp((2.0 * c - 1.0) * (1.0 / spread))
    out = [value]
    for _ in range(1, TS):
        value = value * ratio
        ratio = ratio * math.exp(-2.0 / spread)
        out.append(value)
    return out


def plane_phases(plane):
    base_r, base_i = wave(plane, TS * TS)
    step_r, step_i = base_r * base_r - base_i * base_i, 2.0 * base_r * base_i
    value_r, value_i, turn_r, turn_i = base_r, base_i, base_r, base_i
    out = [(None, None), (value_r, value_i)]
    for _ in range(2, TS // 2 + 1):
        turn_r, turn_i = (
            turn_r * step_r - turn_i * step_i,
            turn_r * step_i + turn_i * step_r,
        )
        value_r, value_i = (
            value_r * turn_r - value_i * turn_i,
            value_r * turn_i + value_i * turn_r,
        )
        out.append((value_r, value_i))
    return out


def kernels_kernel(pixel_ref, row_ref, col_ref):
    def one(g, carry):
        at = pl.ds(pl.multiple_of(g * GROUP, GROUP), GROUP)
        across, along = falloffs(pixel_ref[0, at, :]), falloffs(pixel_ref[1, at, :])
        phases = plane_phases(pixel_ref[2, at, :])
        zero = jnp.zeros(across[0].shape, F32)

        def times(falls, a, z):
            if a == TS // 2:
                return zero if z else falls[a]
            return falls[a] * phases[abs(a - TS // 2)][z]

        for a in range(0, TS, 2):
            rows = pl.ds(a * GROUP, 2 * GROUP)
            for z in range(2):
                row = jnp.concatenate([times(across, a, z), times(across, a + 1, z)], axis=0)
                col = jnp.concatenate([times(along, a, z), times(along, a + 1, z)], axis=0)
                row_ref[g, z, rows, :] = row.astype(BF16)
                col_ref[g, rows, z * LANES : (z + 1) * LANES] = col.astype(BF16)
        return carry

    lax.fori_loop(0, row_ref.shape[0], one, 0, unroll=2)


def kernels(pixels, steps):
    slots = pixels.shape[1]
    groups = slots // GROUP
    rows = TS * GROUP
    return pl.pallas_call(
        kernels_kernel,
        grid=(steps,),
        in_specs=[pl.BlockSpec((3, slots // steps, LANES), lambda i: (0, i, 0))],
        out_specs=[
            pl.BlockSpec((groups // steps, 2, rows, LANES), lambda i: (i, 0, 0, 0)),
            pl.BlockSpec((groups // steps, rows, 2 * LANES), lambda i: (i, 0, 0)),
        ],
        out_shape=[
            jax.ShapeDtypeStruct((groups, 2, rows, LANES), BF16),
            jax.ShapeDtypeStruct((groups, rows, 2 * LANES), BF16),
        ],
        compiler_params=pltpu.CompilerParams(vmem_limit_bytes=VMEM_LIMIT),
        cost_estimate=pl.CostEstimate(
            flops=6_000_000_000, bytes_accessed=9 << 20, transcendentals=0
        ),
        name="kernels",
    )(pixels)


def visit_kernel(ids, *refs):
    n = (len(refs) - 7) // 2
    ins, outs = refs[:n], refs[n + 5 : 2 * n + 5]
    meas_ref, weight_ref, row_ref, col_ref, mask_ref = refs[n : n + 5]
    held, wide = refs[-2:]
    groups = held.shape[0]
    rows = TS * GROUP
    lane = lax.broadcasted_iota(jnp.int32, (2 * TS, LANES), 1) % GROUP

    def one(g, v):
        at = pl.ds(g * GROUP, GROUP)
        blocks = jnp.concatenate(
            [held[g, pl.ds(k, 1), :] * mask_ref[...] for k in range(2 * TS)], axis=0
        ).astype(BF16)
        col = col_ref[g]
        sums = jnp.dot(blocks, col, preferred_element_type=F32)
        part_r = sums[:rows, :LANES] - sums[rows:, LANES:]
        part_i = sums[:rows, LANES:] + sums[rows:, :LANES]
        row_r, row_i = row_ref[g, 0].astype(F32), row_ref[g, 1].astype(F32)
        pred_r = jnp.sum((row_r * part_r - row_i * part_i).reshape(TS, GROUP, LANES), axis=0)
        pred_i = jnp.sum((row_r * part_i + row_i * part_r).reshape(TS, GROUP, LANES), axis=0)
        weight = weight_ref[at, :]
        meas_r, meas_i = (
            meas_ref[pl.ds(2 * GROUP * g + z, GROUP, stride=2), :] for z in range(2)
        )
        res_r = jnp.tile(weight * (meas_r - pred_r), (TS, 1))
        res_i = jnp.tile(weight * (meas_i - pred_i), (TS, 1))
        s_r = (row_r * res_r + row_i * res_i).astype(BF16)
        s_i = (row_r * res_i - row_i * res_r).astype(BF16)
        both = jnp.concatenate(
            [jnp.concatenate([s_r, s_i], axis=1), jnp.concatenate([s_i, -s_r], axis=1)], axis=0
        )
        wide[v] = lax.dot_general(both, col, (((1,), (1,)), ((), ())), preferred_element_type=F32)
        total = wide[v, pl.ds(0, 2 * TS, stride=GROUP), :]
        for slot in range(1, GROUP):
            total = jnp.where(lane == slot, wide[v, pl.ds(slot, 2 * TS, stride=GROUP), :], total)
        return total.astype(BF16)

    for i in range(n):

        @pl.when(pl.program_id(0) == i)
        def _(i=i):
            held[...] = ins[i][...].astype(F32)
            for g, value in enumerate([one(g, g) for g in range(groups)]):
                outs[i][g] = value


def visit(ids, first, blocks, measured, weight, row, col):
    n = len(blocks)
    shape = blocks[0].shape
    groups = shape[0]
    slots = groups * GROUP
    rows = TS * GROUP
    mask = np.arange(GROUP)[:, None] == np.arange(LANES)[None, :] % GROUP
    whole = pl.BlockSpec(shape, lambda i, m: (0, 0, 0))

    def source(i, m):
        return jnp.bitwise_xor(m[1], first + i)

    return pl.pallas_call(
        visit_kernel,
        grid_spec=pltpu.PrefetchScalarGridSpec(
            num_scalar_prefetch=1,
            grid=(n,),
            in_specs=[whole] * n
            + [
                pl.BlockSpec((2 * slots, LANES), lambda i, m: (source(i, m), 0)),
                pl.BlockSpec((slots, LANES), lambda i, m: (source(i, m), 0)),
                pl.BlockSpec((groups, 2, rows, LANES), lambda i, m: (source(i, m), 0, 0, 0)),
                pl.BlockSpec((groups, rows, 2 * LANES), lambda i, m: (source(i, m), 0, 0)),
                pl.BlockSpec((GROUP, LANES), lambda i, m: (0, 0)),
            ],
            out_specs=[whole] * n,
            scratch_shapes=[
                pltpu.VMEM((groups, 2 * TS, LANES), F32),
                pltpu.VMEM((groups, 2 * rows, LANES), F32),
            ],
        ),
        out_shape=[jax.ShapeDtypeStruct(b.shape, b.dtype) for b in blocks],
        compiler_params=pltpu.CompilerParams(vmem_limit_bytes=VMEM_LIMIT),
        cost_estimate=pl.CostEstimate(
            flops=1_800_000_000 * n, bytes_accessed=(5 << 18) * n, transcendentals=0
        ),
        name="visit",
    )(ids, *blocks, measured, weight, row, col, jnp.asarray(mask.astype(np.float32)))


def columns_back(ids, jr, col_off, halves, fr_ref, fi_ref, cw_ref, image, length):
    subs, rows, half = halves[0].shape
    width = fr_ref.shape[0]
    block = rows // 2

    def times(left, right):
        return lax.dot_general(left, right, (((1,), (1,)), ((), ())), preferred_element_type=F32)

    real = imag = 0.0
    for h, ref in enumerate(halves):
        p_r = ref[:, :block, :].reshape(subs * block, half)
        p_i = ref[:, block:, :].reshape(subs * block, half)
        f_r = fr_ref[:, h * half : (h + 1) * half]
        f_i = fi_ref[:, h * half : (h + 1) * half]
        real += times(p_r, f_r) + times(p_i, f_i)
        imag += times(p_i, f_r) + times(p_r, -f_i)
    l_r, l_i = col_level(ids, col_off, jr, cw_ref[...], width * subs, length)
    for z, value in enumerate((real * l_r + imag * l_i, imag * l_r - real * l_i)):
        for s in range(subs):
            for chunk in range(width // LANES):
                image[z, chunk, jnp.bitwise_xor(s, ids[1])] = value[
                    s * block : (s + 1) * block, chunk * LANES : (chunk + 1) * LANES
                ]


def sort_rows(image, off, write):
    _, chunks, subs, block, _ = image.shape
    tile_rows = block // TS
    q2 = SG // TS

    def k1_of(q1):
        return jnp.bitwise_and(off + q1, TS - 1)

    if tile_rows == 4:

        def per_pair(pair, carry):
            rows = pl.ds(pl.multiple_of(pair * 8, 8), 8)
            for z in range(2):
                for chunk in range(chunks):
                    for s in range(0, subs, 4):
                        v = [image[z, chunk, s + n, rows, :] for n in range(4)]
                        pairs = [exchange(v[0], v[1]), exchange(v[2], v[3])]
                        for n in range(2):
                            value = jnp.concatenate([pairs[0][n], pairs[1][n]], axis=0)
                            write(k1_of(2 * pair + n), z * q2 + s * tile_rows, chunk, value)
            return carry

        lax.fori_loop(0, TS // 2, per_pair, 0, unroll=4)
    else:
        assert tile_rows == 1
        for q1 in range(TS):
            for z in range(2):
                for chunk in range(chunks):
                    value = jnp.concatenate(
                        [image[z, chunk, s, q1 : q1 + 1, :] for s in range(subs)], axis=0
                    )
                    write(k1_of(q1), z * q2, chunk, value)


def cols_backward_kernel(
    ids, row_off, col_off, a_ref, b_ref, fr_ref, fi_ref, cw_ref, out_ref, image, *, length
):
    jr = 2 * pl.program_id(0)
    columns_back(
        ids, jr, col_off, (a_ref.at[0], b_ref.at[0]), fr_ref, fi_ref, cw_ref, image, length
    )

    def write(k1, row, chunk, value):
        lanes = slice(chunk * LANES, (chunk + 1) * LANES)
        out_ref[k1, row : row + value.shape[0], lanes] = value.astype(BF16)

    sort_rows(image, row_off[jnp.bitwise_xor(ids[0], jr)], write)


def image_scratch(width, subs):
    return pltpu.VMEM((2, width // LANES, subs, SG // subs, LANES), F32)


def cols_backward(ids, row_off, col_off, halves, tables, col_window, length):
    used, subs, rows, half = halves[0].shape
    width = col_window.shape[1]
    part = 2 * (SG // TS)
    return pl.pallas_call(
        partial(cols_backward_kernel, length=length),
        grid_spec=pltpu.PrefetchScalarGridSpec(
            num_scalar_prefetch=3,
            grid=(used,),
            in_specs=[pl.BlockSpec((1, subs, rows, half), lambda j, *_: (j, 0, 0, 0))] * 2
            + [pl.BlockSpec((width, SG), lambda j, m, *_: (m[1], 0))] * 2
            + [pl.BlockSpec((1, width), lambda j, *_: (0, 0))],
            out_specs=pl.BlockSpec((TS, part, width), lambda j, *_: (0, j, 0)),
            scratch_shapes=[image_scratch(width, subs)],
        ),
        out_shape=jax.ShapeDtypeStruct((TS, used * part, width), BF16),
        compiler_params=pltpu.CompilerParams(vmem_limit_bytes=VMEM_LIMIT),
        cost_estimate=pl.CostEstimate(
            flops=5_000_000_000, bytes_accessed=6 << 20, transcendentals=0
        ),
        name="cols_backward",
    )(ids, row_off, col_off, *halves, *tables, col_window)


def adjoint_tables_kernel(ids, row_off, tr_ref, ti_ref, rw_ref, out_ref, spread_ref, mat):
    part = 2 * (SG // TS)

    def write(k1, place, block):
        mat[k1, place * part : (place + 1) * part, :] = block.astype(F32)

    fill_matrix(ids, row_off, (tr_ref, ti_ref), write, row_off.shape[0])

    def per_k1(k1, carry):
        out_ref[k1] = mat[k1].T.astype(BF16)
        return carry

    lax.fori_loop(0, TS, per_k1, 0, unroll=4)
    spread_window(rw_ref, spread_ref)


def adjoint_tables(ids, row_off, tables, row_window):
    count = row_off.shape[0]
    quarter = tables[0].shape[2]
    part = 2 * (SG // TS)
    vmem = pl.BlockSpec(memory_space=pltpu.VMEM)
    smem = pl.BlockSpec(memory_space=pltpu.SMEM)
    return pl.pallas_call(
        adjoint_tables_kernel,
        in_specs=[smem] * 2 + [vmem] * 3,
        out_specs=[vmem] * 2,
        out_shape=[
            jax.ShapeDtypeStruct((TS, 2 * quarter, count * part), BF16),
            jax.ShapeDtypeStruct((row_window.size, LANES), F32),
        ],
        scratch_shapes=[pltpu.VMEM((TS, count * part, 2 * quarter), F32)],
        compiler_params=pltpu.CompilerParams(vmem_limit_bytes=VMEM_LIMIT),
        cost_estimate=pl.CostEstimate(
            flops=7_000_000_000, bytes_accessed=7 << 20, transcendentals=0
        ),
        name="adjoint_tables",
    )(ids, row_off, *tables, row_window)


def backward_kernel(
    ids,
    row_off,
    col_off,
    a_ref,
    b_ref,
    fr_ref,
    fi_ref,
    cw_ref,
    even_ref,
    mat_ref,
    spread_ref,
    out_ref,
    image,
    odd,
    middle,
    mat,
    spread,
    update,
    arrived,
    left,
):
    used = row_off.shape[0] // 2
    quarter = mat.shape[1] // 2
    blocks, _, _, _, block = update.shape
    pieces = left.shape[1]
    piece = quarter // pieces
    part = 2 * (SG // TS)
    step = pl.program_id(0)

    def fetches():
        return (
            pltpu.make_async_copy(mat_ref, mat, arrived.at[0]),
            pltpu.make_async_copy(spread_ref, spread, arrived.at[1]),
        )

    def leave(b, n):
        rows = pl.ds(pl.multiple_of(n * piece, piece), piece)
        lanes = pl.ds(pl.multiple_of(b * block, block), block)
        return pltpu.make_async_copy(
            update.at[b, :, :, rows, :], out_ref.at[:, :, rows, lanes], left.at[b, n]
        )

    @pl.when(step == 0)
    def _():
        for copy in fetches():
            copy.start()

    @pl.when(step < used)
    def _():
        jr = 2 * step + 1
        columns_back(
            ids,
            jr,
            col_off,
            (a_ref.at[0], b_ref.at[0]),
            fr_ref,
            fi_ref,
            cw_ref,
            image,
            quarter * TS,
        )

        def write(k1, row, chunk, value):
            rows = pl.ds(pl.multiple_of(step * part + row, 16), value.shape[0])
            odd[k1, rows, chunk * LANES : (chunk + 1) * LANES] = value.astype(BF16)

        sort_rows(image, row_off[jnp.bitwise_xor(ids[0], jr)], write)

    @pl.when(step == used)
    def _():
        for copy in fetches():
            copy.wait()

    @pl.when(step >= used)
    def _():
        b = step - used
        lanes = pl.ds(pl.multiple_of(b * block, block), block)

        def per_k1(k1, carry):
            rows = jnp.concatenate([even_ref[k1], odd[k1, :, lanes]], axis=0)
            middle[k1] = jnp.dot(mat[k1], rows, preferred_element_type=F32)
            return carry

        lax.fori_loop(0, TS, per_k1, 0, unroll=16)

        def butterfly(chunk, carry):
            n2 = pl.multiple_of(chunk * 16, 16)
            for lane in range(0, block, LANES):
                values = [
                    tuple(
                        middle[
                            k1,
                            pl.ds(pl.multiple_of(z * quarter + n2, 16), 16),
                            lane : lane + LANES,
                        ]
                        for z in range(2)
                    )
                    for k1 in range(TS)
                ]
                for n1, pair in enumerate(dft16(values, 1)):
                    window = spread[pl.ds(pl.multiple_of(n1 * quarter + n2, 16), 16), :]
                    for z in range(2):
                        update[b, z, n1, pl.ds(n2, 16), lane : lane + LANES] = (
                            pair[z] * window
                        ).astype(BF16)
            return carry

        def per_piece(n, carry):
            chunks = piece // 16
            lax.fori_loop(n * chunks, (n + 1) * chunks, butterfly, 0)
            leave(b, n).start()
            return carry

        lax.fori_loop(0, pieces, per_piece, 0)

    @pl.when(step == used + blocks - 1)
    def _():
        for b in range(blocks):
            for n in range(pieces):
                leave(b, n).wait()


def backward(ids, row_off, col_off, halves, tables, col_window, even, matrix, spread):
    used, subs, rows, half = halves[0].shape
    _, depth, width = even.shape
    length = spread.shape[0]
    quarter = length // TS
    block = min(2 * LANES, width)
    blocks = width // block
    pieces = 4

    def early(c, *_):
        return (jnp.minimum(c, used - 1), 0, 0, 0)

    update = pl.pallas_call(
        backward_kernel,
        grid_spec=pltpu.PrefetchScalarGridSpec(
            num_scalar_prefetch=3,
            grid=(used + blocks,),
            in_specs=[pl.BlockSpec((1, subs, rows, half), early)] * 2
            + [pl.BlockSpec((width, SG), lambda c, m, *_: (m[1], 0))] * 2
            + [
                pl.BlockSpec((1, width), lambda c, *_: (0, 0)),
                pl.BlockSpec((TS, depth, block), lambda c, *_: (0, 0, jnp.maximum(c - used, 0))),
                pl.BlockSpec(memory_space=pl.ANY),
                pl.BlockSpec(memory_space=pl.ANY),
            ],
            out_specs=pl.BlockSpec(memory_space=pl.ANY),
            scratch_shapes=[
                image_scratch(width, subs),
                pltpu.VMEM((TS, depth, width), BF16),
                pltpu.VMEM((TS, 2 * quarter, block), F32),
                pltpu.VMEM(matrix.shape, BF16),
                pltpu.VMEM(spread.shape, F32),
                pltpu.VMEM((blocks, 2, TS, quarter, block), BF16),
                pltpu.SemaphoreType.DMA((2,)),
                pltpu.SemaphoreType.DMA((blocks, pieces)),
            ],
        ),
        out_shape=jax.ShapeDtypeStruct((2, TS, quarter, width), BF16),
        compiler_params=pltpu.CompilerParams(vmem_limit_bytes=VMEM_LIMIT),
        name="backward",
    )(ids, row_off, col_off, *halves, *tables, col_window, even, matrix, spread)
    return update.reshape(2, length, width)


def swap(value, axis, bit):
    return lax.ppermute(value, axis, [(i, i ^ bit) for i in range(lax.axis_size(axis))])


def bits_of(axis):
    return [(axis, 1 << n) for n in range(lax.axis_size(axis).bit_length() - 1)]


def orders():
    facet, sub = bits_of("facet")[1:], bits_of("sub")
    rest = facet[1:] + sub[1:]
    return facet[:1] + sub[:1] + rest, sub[:1] + facet[:1] + rest


def dimensions():
    return bits_of("facet")[:0:-1] + bits_of("sub")[::-1]


def sum_blocks(kept, sent, beside, operand):
    values = [k + swap(s, "facet", 1) for k, s in zip(kept, sent)]
    values[0], operand = lax.optimization_barrier((values[0], operand))
    extra = beside(operand)
    left = [dimensions(), dimensions()]
    values = [value.reshape((2,) * len(left[0]) + value.shape[2:]) for value in values]

    def halve(n, step):
        at = left[n].index(step)
        left[n].remove(step)
        mine = lax.index_in_dim(values[n], 0, at, keepdims=False)
        return mine, swap(lax.index_in_dim(values[n], 1, at, keepdims=False), *step)

    steps = list(zip(*orders()))
    for pair in steps[:-1]:
        halved = [halve(n, step) for n, step in enumerate(pair)]
        if pair is steps[0]:
            halved, extra = lax.optimization_barrier((halved, extra))
        values = [mine + arrived for mine, arrived in halved]
    last = [halve(n, step) for n, step in enumerate(steps[-1])]
    return last[0] + last[1], extra


def gather_blocks(halves, facet_count, sub_count, beside, operand):
    shape = halves[0].shape
    every = dimensions()
    have = [[], []]
    values = list(halves)

    def grow(n, step):
        at = len([d for d in every if d in have[n] and every.index(d) < every.index(step)])
        have[n].append(step)
        values[n] = jnp.stack([values[n], swap(values[n], *step)], axis=at)

    steps = list(zip(*[order[::-1] for order in orders()]))
    for pair in steps[:-1]:
        for n, step in enumerate(pair):
            grow(n, step)
    values, operand = lax.optimization_barrier((values, operand))
    extra = beside(operand)
    for n, step in enumerate(steps[-1]):
        grow(n, step)
    values, extra = lax.optimization_barrier((values, extra))
    result = []
    for value in values:
        value = value.reshape((facet_count // 2, sub_count) + shape)
        result.append((value, swap(value, "facet", 1)))
    return result, extra


def per_device(
    facet_strips,
    row_window,
    col_window,
    row_offsets,
    col_offsets,
    tile_owner,
    measured,
    vis_weight,
    uvw_pixels,
    vis_count,
):
    sub_count = lax.axis_size("sub")
    facet_count = lax.axis_size("facet")
    _, length, strip_width = facet_strips.shape
    full_width = strip_width * sub_count
    ids = jnp.stack([lax.axis_index("facet"), lax.axis_index("sub")]).astype(jnp.int32)
    row_win = row_window.reshape(length // LANES, LANES)
    col_win = col_window.reshape(1, strip_width)
    row_consts = row_tables(length)
    col_consts = column_tables(full_width)

    spectrum, *sent = forward(
        ids,
        row_offsets,
        col_offsets,
        facet_strips,
        row_win,
        col_win,
        row_consts,
        col_consts,
        sub_count,
    )
    spectrum = spectrum.reshape(facet_count // 2, 2, SG, strip_width)
    kept = cols_forward(ids, spectrum, col_consts, sub_count)

    owners = tile_owner.reshape(-1)
    slots = measured.shape[2]
    capacity = slots // sub_count
    padded = -(-capacity // GROUP) * GROUP
    groups = padded // GROUP

    def per_slot(value):
        if padded == capacity:
            return value
        value = value.reshape((sub_count, capacity) + value.shape[1:])
        value = jnp.pad(value, ((0, 0), (0, padded - capacity)) + ((0, 0),) * (value.ndim - 2))
        return value.reshape((sub_count * padded,) + value.shape[2:])

    def prepare(operand):
        pixels, values, weights, counts = operand
        live = jnp.arange(weights.shape[1], dtype=jnp.int32)[None, :] < counts[:, None]
        weights = per_slot(jnp.where(live, weights, 0.0))
        values = per_slot(values).reshape(-1, values.shape[2])
        pixels = jnp.transpose(per_slot(pixels), (1, 0, 2))
        return values, weights, kernels(pixels, 4)

    parts, (values, weights, (row_kernels, col_kernels)) = sum_blocks(
        kept,
        sent,
        prepare,
        (uvw_pixels[0, 0], measured[0, 0], vis_weight[0, 0], vis_count[0, 0]),
    )
    routed = route(ids, owners, parts, sub_count, groups)
    outgoing, where = routed[:-1], routed[-1]
    arrived = [outgoing[0]] + [swap(outgoing[r], "sub", r) for r in range(1, sub_count)]
    returned = []
    for first in range(0, sub_count, sub_count // 2):
        chosen = arrived[first : first + sub_count // 2]
        answered = visit(ids, first, chosen, values, weights, row_kernels, col_kernels)
        returned += [
            swap(value, "sub", first + n) if first + n else value
            for n, value in enumerate(answered)
        ]
    halves = unroute(where, returned, 2 * SG // sub_count)

    ((a_own, a_other), (b_own, b_other)), (matrix, spread) = gather_blocks(
        halves,
        facet_count,
        sub_count,
        lambda window: adjoint_tables(ids, row_offsets, row_consts, window),
        row_win,
    )
    even = cols_backward(
        ids, row_offsets, col_offsets, (a_own, b_own), col_consts, col_win, length
    )
    return backward(
        ids,
        row_offsets,
        col_offsets,
        (a_other, b_other),
        col_consts,
        col_win,
        even,
        matrix,
        spread,
    )


def solution(mesh):
    in_specs = (
        P(None, "facet", "sub"),
        P(),
        P("sub"),
        P(),
        P(),
        P("sub", "facet", None, None),
        P("facet", "sub", None, None, None),
        P("facet", "sub", None, None),
        P("facet", "sub", None, None, None),
        P("facet", "sub", None),
    )
    out_specs = P(None, "facet", "sub")
    return jax.shard_map(
        per_device, mesh=mesh, in_specs=in_specs, out_specs=out_specs, check_vma=False
    )
```
